32 devices in a mesh: pipe: 4 (over z), row: 4 (over y, x), col: 2 (over core).
Axes of the slice: x: 2, y: 2, z: 4, core: 2. Of those that a mesh axis runs over, the one named last changes fastest.
Arguments:
- saved_in: bfloat16 [4, 32, 32, 2048], P('pipe', 'row', 'col'), may hold values from -400 to 400
- cotangent: bfloat16 [4, 32, 32, 2048], P('pipe', 'row', 'col'), may hold values from -6 to 6
- section_gains: float32 [4, 5, 2048], P('pipe'), may hold values from -8 to 8
Outputs:
- next_grad: bfloat16 [4, 32, 32, 2048], P('pipe', 'row', 'col')
The draws below stay inside these ranges and needn't reach their ends.
All inputs are finite; a program needn't handle non-finite values.
Results may differ from the reference program's by a relative error of at most 0.0028.
The reference program's roundings to bfloat16 on the way count: a program that leaves them out, or rounds other values in their place, can miss the bound.
Values may be sent and summed in bfloat16 or wider, within the bound.
No kernel may reach another device: no remote copies, remote signals or barrier semaphores. Data moves between devices by JAX's collectives and lax.ppermute only.
A program may use at most 64 MiB of HBM per device.

```python
import math
import jax
import jax.numpy as jnp
from jax import lax

D = 2048
HEADS = 16
HEAD_DIM = 128
TILE = 8
SPAN = 5
IMG_ROWS = 32
IMG_COLS = 32
N_PIPE = 4


def draw_image(key, salt):
    keys = jax.random.split(jax.random.fold_in(key, salt), 3)
    shape = (N_PIPE, IMG_ROWS, IMG_COLS, D)
    base = jnp.clip(jax.random.normal(keys[0], shape, jnp.float32), -4.0, 4.0)
    row_scale = jnp.exp(jax.random.uniform(keys[1], (N_PIPE, IMG_ROWS, IMG_COLS, 1), jnp.float32, math.log(0.3), math.log(3.0)))
    col_scale = jnp.exp(jax.random.uniform(keys[2], (N_PIPE, 1, 1, D), jnp.float32, math.log(0.3), math.log(3.0)))
    return (base * row_scale * col_scale).astype(jnp.bfloat16)


def draw_saved_in(key, part):
    return draw_image(key, 23)


def draw_section_gains(key, part):
    keys = jax.random.split(jax.random.fold_in(key, 37), 9)
    shape = (N_PIPE, 1, D)
    norm_gain = jnp.exp(jax.random.uniform(keys[0], shape, jnp.float32, math.log(0.5), math.log(2.0)))
    query_gain = jnp.clip(jax.random.normal(keys[3], shape, jnp.float32), -3.0, 3.0)
    key_gain = jnp.clip(jax.random.normal(keys[5], shape, jnp.float32), -3.0, 3.0)
    value_gain = jnp.clip(jax.random.normal(keys[7], shape, jnp.float32), -3.0, 3.0)
    output_gain = jnp.clip(jax.random.normal(keys[8], shape, jnp.float32), -3.0, 3.0)
    stacked = jnp.concatenate([norm_gain, query_gain, key_gain, value_gain, output_gain], axis=1)
    return jnp.clip(stacked, -8.0, 8.0).astype(jnp.float32)


def block_scale(own_key, shape, shards, low, top_value):
    def one(dim, blocks):
        steps = jax.random.uniform(jax.random.fold_in(jax.random.fold_in(own_key, 6), dim), (blocks,), jnp.float32, low / len(shards), top_value / len(shards))
        return jnp.repeat(jnp.exp(steps), shape[dim] // blocks).reshape((-1,) + (1,) * (len(shape) - dim - 1))

    level = one(*shards[0])
    for cut in shards[1:]:
        level = level * one(*cut)
    return level


def noise(stream_key, dims, scale, limit, cuts=(), kind=jnp.bfloat16):
    drawn = scale * jax.random.normal(stream_key, dims, jnp.float32)
    if cuts:
        drawn = drawn * block_scale(stream_key, dims, cuts, -0.22, 0.18)
    return jnp.clip(drawn, -limit, limit).astype(kind)


def setup_inputs(seed: int = 0) -> dict:
    seeds = jax.random.split(jax.random.key(seed), 4)
    return {
        "saved_in": draw_saved_in(jax.random.fold_in(seeds[3], 71), 0),
        "cotangent": noise(seeds[1], (N_PIPE, IMG_ROWS, IMG_COLS, D), 1.0, 6.0, ((0, 4), (1, 4), (2, 2))),
        "section_gains": draw_section_gains(jax.random.fold_in(seeds[3], 71), 0),
    }


NEGATIVE = -1e+30
EPSILON = 1e-06

def to_tiles(image):
    height, width, channels = image.shape
    image = image.reshape(height // TILE, TILE, width // TILE, TILE, channels)
    return image.transpose(0, 2, 1, 3, 4).reshape(height // TILE, width // TILE, TILE * TILE, channels)

def from_tiles(tiled):
    tile_rows, tile_cols, area, channels = tiled.shape
    tiled = tiled.reshape(tile_rows, tile_cols, TILE, TILE, channels)
    return tiled.transpose(0, 2, 1, 3, 4).reshape(tile_rows * TILE, tile_cols * TILE, channels)

def windows(extended, tile_rows, tile_cols):
    return jnp.concatenate([extended[row_off:row_off + tile_rows, col_off:col_off + tile_cols] for row_off in range(SPAN) for col_off in range(SPAN)], axis=2)

def key_valid(base_row, base_col, tile_rows, tile_cols, all_rows, all_cols):
    reach_tiles = SPAN // 2
    offsets = jnp.arange(SPAN, dtype=jnp.int32) - reach_tiles
    row_ids = base_row + jnp.arange(tile_rows, dtype=jnp.int32)[:, None] + offsets[None, :]
    col_ids = base_col + jnp.arange(tile_cols, dtype=jnp.int32)[:, None] + offsets[None, :]
    row_ok = (row_ids >= 0) & (row_ids < all_rows)
    col_ok = (col_ids >= 0) & (col_ids < all_cols)
    allowed = row_ok[:, None, :, None] & col_ok[None, :, None, :]
    return jnp.repeat(allowed.reshape(tile_rows, tile_cols, SPAN * SPAN), TILE * TILE, axis=2)

def split_heads(array):
    return array.reshape(array.shape[:-1] + (HEADS, array.shape[-1] // HEADS))

def contract(form, left, right):
    return jnp.einsum(form, left.astype(jnp.float32), right.astype(jnp.float32), precision=lax.Precision.HIGHEST)

def project(normed, scales, factor):
    return (normed.astype(jnp.float32) * (scales * factor)).astype(jnp.bfloat16)

def normalize(image, scales):
    x_float = image.astype(jnp.float32)
    inverse = lax.rsqrt(lax.optimization_barrier(jnp.mean(x_float * x_float, axis=-1, keepdims=True)) + EPSILON)
    return (x_float, inverse, (x_float * inverse * scales).astype(jnp.bfloat16))

def attend(queries, key_win, value_win, allowed):
    scores = contract('ijqhc,ijkhc->ijhqk', split_heads(queries), split_heads(key_win))
    scores = jnp.where(allowed[:, :, None, None, :], scores, NEGATIVE)
    row_max = lax.optimization_barrier(jnp.max(scores, axis=-1, keepdims=True))
    log_total = row_max + jnp.log(lax.optimization_barrier(jnp.sum(jnp.exp(scores - row_max), axis=-1, keepdims=True)))
    weights = jnp.exp(scores - log_total)
    rounded = weights.astype(jnp.bfloat16)
    output = contract('ijhqk,ijkhc->ijqhc', rounded, split_heads(value_win))
    return (log_total, weights, rounded, output.reshape(queries.shape))

def prepare(image, scales):
    tiled = to_tiles(image)
    reach_tiles = SPAN // 2
    factor = 1.0 / math.sqrt(HEAD_DIM)
    x_float, inverse, normed = normalize(tiled, scales[0])
    padded = jnp.pad(normed, ((reach_tiles, reach_tiles), (reach_tiles, reach_tiles), (0, 0), (0, 0)))
    queries = project(normed, scales[1], factor)
    keys_ext = project(padded, scales[2], 1.0)
    values_ext = project(padded, scales[3], 1.0)
    return (tiled, x_float, inverse, padded, queries, keys_ext, values_ext)

def row_attention(queries, keys_ext, values_ext, index, tile_rows, tile_cols):
    allowed = key_valid(index, 0, 1, tile_cols, tile_rows, tile_cols)
    key_win = windows(lax.dynamic_slice_in_dim(keys_ext, index, SPAN, 0), 1, tile_cols)
    value_win = windows(lax.dynamic_slice_in_dim(values_ext, index, SPAN, 0), 1, tile_cols)
    query_row = lax.dynamic_slice_in_dim(queries, index, 1, 0)
    return (query_row, key_win, value_win, attend(query_row, key_win, value_win, allowed))

def backward_image(image, upstream_image, scales):
    tiled, x_float, inverse, padded, queries, keys_ext, values_ext = prepare(image, scales)
    tile_rows, tile_cols = (tiled.shape[0], tiled.shape[1])
    factor = 1.0 / math.sqrt(HEAD_DIM)
    tile_area = TILE * TILE
    upstream = to_tiles(upstream_image).astype(jnp.float32)
    out_grad = (upstream * scales[4]).astype(jnp.bfloat16)

    def one_row(spread, index):
        query_row, key_win, value_win, parts = row_attention(queries, keys_ext, values_ext, index, tile_rows, tile_cols)
        log_total, weights, rounded, output = parts
        grad_row = lax.dynamic_slice_in_dim(out_grad, index, 1, 0)
        delta_sum = lax.optimization_barrier(jnp.sum(split_heads(grad_row.astype(jnp.float32)) * split_heads(output), axis=-1))
        prob_grad = contract('ijqhc,ijkhc->ijhqk', split_heads(grad_row), split_heads(value_win))
        dscore = (weights * (prob_grad - jnp.swapaxes(delta_sum, 2, 3)[..., None])).astype(jnp.bfloat16)
        dquery = contract('ijhqk,ijkhc->ijqhc', dscore, split_heads(key_win)).reshape(query_row.shape)
        key_grad = contract('ijhqk,ijqhc->ijkhc', dscore, split_heads(query_row)).reshape(key_win.shape)
        dvalue = contract('ijhqk,ijqhc->ijkhc', rounded, split_heads(grad_row)).reshape(key_win.shape)
        terms = key_grad * scales[2] + dvalue * scales[3]
        slab = lax.dynamic_slice_in_dim(spread, index, SPAN, 0)
        for row_off in range(SPAN):
            for col_off in range(SPAN):
                offset_id = row_off * SPAN + col_off
                slab = slab.at[row_off:row_off + 1, col_off:col_off + tile_cols].add(terms[:, :, offset_id * tile_area:(offset_id + 1) * tile_area])
        spread = lax.dynamic_update_slice_in_dim(spread, slab, index, 0)
        return (spread, (dquery * (scales[1] * factor))[0])
    spread, dquery_all = lax.scan(one_row, jnp.zeros(padded.shape, jnp.float32), jnp.arange(tile_rows, dtype=jnp.int32))
    reach_tiles = SPAN // 2
    dnormed = dquery_all + spread[reach_tiles:reach_tiles + tile_rows, reach_tiles:reach_tiles + tile_cols]
    scaled = scales[0] * dnormed
    image_grad = upstream + inverse * scaled - x_float * (inverse * inverse * inverse) * lax.optimization_barrier(jnp.mean(x_float * scaled, axis=-1, keepdims=True))
    return from_tiles(image_grad.astype(jnp.bfloat16))

def reference(saved_in, cotangent, section_gains):
    gradients = [backward_image(saved_in[segment], cotangent[segment], section_gains[segment]) for segment in range(N_PIPE)]
    zeros_image = jnp.zeros_like(gradients[0])
    return jnp.stack(gradients[1:] + [zeros_image])
```

```python
import functools
import math

import jax
import jax.numpy as jnp
from jax import lax
from jax.experimental import pallas as pl
from jax.experimental.pallas import tpu as pltpu
from jax.sharding import PartitionSpec as P

HEADS = 16
HEAD_DIM = 128
TILE = 8
SPAN = 5


NEGATIVE = -1e30
EPSILON = 1e-06


def passed_along(block, axis, distance):
    devices = range(lax.axis_size(axis))
    route = [(i - distance, i) for i in devices if i - distance in devices]
    return lax.ppermute(block, axis, route)


def to_tiles(image):
    lead = image.shape[:-3]
    height, width, channels = image.shape[-3:]
    count = len(lead)
    image = image.reshape(lead + (height // TILE, TILE, width // TILE, TILE, channels))
    order = tuple(range(count)) + (count, count + 2, count + 1, count + 3, count + 4)
    return image.transpose(order).reshape(
        lead + (height // TILE, width // TILE, TILE * TILE, channels)
    )


def from_tiles(tiled):
    tile_rows, tile_cols, area, channels = tiled.shape
    tiled = tiled.reshape(tile_rows, tile_cols, TILE, TILE, channels)
    return tiled.transpose(0, 2, 1, 3, 4).reshape(tile_rows * TILE, tile_cols * TILE, channels)


def windows(extended, tile_rows, tile_cols):
    return jnp.concatenate(
        [
            extended[row_off : row_off + tile_rows, col_off : col_off + tile_cols]
            for row_off in range(SPAN)
            for col_off in range(SPAN)
        ],
        axis=2,
    )


def key_valid(base_row, base_col, tile_rows, tile_cols, all_rows, all_cols):
    reach_tiles = SPAN // 2
    offsets = jnp.arange(SPAN, dtype=jnp.int32) - reach_tiles
    row_ids = base_row + jnp.arange(tile_rows, dtype=jnp.int32)[:, None] + offsets[None, :]
    col_ids = base_col + jnp.arange(tile_cols, dtype=jnp.int32)[:, None] + offsets[None, :]
    row_ok = (row_ids >= 0) & (row_ids < all_rows)
    col_ok = (col_ids >= 0) & (col_ids < all_cols)
    allowed = row_ok[:, None, :, None] & col_ok[None, :, None, :]
    return jnp.repeat(allowed.reshape(tile_rows, tile_cols, SPAN * SPAN), TILE * TILE, axis=2)


def project(normed, scales, factor):
    return (normed.astype(jnp.float32) * (scales * factor)).astype(jnp.bfloat16)


def normalize(image, scales):
    x_float = image.astype(jnp.float32)
    inverse = lax.rsqrt(jnp.mean(x_float * x_float, axis=-1, keepdims=True) + EPSILON)
    return (x_float, inverse, (x_float * inverse * scales).astype(jnp.bfloat16))


def widen(array, dim, reach, move):
    own = array.shape[dim]
    need = -(-reach // own)
    above = []
    below = []
    for step_by in range(need, 0, -1):
        lower_end = max(-step_by * own, -reach)
        upper_end = -(step_by - 1) * own
        piece = array
        above.append(move(piece, step_by))
    for step_by in range(1, need + 1):
        length = min((step_by + 1) * own, own + reach) - step_by * own
        piece = array
        below.append(move(piece, -step_by))
    return jnp.concatenate(above + [array] + below, axis=dim)


def halo_per_device(saved_in, cotangent, section_gains):
    scales = section_gains[0]
    reach_tiles = SPAN // 2
    reach_cells = TILE * reach_tiles
    factor = 1.0 / math.sqrt(HEAD_DIM)
    tile_rows = saved_in.shape[1] // TILE
    tile_cols = saved_in.shape[2] // TILE
    allowed = key_valid(
        lax.axis_index("row") * tile_rows,
        lax.axis_index("col") * tile_cols,
        tile_rows,
        tile_cols,
        tile_rows * lax.axis_size("row"),
        tile_cols * lax.axis_size("col"),
    )
    saved_float, saved_inverse, saved_normed = normalize(saved_in[0], scales[0])
    upstream_image = cotangent[0].astype(jnp.float32)
    grad_image = (upstream_image * scales[4]).astype(jnp.bfloat16)
    paired = jnp.stack([saved_normed, grad_image])

    def move_cols(piece, step_by):
        return passed_along(piece, "col", step_by)

    def move_rows(piece, step_by):
        return passed_along(piece, "row", step_by)

    paired_wide = widen(widen(paired, 2, reach_cells, move_cols), 1, reach_cells, move_rows)
    paired_ext = to_tiles(paired_wide)
    normed_ext = paired_ext[0]
    grad_ext = paired_ext[1]
    normed_tiles = to_tiles(saved_normed)
    grad_tiles = to_tiles(grad_image)
    stat_shape = (HEADS, tile_rows, tile_cols, TILE * TILE)

    def own_head(head, carry):
        dnormed, log_all, delta_all = carry
        start = head * HEAD_DIM

        def part(array):
            return lax.dynamic_slice_in_dim(array, start, HEAD_DIM, array.ndim - 1)

        queries = project(part(normed_tiles), part(scales[1]), factor)
        key_win = windows(project(part(normed_ext), part(scales[2]), 1.0), tile_rows, tile_cols)
        value_win = windows(project(part(normed_ext), part(scales[3]), 1.0), tile_rows, tile_cols)
        scores = jnp.einsum("ijqc,ijkc->ijqk", queries, key_win, preferred_element_type=jnp.float32)
        scores = jnp.where(allowed[:, :, None, :], scores, NEGATIVE)
        row_max = jnp.max(scores, axis=-1, keepdims=True)
        log_total = row_max + jnp.log(jnp.sum(jnp.exp(scores - row_max), axis=-1, keepdims=True))
        weights = jnp.exp(scores - log_total)
        rounded = weights.astype(jnp.bfloat16)
        output = jnp.einsum(
            "ijqk,ijkc->ijqc", rounded, value_win, preferred_element_type=jnp.float32
        )
        grads = part(grad_tiles)
        delta_sum = jnp.sum(grads.astype(jnp.float32) * output, axis=-1)
        prob_grad = jnp.einsum(
            "ijqc,ijkc->ijqk", grads, value_win, preferred_element_type=jnp.float32
        )
        dscore = (weights * (prob_grad - delta_sum[..., None])).astype(jnp.bfloat16)
        dquery = jnp.einsum("ijqk,ijkc->ijqc", dscore, key_win, preferred_element_type=jnp.float32)
        dnormed = lax.dynamic_update_slice_in_dim(
            dnormed, dquery * (part(scales[1]) * factor), start, 3
        )
        log_all = log_all.at[head].set(log_total[..., 0])
        delta_all = delta_all.at[head].set(delta_sum)
        return (dnormed, log_all, delta_all)

    dnormed, log_all, delta_all = lax.fori_loop(
        0,
        HEADS,
        own_head,
        (
            jnp.zeros(normed_tiles.shape, jnp.float32),
            jnp.zeros(stat_shape, jnp.float32),
            jnp.zeros(stat_shape, jnp.float32),
        ),
    )
    stat_tiles = jnp.concatenate([log_all, delta_all], axis=0).transpose(1, 2, 3, 0)

    def stat_cols(piece, step_by):
        return passed_along(piece, "col", step_by)

    def stat_rows(piece, step_by):
        return passed_along(piece, "row", step_by)

    stat_wide = widen(
        widen(from_tiles(stat_tiles), 1, reach_cells, stat_cols), 0, reach_cells, stat_rows
    )
    stat_win = windows(to_tiles(stat_wide), tile_rows, tile_cols)

    def far_head(head, dnormed):
        start = head * HEAD_DIM

        def part(array):
            return lax.dynamic_slice_in_dim(array, start, HEAD_DIM, array.ndim - 1)

        query_win = windows(
            project(part(normed_ext), part(scales[1]), factor), tile_rows, tile_cols
        )
        grad_win = windows(part(grad_ext), tile_rows, tile_cols)
        own_keys = project(part(normed_tiles), part(scales[2]), 1.0)
        own_values = project(part(normed_tiles), part(scales[3]), 1.0)
        far_log = lax.dynamic_index_in_dim(stat_win, head, 3, keepdims=False)
        far_delta = lax.dynamic_index_in_dim(stat_win, HEADS + head, 3, keepdims=False)
        scores = jnp.einsum(
            "ijqc,ijkc->ijqk", query_win, own_keys, preferred_element_type=jnp.float32
        )
        weights = jnp.exp(jnp.where(allowed[..., None], scores - far_log[..., None], NEGATIVE))
        prob_grad = jnp.einsum(
            "ijqc,ijkc->ijqk", grad_win, own_values, preferred_element_type=jnp.float32
        )
        dscore = (weights * (prob_grad - far_delta[..., None])).astype(jnp.bfloat16)
        key_grad = jnp.einsum(
            "ijqk,ijqc->ijkc", dscore, query_win, preferred_element_type=jnp.float32
        )
        dvalue = jnp.einsum(
            "ijqk,ijqc->ijkc",
            weights.astype(jnp.bfloat16),
            grad_win,
            preferred_element_type=jnp.float32,
        )
        terms = key_grad * part(scales[2]) + dvalue * part(scales[3])
        return lax.dynamic_update_slice_in_dim(dnormed, part(dnormed) + terms, start, 3)

    dnormed = lax.fori_loop(0, HEADS, far_head, dnormed)
    scaled = scales[0] * dnormed
    x_tiles = to_tiles(saved_float)
    inv_tiles = to_tiles(saved_inverse)
    upstream = to_tiles(upstream_image)
    image_grad = (
        upstream
        + inv_tiles * scaled
        - x_tiles
        * (inv_tiles * inv_tiles * inv_tiles)
        * jnp.mean(x_tiles * scaled, axis=-1, keepdims=True)
    )
    sent_back = passed_along(from_tiles(image_grad.astype(jnp.bfloat16)), "pipe", -1)
    return sent_back[None]


PIECES = 16


def crossing(axes_sizes, row_step, col_step):
    rows, cols = axes_sizes
    return [
        (row * cols + col, (row ^ row_step) * cols + (col ^ col_step))
        for row in range(rows)
        for col in range(cols)
    ]


def crossing_back(axes_sizes, row_step):
    pipes, rows, cols = axes_sizes
    return [
        (
            (pipe * rows + row) * cols + col,
            ((pipe - 1) % pipes * rows + (row ^ row_step)) * cols + col,
        )
        for pipe in range(pipes)
        for row in range(rows)
        for col in range(cols)
    ]


def row_to_column(row):
    return jnp.broadcast_to(row, (row.shape[1], row.shape[1])).T


def pack_kernel(rows, width, x_ref, c_ref, *outs):
    tokens, channels = x_ref.shape
    row = lax.axis_index("row")
    col = lax.axis_index("col")
    squares = None
    for lane in range(0, channels, 128):
        part = x_ref[:, lane : lane + 128].astype(jnp.float32)
        part = part * part
        squares = part if squares is None else squares + part
    total = jnp.sum(squares.T, axis=0, keepdims=True)
    inverse = lax.rsqrt(total / channels + EPSILON)
    high = inverse.astype(jnp.bfloat16).astype(jnp.float32)
    mid = (inverse - high).astype(jnp.bfloat16).astype(jnp.float32)
    low = inverse - high - mid
    place = lax.broadcasted_iota(jnp.int32, (PIECES, tokens), 0)
    pieces = jnp.where(place == 0, high, jnp.where(place == 1, mid, jnp.where(place == 2, low, 0.0)))
    pieces = pieces.astype(jnp.bfloat16)
    for step in range(rows):
        for slot in range(2):
            start = pl.multiple_of(((row ^ step) * 2 + (col ^ slot)) * width, width)
            out = outs[step]
            out[slot, 0:tokens, :] = x_ref[:, pl.ds(start, width)]
            out[slot, tokens : 2 * tokens, :] = c_ref[:, pl.ds(start, width)]
            out[slot, 2 * tokens :, 0:tokens] = pieces
            if width > tokens:
                out[slot, 2 * tokens :, tokens:] = jnp.zeros((PIECES, width - tokens), jnp.bfloat16)


def inverse_columns(block_pieces):
    pieces = block_pieces.astype(jnp.float32)
    return row_to_column(pieces[0:1] + pieces[1:2] + pieces[2:3])


def attention_kernel(rows, width, reach, g_ref, *refs):
    mine = refs[0:rows]
    passed = refs[rows : 2 * rows]
    keep_ref, give_ref = refs[2 * rows : 2 * rows + 2]
    (q_s, k_s, v_s, d_s, p_s, ds_s, s_s, dp_s, acck_s, accv_s, dq_s) = refs[2 * rows + 2 :]
    tokens = (mine[0].shape[1] - PIECES) // 2
    heads = width // HEAD_DIM
    row = lax.axis_index("row")
    col = lax.axis_index("col")
    factor = 1.0 / math.sqrt(HEAD_DIM)
    start = pl.multiple_of((row * 2 + col) * width, width)
    gains = g_ref[:, pl.ds(start, width)]
    gn, gq, gk, gv, go = (gains[i : i + 1] for i in range(5))
    gq = gq * factor
    token = lax.broadcasted_iota(jnp.int32, (tokens, HEAD_DIM), 0)
    lane = lax.broadcasted_iota(jnp.int32, (tokens, HEAD_DIM), 1)
    right = (token // TILE) % 2
    block_rows = 2 * tokens

    def block(step, slot):
        return (mine[step], 0) if slot == 0 else (passed[step], 0)

    def prepare():
        for step in range(rows):
            for slot in range(2):
                ref, index = block(step, slot)
                side = col ^ slot
                place = pl.multiple_of(((row ^ step) * 2 + side) * tokens, tokens)
                inverse = inverse_columns(ref[index, 2 * tokens :, 0:tokens])
                tile_col = side * 2 + right
                first = tile_col == 0
                last = tile_col == 3
                q_mask = jnp.where((first & (lane == 0)) | (last & (lane == 1)), 1.0, 0.0)
                k_mask = jnp.where((last & (lane == 0)) | (first & (lane == 1)), NEGATIVE, 0.0)
                for head in range(heads):
                    at = slice(head * HEAD_DIM, (head + 1) * HEAD_DIM)
                    x = ref[index, 0:tokens, at].astype(jnp.float32)
                    c = ref[index, tokens : 2 * tokens, at].astype(jnp.float32)
                    normed = (x * inverse * gn[:, at]).astype(jnp.bfloat16).astype(jnp.float32)
                    here = pl.ds(place, tokens)
                    q_s[head, here, 0:HEAD_DIM] = (normed * gq[:, at]).astype(jnp.bfloat16)
                    q_s[head, here, HEAD_DIM:] = q_mask.astype(jnp.bfloat16)
                    k_s[head, here, 0:HEAD_DIM] = (normed * gk[:, at]).astype(jnp.bfloat16)
                    k_s[head, here, HEAD_DIM:] = k_mask.astype(jnp.bfloat16)
                    v_s[head, here, :] = (normed * gv[:, at]).astype(jnp.bfloat16)
                    d_s[head, here, :] = (c * go[:, at]).astype(jnp.bfloat16)

    prepare()
    contract_last = (((1,), (1,)), ((), ()))
    contract_first = (((0,), (0,)), ((), ()))

    def one_head(head, carry):
        acck_s[...] = jnp.zeros(acck_s.shape, jnp.float32)
        accv_s[...] = jnp.zeros(accv_s.shape, jnp.float32)
        for q_row in range(rows):
            here = slice(q_row * block_rows, (q_row + 1) * block_rows)
            key_rows = [r for r in range(rows) if abs(r - q_row) <= reach]
            q = q_s[head, here, :]
            d = d_s[head, here, :]
            top = None
            for r in key_rows:
                at = slice(r * block_rows, (r + 1) * block_rows)
                s = lax.dot_general(k_s[head, at, :], q, contract_last, preferred_element_type=jnp.float32)
                s_s[at, :] = s
                high = jnp.max(s, axis=0, keepdims=True)
                top = high if top is None else jnp.maximum(top, high)
            total = None
            for r in key_rows:
                at = slice(r * block_rows, (r + 1) * block_rows)
                e = jnp.exp(s_s[at, :] - top)
                s_s[at, :] = e
                part = jnp.sum(e, axis=0, keepdims=True)
                total = part if total is None else total + part
            scale = 1.0 / total
            delta = None
            for r in key_rows:
                at = slice(r * block_rows, (r + 1) * block_rows)
                dp = lax.dot_general(v_s[head, at, :], d, contract_last, preferred_element_type=jnp.float32)
                dp_s[at, :] = dp
                p = s_s[at, :] * scale
                s_s[at, :] = p
                pb = p.astype(jnp.bfloat16)
                p_s[at, :] = pb
                part = jnp.sum(pb.astype(jnp.float32) * dp, axis=0, keepdims=True)
                delta = part if delta is None else delta + part
            dq = None
            for r in key_rows:
                at = slice(r * block_rows, (r + 1) * block_rows)
                ds = (s_s[at, :] * (dp_s[at, :] - delta)).astype(jnp.bfloat16)
                k = k_s[head, at, 0:HEAD_DIM]
                acck_s[at, :] += jnp.dot(ds, q[:, 0:HEAD_DIM], preferred_element_type=jnp.float32)
                accv_s[at, :] += jnp.dot(p_s[at, :], d, preferred_element_type=jnp.float32)
                part = lax.dot_general(k, ds, contract_first, preferred_element_type=jnp.float32)
                dq = part if dq is None else dq + part
            dq_s[here, :] = dq.T
        lanes = pl.ds(pl.multiple_of(head * HEAD_DIM, HEAD_DIM), HEAD_DIM)
        of = pl.ds(pl.multiple_of(start + head * HEAD_DIM, HEAD_DIM), HEAD_DIM)
        g = g_ref[:, of]
        for step in range(rows):
            for slot in range(2):
                ref, index = block(step, slot)
                place = pl.multiple_of(((row ^ step) * 2 + (col ^ slot)) * tokens, tokens)
                at = pl.ds(place, tokens)
                inverse = inverse_columns(ref[index, 2 * tokens :, 0:tokens])
                c = ref[index, tokens : 2 * tokens, lanes].astype(jnp.float32)
                scaled = g[0:1] * (
                    dq_s[at, :] * (g[1:2] * factor) + acck_s[at, :] * g[2:3] + accv_s[at, :] * g[3:4]
                )
                out = keep_ref if slot == 0 else give_ref
                out[step, 0:tokens, lanes] = c + inverse * scaled
                x = ref[index, 0:tokens, lanes].astype(jnp.float32)
                part = jnp.sum((x * scaled).T, axis=0, keepdims=True)
                before = jnp.where(head == 0, 0.0, out[step, tokens : tokens + 8, 0:tokens])
                out[step, tokens : tokens + 8, 0:tokens] = before + part
        return carry

    lax.fori_loop(0, heads, one_head, 0)


def finish_kernel(rows, width, channels, *refs):
    mine = refs[0:rows]
    keep_ref, got_ref = refs[rows : rows + 2]
    sums = refs[rows + 2 : 2 * rows + 2]
    outs = refs[2 * rows + 2 :]
    tokens = keep_ref.shape[1] - 8
    col = lax.axis_index("col")
    for step in range(rows):
        total = sums[0][step : step + 1]
        for other in range(1, rows):
            total = total + sums[other][step ^ other : (step ^ other) + 1]
        mean = row_to_column(total / channels)
        inverse = inverse_columns(mine[step][0, 2 * tokens :, 0:tokens])
        weight = inverse * inverse * inverse * mean
        for slot, source in ((0, keep_ref), (1, got_ref)):
            for lane in range(0, width, 128):
                x = mine[step][slot, 0:tokens, lane : lane + 128].astype(jnp.float32)
                start = pl.multiple_of((col ^ slot) * width + lane, 128)
                grad = source[step, 0:tokens, lane : lane + 128] - x * weight
                outs[step][:, pl.ds(start, 128)] = grad.astype(jnp.bfloat16)


def collect_kernel(rows, *refs):
    out_ref = refs[rows]
    width = refs[0].shape[1]
    row = lax.axis_index("row")
    last = lax.axis_index("pipe") == lax.axis_size("pipe") - 1
    for step in range(rows):
        start = pl.multiple_of((row ^ step) * width, width)
        part = refs[step][...]
        out_ref[:, pl.ds(start, width)] = jnp.where(last, jnp.zeros_like(part), part)


def local_call(kernel, out_shape, scratch_shapes=()):
    return pl.pallas_call(
        kernel,
        out_shape=out_shape,
        scratch_shapes=scratch_shapes,
        compiler_params=pltpu.CompilerParams(vmem_limit_bytes=60 * 1024 * 1024),
    )


def split_heads_per_device(saved_in, cotangent, section_gains):
    pipes, rows, cols = (lax.axis_size(name) for name in ("pipe", "row", "col"))
    channels = saved_in.shape[-1]
    tokens = saved_in.shape[1] * saved_in.shape[2]
    width = channels // (rows * cols)
    heads = width // HEAD_DIM
    plane = (rows, cols)
    x = saved_in.reshape(tokens, channels)
    c = cotangent.reshape(tokens, channels)
    gains = section_gains[0]
    packet = jax.ShapeDtypeStruct((2, 2 * tokens + PIECES, width), jnp.bfloat16)
    packed = local_call(functools.partial(pack_kernel, rows, width), [packet] * rows)(x, c)
    mine = [packed[0]]
    for step in range(1, rows):
        mine.append(lax.ppermute(packed[step], ("row", "col"), crossing(plane, step, 0)))
    passed = [lax.ppermute(m[1:2], ("row", "col"), crossing(plane, 0, 1)) for m in mine]
    part = jax.ShapeDtypeStruct((rows, tokens + 8, width), jnp.float32)
    count = rows * cols * tokens
    square = 2 * tokens
    bf = jnp.bfloat16
    f32 = jnp.float32
    keep, give = local_call(
        functools.partial(attention_kernel, rows, width, SPAN // 2),
        [part, part],
        [
            pltpu.VMEM((heads, count, 2 * HEAD_DIM), bf),
            pltpu.VMEM((heads, count, 2 * HEAD_DIM), bf),
            pltpu.VMEM((heads, count, HEAD_DIM), bf),
            pltpu.VMEM((heads, count, HEAD_DIM), bf),
            pltpu.VMEM((count, square), bf),
            pltpu.VMEM((count, square), bf),
            pltpu.VMEM((count, square), f32),
            pltpu.VMEM((count, square), f32),
            pltpu.VMEM((count, HEAD_DIM), f32),
            pltpu.VMEM((count, HEAD_DIM), f32),
            pltpu.VMEM((count, HEAD_DIM), f32),
        ],
    )(gains, *mine, *passed)
    got = lax.ppermute(give, ("row", "col"), crossing(plane, 0, 1))
    total = keep[:, tokens, 0:tokens] + got[:, tokens, 0:tokens]
    sums = [total]
    for step in range(1, rows):
        sums.append(lax.ppermute(total, ("row", "col"), crossing(plane, step, 0)))
    piece = jax.ShapeDtypeStruct((tokens, 2 * width), jnp.bfloat16)
    grads = local_call(functools.partial(finish_kernel, rows, width, channels), [piece] * rows)(
        *mine, keep, got, *sums
    )
    sent = [
        lax.ppermute(grads[step], ("pipe", "row", "col"), crossing_back((pipes, rows, cols), step))
        for step in range(rows)
    ]
    out = local_call(
        functools.partial(collect_kernel, rows), jax.ShapeDtypeStruct((tokens, channels), jnp.bfloat16)
    )(*sent)
    return out.reshape(saved_in.shape)


def per_device(saved_in, cotangent, section_gains):
    rows, cols = lax.axis_size("row"), lax.axis_size("col")
    block_fits = saved_in.shape[1] == TILE and saved_in.shape[2] == 2 * TILE
    devices_fit = cols == 2 and rows & (rows - 1) == 0 and HEADS % (rows * cols) == 0
    plan = split_heads_per_device if block_fits and devices_fit else halo_per_device
    return plan(saved_in, cotangent, section_gains)


def solution(mesh):
    return jax.shard_map(
        per_device,
        mesh=mesh,
        in_specs=(
            P("pipe", "row", "col", None),
            P("pipe", "row", "col", None),
            P("pipe", None, None),
        ),
        out_specs=P("pipe", "row", "col", None),
        check_vma=False,
    )
```

```python
import functools
import math

import jax
import jax.numpy as jnp
from jax import lax
from jax.experimental import pallas as pl
from jax.experimental.pallas import tpu as pltpu
from jax.sharding import PartitionSpec as P

HEADS = 16
HEAD_DIM = 128
TILE = 8
SPAN = 5


NEGATIVE = -1e30
EPSILON = 1e-06


def passed_along(block, axis, distance):
    devices = range(lax.axis_size(axis))
    route = [(i - distance, i) for i in devices if i - distance in devices]
    return lax.ppermute(block, axis, route)


def to_tiles(image):
    lead = image.shape[:-3]
    height, width, channels = image.shape[-3:]
    count = len(lead)
    image = image.reshape(lead + (height // TILE, TILE, width // TILE, TILE, channels))
    order = tuple(range(count)) + (count, count + 2, count + 1, count + 3, count + 4)
    return image.transpose(order).reshape(
        lead + (height // TILE, width // TILE, TILE * TILE, channels)
    )


def from_tiles(tiled):
    tile_rows, tile_cols, area, channels = tiled.shape
    tiled = tiled.reshape(tile_rows, tile_cols, TILE, TILE, channels)
    return tiled.transpose(0, 2, 1, 3, 4).reshape(tile_rows * TILE, tile_cols * TILE, channels)


def windows(extended, tile_rows, tile_cols):
    return jnp.concatenate(
        [
            extended[row_off : row_off + tile_rows, col_off : col_off + tile_cols]
            for row_off in range(SPAN)
            for col_off in range(SPAN)
        ],
        axis=2,
    )


def key_valid(base_row, base_col, tile_rows, tile_cols, all_rows, all_cols):
    reach_tiles = SPAN // 2
    offsets = jnp.arange(SPAN, dtype=jnp.int32) - reach_tiles
    row_ids = base_row + jnp.arange(tile_rows, dtype=jnp.int32)[:, None] + offsets[None, :]
    col_ids = base_col + jnp.arange(tile_cols, dtype=jnp.int32)[:, None] + offsets[None, :]
    row_ok = (row_ids >= 0) & (row_ids < all_rows)
    col_ok = (col_ids >= 0) & (col_ids < all_cols)
    allowed = row_ok[:, None, :, None] & col_ok[None, :, None, :]
    return jnp.repeat(allowed.reshape(tile_rows, tile_cols, SPAN * SPAN), TILE * TILE, axis=2)


def project(normed, scales, factor):
    return (normed.astype(jnp.float32) * (scales * factor)).astype(jnp.bfloat16)


def normalize(image, scales):
    x_float = image.astype(jnp.float32)
    inverse = lax.rsqrt(jnp.mean(x_float * x_float, axis=-1, keepdims=True) + EPSILON)
    return (x_float, inverse, (x_float * inverse * scales).astype(jnp.bfloat16))


def widen(array, dim, reach, move):
    own = array.shape[dim]
    need = -(-reach // own)
    above = []
    below = []
    for step_by in range(need, 0, -1):
        lower_end = max(-step_by * own, -reach)
        upper_end = -(step_by - 1) * own
        piece = array
        above.append(move(piece, step_by))
    for step_by in range(1, need + 1):
        length = min((step_by + 1) * own, own + reach) - step_by * own
        piece = array
        below.append(move(piece, -step_by))
    return jnp.concatenate(above + [array] + below, axis=dim)


def halo_per_device(saved_in, cotangent, section_gains):
    scales = section_gains[0]
    reach_tiles = SPAN // 2
    reach_cells = TILE * reach_tiles
    factor = 1.0 / math.sqrt(HEAD_DIM)
    tile_rows = saved_in.shape[1] // TILE
    tile_cols = saved_in.shape[2] // TILE
    allowed = key_valid(
        lax.axis_index("row") * tile_rows,
        lax.axis_index("col") * tile_cols,
        tile_rows,
        tile_cols,
        tile_rows * lax.axis_size("row"),
        tile_cols * lax.axis_size("col"),
    )
    saved_float, saved_inverse, saved_normed = normalize(saved_in[0], scales[0])
    upstream_image = cotangent[0].astype(jnp.float32)
    grad_image = (upstream_image * scales[4]).astype(jnp.bfloat16)
    paired = jnp.stack([saved_normed, grad_image])

    def move_cols(piece, step_by):
        return passed_along(piece, "col", step_by)

    def move_rows(piece, step_by):
        return passed_along(piece, "row", step_by)

    paired_wide = widen(widen(paired, 2, reach_cells, move_cols), 1, reach_cells, move_rows)
    paired_ext = to_tiles(paired_wide)
    normed_ext = paired_ext[0]
    grad_ext = paired_ext[1]
    normed_tiles = to_tiles(saved_normed)
    grad_tiles = to_tiles(grad_image)
    stat_shape = (HEADS, tile_rows, tile_cols, TILE * TILE)

    def own_head(head, carry):
        dnormed, log_all, delta_all = carry
        start = head * HEAD_DIM

        def part(array):
            return lax.dynamic_slice_in_dim(array, start, HEAD_DIM, array.ndim - 1)

        queries = project(part(normed_tiles), part(scales[1]), factor)
        key_win = windows(project(part(normed_ext), part(scales[2]), 1.0), tile_rows, tile_cols)
        value_win = windows(project(part(normed_ext), part(scales[3]), 1.0), tile_rows, tile_cols)
        scores = jnp.einsum("ijqc,ijkc->ijqk", queries, key_win, preferred_element_type=jnp.float32)
        scores = jnp.where(allowed[:, :, None, :], scores, NEGATIVE)
        row_max = jnp.max(scores, axis=-1, keepdims=True)
        log_total = row_max + jnp.log(jnp.sum(jnp.exp(scores - row_max), axis=-1, keepdims=True))
        weights = jnp.exp(scores - log_total)
        rounded = weights.astype(jnp.bfloat16)
        output = jnp.einsum(
            "ijqk,ijkc->ijqc", rounded, value_win, preferred_element_type=jnp.float32
        )
        grads = part(grad_tiles)
        delta_sum = jnp.sum(grads.astype(jnp.float32) * output, axis=-1)
        prob_grad = jnp.einsum(
            "ijqc,ijkc->ijqk", grads, value_win, preferred_element_type=jnp.float32
        )
        dscore = (weights * (prob_grad - delta_sum[..., None])).astype(jnp.bfloat16)
        dquery = jnp.einsum("ijqk,ijkc->ijqc", dscore, key_win, preferred_element_type=jnp.float32)
        dnormed = lax.dynamic_update_slice_in_dim(
            dnormed, dquery * (part(scales[1]) * factor), start, 3
        )
        log_all = log_all.at[head].set(log_total[..., 0])
        delta_all = delta_all.at[head].set(delta_sum)
        return (dnormed, log_all, delta_all)

    dnormed, log_all, delta_all = lax.fori_loop(
        0,
        HEADS,
        own_head,
        (
            jnp.zeros(normed_tiles.shape, jnp.float32),
            jnp.zeros(stat_shape, jnp.float32),
            jnp.zeros(stat_shape, jnp.float32),
        ),
    )
    stat_tiles = jnp.concatenate([log_all, delta_all], axis=0).transpose(1, 2, 3, 0)

    def stat_cols(piece, step_by):
        return passed_along(piece, "col", step_by)

    def stat_rows(piece, step_by):
        return passed_along(piece, "row", step_by)

    stat_wide = widen(
        widen(from_tiles(stat_tiles), 1, reach_cells, stat_cols), 0, reach_cells, stat_rows
    )
    stat_win = windows(to_tiles(stat_wide), tile_rows, tile_cols)

    def far_head(head, dnormed):
        start = head * HEAD_DIM

        def part(array):
            return lax.dynamic_slice_in_dim(array, start, HEAD_DIM, array.ndim - 1)

        query_win = windows(
            project(part(normed_ext), part(scales[1]), factor), tile_rows, tile_cols
        )
        grad_win = windows(part(grad_ext), tile_rows, tile_cols)
        own_keys = project(part(normed_tiles), part(scales[2]), 1.0)
        own_values = project(part(normed_tiles), part(scales[3]), 1.0)
        far_log = lax.dynamic_index_in_dim(stat_win, head, 3, keepdims=False)
        far_delta = lax.dynamic_index_in_dim(stat_win, HEADS + head, 3, keepdims=False)
        scores = jnp.einsum(
            "ijqc,ijkc->ijqk", query_win, own_keys, preferred_element_type=jnp.float32
        )
        weights = jnp.exp(jnp.where(allowed[..., None], scores - far_log[..., None], NEGATIVE))
        prob_grad = jnp.einsum(
            "ijqc,ijkc->ijqk", grad_win, own_values, preferred_element_type=jnp.float32
        )
        dscore = (weights * (prob_grad - far_delta[..., None])).astype(jnp.bfloat16)
        key_grad = jnp.einsum(
            "ijqk,ijqc->ijkc", dscore, query_win, preferred_element_type=jnp.float32
        )
        dvalue = jnp.einsum(
            "ijqk,ijqc->ijkc",
            weights.astype(jnp.bfloat16),
            grad_win,
            preferred_element_type=jnp.float32,
        )
        terms = key_grad * part(scales[2]) + dvalue * part(scales[3])
        return lax.dynamic_update_slice_in_dim(dnormed, part(dnormed) + terms, start, 3)

    dnormed = lax.fori_loop(0, HEADS, far_head, dnormed)
    scaled = scales[0] * dnormed
    x_tiles = to_tiles(saved_float)
    inv_tiles = to_tiles(saved_inverse)
    upstream = to_tiles(upstream_image)
    image_grad = (
        upstream
        + inv_tiles * scaled
        - x_tiles
        * (inv_tiles * inv_tiles * inv_tiles)
        * jnp.mean(x_tiles * scaled, axis=-1, keepdims=True)
    )
    sent_back = passed_along(from_tiles(image_grad.astype(jnp.bfloat16)), "pipe", -1)
    return sent_back[None]


PIECES = 16


def crossing(sizes, row_step, col_step):
    rows, cols = sizes
    return [
        (row * cols + col, (row ^ row_step) * cols + (col ^ col_step))
        for row in range(rows)
        for col in range(cols)
    ]


def crossing_back(sizes, row_step):
    pipes, rows, cols = sizes
    return [
        (
            (pipe * rows + row) * cols + col,
            ((pipe - 1) % pipes * rows + (row ^ row_step)) * cols + col,
        )
        for pipe in range(pipes)
        for row in range(rows)
        for col in range(cols)
    ]


def row_to_column(row):
    return jnp.broadcast_to(row, (row.shape[1], row.shape[1])).T


def inverse_columns(pieces):
    pieces = pieces.astype(jnp.float32)
    return row_to_column(pieces[0:1] + pieces[1:2] + pieces[2:3])


def pack_kernel(rows, heads, x_hbm, c_hbm, *refs):
    outs = refs[: heads * 2]
    x_ref, c_ref, x_sem, c_sem = refs[heads * 2 :]
    tokens, channels = x_ref.shape
    row = lax.axis_index("row")
    col = lax.axis_index("col")
    parts = x_sem.shape[0]
    wide = channels // parts

    def fetch(source, target, sems, part):
        lanes = pl.ds(part * wide, wide)
        return pltpu.make_async_copy(source.at[:, lanes], target.at[:, lanes], sems.at[part])

    fetches = [fetch(x_hbm, x_ref, x_sem, part) for part in range(parts)]
    fetches += [fetch(c_hbm, c_ref, c_sem, part) for part in range(parts)]
    for copy in fetches:
        copy.start()
    squares = None
    for lane in range(0, channels, HEAD_DIM):
        if lane % wide == 0:
            fetches[lane // wide].wait()
        part = x_ref[:, lane : lane + HEAD_DIM].astype(jnp.float32)
        part = part * part
        squares = part if squares is None else squares + part
    for copy in fetches[parts:]:
        copy.wait()
    total = jnp.sum(squares.T, axis=0, keepdims=True)
    inverse = lax.rsqrt(total / channels + EPSILON)
    high = inverse.astype(jnp.bfloat16).astype(jnp.float32)
    mid = (inverse - high).astype(jnp.bfloat16).astype(jnp.float32)
    low = inverse - high - mid
    place = lax.broadcasted_iota(jnp.int32, (PIECES, tokens), 0)
    pieces = jnp.where(place == 0, high, jnp.where(place == 1, mid, jnp.where(place == 2, low, 0.0)))
    pieces = pieces.astype(jnp.bfloat16)
    for head in range(heads):
        for step in range(rows):
            for slot in range(2):
                first = ((row ^ step) * 2 + (col ^ slot)) * heads + head
                lanes = pl.ds(pl.multiple_of(first * HEAD_DIM, HEAD_DIM), HEAD_DIM)
                out = outs[head * 2 + slot]
                out[step, 0:tokens, :] = x_ref[:, lanes]
                out[step, tokens : 2 * tokens, :] = c_ref[:, lanes]
                if head == 0:
                    out[step, 2 * tokens :, :] = pieces


def attention_kernel(rows, heads, head, g_ref, *refs):
    held = rows + 1
    arrays, inverses = refs[0:held], refs[held : 2 * held]
    before_ref, keep_ref, give_ref, sums_ref = refs[2 * held : 2 * held + 4]
    q_s, k_s, kt_s, v_s, d_s, p_s, ds_s, s_s, dp_s, dk_s, dv_s, dq_s = refs[2 * held + 4 :]
    tokens = keep_ref.shape[1] // rows
    row = lax.axis_index("row")
    col = lax.axis_index("col")
    lanes = pl.ds(pl.multiple_of(((row * 2 + col) * heads + head) * HEAD_DIM, HEAD_DIM), HEAD_DIM)
    gn, gq, gk, gv, go = (g_ref[i : i + 1, lanes] for i in range(5))
    gq = gq * (1.0 / math.sqrt(HEAD_DIM))
    square = 2 * tokens
    pattern = (tokens // (2 * TILE), 2, TILE, tokens)
    query_right = (lax.broadcasted_iota(jnp.int32, pattern[1:], 2) // TILE) % 2
    key_right = lax.broadcasted_iota(jnp.int32, pattern[1:], 0)
    no_cap = float(jnp.finfo(jnp.float32).max)
    left_keys = jnp.where((key_right == 0) & (query_right == 1), NEGATIVE, no_cap)
    right_keys = jnp.where((key_right == 1) & (query_right == 0), NEGATIVE, no_cap)

    def capped(s, cap):
        return jnp.minimum(s.reshape(pattern), cap[None]).reshape(tokens, tokens)

    def block(step, slot):
        number, index = (slot, 0) if step == 0 else (step + 1, slot)
        ref = arrays[number]
        place = pl.multiple_of(((row ^ step) * 2 + (col ^ slot)) * tokens, tokens)
        x = ref[index, 0:tokens, :].astype(jnp.float32)
        c = ref[index, tokens : 2 * tokens, :].astype(jnp.float32)
        inverse = inverse_columns(inverses[number][index, 2 * tokens :, :])
        return pl.ds(place, tokens), x, c, inverse

    blocks = [(step, slot) for step in range(rows) for slot in range(2)]
    for step, slot in blocks:
        here, x, c, inverse = block(step, slot)
        normed = (x * inverse * gn).astype(jnp.bfloat16).astype(jnp.float32)
        q_s[here, :] = (normed * gq).astype(jnp.bfloat16)
        key = (normed * gk).astype(jnp.bfloat16)
        k_s[here, :] = key
        kt_s[:, here] = key.astype(jnp.float32).T.astype(jnp.bfloat16)
        v_s[here, :] = (normed * gv).astype(jnp.bfloat16)
        d_s[here, :] = (c * go).astype(jnp.bfloat16)

    contract_last = (((1,), (1,)), ((), ()))
    reach = SPAN // 2
    spans = []
    for at in range(rows):
        near = [r for r in range(rows) if abs(r - at) <= reach]
        spans.append((near[0] * square, (near[-1] + 1) * square))

    def own(at):
        return slice(at * square, (at + 1) * square)

    def cells(at):
        return [slice(start, start + square) for start in range(*spans[at], square)]

    def fold(combine, parts):
        total = parts[0]
        for part in parts[1:]:
            total = combine(total, part)
        return total

    def products(at, tops):
        buffer = at % 2
        q, d = q_s[own(at), :], d_s[own(at), :]
        left, right = [], []
        for cell in cells(at):
            s = lax.dot_general(k_s[cell, :], q, contract_last, preferred_element_type=jnp.float32)
            upper = slice(cell.start, cell.start + tokens)
            lower = slice(cell.start + tokens, cell.stop)
            upper_left, upper_right = s[0:tokens, 0:tokens], capped(s[0:tokens, tokens:], left_keys)
            lower_left, lower_right = capped(s[tokens:, 0:tokens], right_keys), s[tokens:, tokens:]
            s_s[buffer, upper, 0:tokens] = upper_left
            s_s[buffer, upper, tokens:] = upper_right
            s_s[buffer, lower, 0:tokens] = lower_left
            s_s[buffer, lower, tokens:] = lower_right
            left.append(jnp.max(jnp.maximum(upper_left, lower_left), axis=0, keepdims=True))
            right.append(jnp.max(jnp.maximum(upper_right, lower_right), axis=0, keepdims=True))
            yield
            dp_s[buffer, cell, :] = lax.dot_general(
                v_s[cell, :], d, contract_last, preferred_element_type=jnp.float32
            )
            yield
        tops[at] = jnp.concatenate([fold(jnp.maximum, left), fold(jnp.maximum, right)], axis=1)

    def softmax(at, tops):
        buffer = at % 2
        top = tops[at]
        sums = []
        for cell in cells(at):
            e = jnp.exp(s_s[buffer, cell, :] - top)
            s_s[buffer, cell, :] = e
            sums.append(jnp.sum(e, axis=0, keepdims=True))
            yield
        scale = 1.0 / fold(jnp.add, sums)
        sums = []
        for cell in cells(at):
            p = s_s[buffer, cell, :] * scale
            pb = p.astype(jnp.bfloat16)
            p_s[cell, own(at)] = pb
            sums.append(jnp.sum(pb.astype(jnp.float32) * dp_s[buffer, cell, :], axis=0, keepdims=True))
            yield
        delta = fold(jnp.add, sums)
        for cell in cells(at):
            p = s_s[buffer, cell, :] * scale
            ds_s[cell, own(at)] = (p * (dp_s[buffer, cell, :] - delta)).astype(jnp.bfloat16)
            yield

    def query_side(at):
        span = slice(*spans[at])
        dq = jnp.dot(kt_s[:, span], ds_s[span, own(at)], preferred_element_type=jnp.float32)
        yield
        dq_s[own(at), :] = dq.T
        yield

    def key_side(first, last):
        for at in range(rows):
            low, high = max(spans[at][0], first * square), min(spans[at][1], last * square)
            if low >= high:
                continue
            span = slice(low, high)
            dk = jnp.dot(ds_s[own(at), span], q_s[span, :], preferred_element_type=jnp.float32)
            fresh = low == spans[at][0]
            dk_s[own(at), :] = dk if fresh else dk_s[own(at), :] + dk
            yield
            dv = jnp.dot(p_s[own(at), span], d_s[span, :], preferred_element_type=jnp.float32)
            dv_s[own(at), :] = dv if fresh else dv_s[own(at), :] + dv
            yield

    def together(*works):
        works = list(works)
        while works:
            works = [work for work in works if next(work, works) is not works]


    def all_queries():
        dq = jnp.dot(kt_s[...], ds_s[...], preferred_element_type=jnp.float32)
        yield
        dq_s[...] = dq.T
        yield

    for at in range(rows):
        for other in range(rows):
            if abs(at - other) > reach:
                ds_s[own(at), own(other)] = jnp.zeros((square, square), jnp.bfloat16)
    tops = {}
    together(products(0, tops))
    for at in range(rows):
        works = [softmax(at, tops)]
        if at + 1 < rows:
            works.append(products(at + 1, tops))
        if at > 0:
            works += [key_side(at - 1, at)]
        together(*works)
    together(key_side(rows - 1, rows), all_queries())
    for step, slot in blocks:
        here, x, c, inverse = block(step, slot)
        scaled = gn * (dq_s[here, :] * gq + dk_s[here, :] * gk + dv_s[here, :] * gv)
        out = (keep_ref, give_ref)[slot]
        out[0, step * tokens : (step + 1) * tokens, :] = c + inverse * scaled
        out[1, step * tokens : (step + 1) * tokens, :] = x * (inverse * inverse * inverse)
        part = jnp.sum((x * scaled).T, axis=0, keepdims=True)
        index = slot * rows + step
        if head > 0:
            part = part + before_ref[index : index + 1, :]
        sums_ref[index : index + 1, :] = part


def finish_kernel(rows, heads, channels, *refs):
    parts = refs[0 : 2 * heads]
    sums = refs[2 * heads : 2 * heads + rows]
    outs = refs[2 * heads + rows :]
    tokens = outs[0].shape[0]
    col = lax.axis_index("col")
    for step in range(rows):
        total = sums[0][step : step + 1, :]
        for other in range(1, rows):
            total = total + sums[other][step ^ other : (step ^ other) + 1, :]
        mean = row_to_column(total / channels)
        here = slice(step * tokens, (step + 1) * tokens)
        for slot in range(2):
            for head in range(heads):
                part = parts[slot * heads + head]
                grad = part[0, here, :] - part[1, here, :] * mean
                start = pl.multiple_of(((col ^ slot) * heads + head) * HEAD_DIM, HEAD_DIM)
                outs[step][:, pl.ds(start, HEAD_DIM)] = grad.astype(jnp.bfloat16)


def collect_kernel(rows, *refs):
    out_ref = refs[rows]
    width = refs[0].shape[1]
    row = lax.axis_index("row")
    last = lax.axis_index("pipe") == lax.axis_size("pipe") - 1
    for step in range(rows):
        start = pl.multiple_of((row ^ step) * width, width)
        part = refs[step][...]
        out_ref[:, pl.ds(start, width)] = jnp.where(last, jnp.zeros_like(part), part)


def local_call(kernel, out_shape, scratch_shapes=(), in_specs=None):
    placed = {} if in_specs is None else {"in_specs": in_specs}
    return pl.pallas_call(
        kernel,
        out_shape=out_shape,
        **placed,
        scratch_shapes=scratch_shapes,
        compiler_params=pltpu.CompilerParams(vmem_limit_bytes=24 * 1024 * 1024),
    )


def near(arrays):
    return [pltpu.with_memory_space_constraint(array, pltpu.VMEM) for array in arrays]


def split_heads_per_device(saved_in, cotangent, section_gains):
    pipes, rows, cols = (lax.axis_size(name) for name in ("pipe", "row", "col"))
    channels = saved_in.shape[-1]
    tokens = saved_in.shape[1] * saved_in.shape[2]
    heads = channels // HEAD_DIM // (rows * cols)
    plane = ("row", "col")
    sizes = (rows, cols)
    bf, f32 = jnp.bfloat16, jnp.float32
    x = saved_in.reshape(tokens, channels)
    c = cotangent.reshape(tokens, channels)
    gains = section_gains[0]
    packets = []
    for head in range(heads):
        packets += [pltpu.VMEM((rows, 2 * tokens + (PIECES if head == 0 else 0), HEAD_DIM), bf)] * 2
    far = pl.BlockSpec(memory_space=pltpu.HBM)
    staged = [pltpu.VMEM((tokens, channels), bf)] * 2 + [pltpu.SemaphoreType.DMA((4,))] * 2
    packed = local_call(functools.partial(pack_kernel, rows, heads), packets, staged, [far, far])(
        pltpu.with_memory_space_constraint(x, pltpu.HBM), pltpu.with_memory_space_constraint(c, pltpu.HBM)
    )
    passed = [lax.ppermute(packed[2 * head + 1], plane, crossing(sizes, 0, 1)) for head in range(heads)]
    arrays = []
    for head in range(heads):
        own, other = packed[2 * head], passed[head]
        held = [own, other]
        packets = [jnp.stack([own[step], other[step]]) for step in range(1, rows)]
        if head > 0:
            packets, arrays[head - 1][2] = lax.optimization_barrier((packets, arrays[head - 1][2]))
        for step in range(1, rows):
            held.append(lax.ppermute(packets[step - 1], plane, crossing(sizes, step, 0)))
        arrays.append(held)
    count = rows * cols * tokens
    square = 2 * tokens
    scratch = [
        pltpu.VMEM((count, HEAD_DIM), bf),
        pltpu.VMEM((count, HEAD_DIM), bf),
        pltpu.VMEM((HEAD_DIM, count), bf),
        pltpu.VMEM((count, HEAD_DIM), bf),
        pltpu.VMEM((count, HEAD_DIM), bf),
        pltpu.VMEM((count, count), bf),
        pltpu.VMEM((count, count), bf),
        pltpu.VMEM((2, count, square), f32),
        pltpu.VMEM((2, count, square), f32),
        pltpu.VMEM((count, HEAD_DIM), f32),
        pltpu.VMEM((count, HEAD_DIM), f32),
        pltpu.VMEM((count, HEAD_DIM), f32),
    ]
    part = pltpu.VMEM((2, rows * tokens, HEAD_DIM), f32)
    sums_shape = pltpu.VMEM((2 * rows, tokens), f32)
    sums = jnp.zeros((2 * rows, tokens), f32)
    keep, give = [], []
    for head in range(heads):
        kept, given, sums = local_call(
            functools.partial(attention_kernel, rows, heads, head), [part, part, sums_shape], scratch
        )(gains, *near(arrays[head]), *near(arrays[0]), *near([sums]))
        keep.append(kept)
        give.append(given)
    own = sums[0:rows] + lax.ppermute(sums[rows:], plane, crossing(sizes, 0, 1))
    give, own = lax.optimization_barrier((give, own))
    got = [lax.ppermute(given, plane, crossing(sizes, 0, 1)) for given in give]
    totals = [own]
    for step in range(1, rows):
        totals.append(lax.ppermute(own, plane, crossing(sizes, step, 0)))
    piece = pltpu.VMEM((tokens, 2 * heads * HEAD_DIM), bf)
    grads = local_call(functools.partial(finish_kernel, rows, heads, channels), [piece] * rows)(
        *near(keep + got + totals)
    )
    sent = [
        lax.ppermute(grads[step], ("pipe",) + plane, crossing_back((pipes, rows, cols), step))
        for step in range(rows)
    ]
    out = local_call(
        functools.partial(collect_kernel, rows), jax.ShapeDtypeStruct((tokens, channels), bf)
    )(*near(sent))
    return out.reshape(saved_in.shape)


def per_device(saved_in, cotangent, section_gains):
    rows, cols = lax.axis_size("row"), lax.axis_size("col")
    block_fits = saved_in.shape[1] == TILE and saved_in.shape[2] == 2 * TILE
    devices_fit = cols == 2 and rows & (rows - 1) == 0 and HEADS % (rows * cols) == 0
    plan = split_heads_per_device if block_fits and devices_fit else halo_per_device
    return plan(saved_in, cotangent, section_gains)


def solution(mesh):
    return jax.shard_map(
        per_device,
        mesh=mesh,
        in_specs=(
            P("pipe", "row", "col", None),
            P("pipe", "row", "col", None),
            P("pipe", None, None),
        ),
        out_specs=P("pipe", "row", "col", None),
        check_vma=False,
    )
```

```python
import functools
import math

import jax
import jax.numpy as jnp
from jax import lax
from jax.experimental import pallas as pl
from jax.experimental.pallas import tpu as pltpu
from jax.sharding import PartitionSpec as P

HEADS = 16
HEAD_DIM = 128
TILE = 8
SPAN = 5


NEGATIVE = -1e30
EPSILON = 1e-06


def passed_along(block, axis, distance):
    devices = range(lax.axis_size(axis))
    route = [(i - distance, i) for i in devices if i - distance in devices]
    return lax.ppermute(block, axis, route)


def to_tiles(image):
    lead = image.shape[:-3]
    height, width, channels = image.shape[-3:]
    count = len(lead)
    image = image.reshape(lead + (height // TILE, TILE, width // TILE, TILE, channels))
    order = tuple(range(count)) + (count, count + 2, count + 1, count + 3, count + 4)
    return image.transpose(order).reshape(
        lead + (height // TILE, width // TILE, TILE * TILE, channels)
    )


def from_tiles(tiled):
    tile_rows, tile_cols, area, channels = tiled.shape
    tiled = tiled.reshape(tile_rows, tile_cols, TILE, TILE, channels)
    return tiled.transpose(0, 2, 1, 3, 4).reshape(tile_rows * TILE, tile_cols * TILE, channels)


def windows(extended, tile_rows, tile_cols):
    return jnp.concatenate(
        [
            extended[row_off : row_off + tile_rows, col_off : col_off + tile_cols]
            for row_off in range(SPAN)
            for col_off in range(SPAN)
        ],
        axis=2,
    )


def key_valid(base_row, base_col, tile_rows, tile_cols, all_rows, all_cols):
    reach_tiles = SPAN // 2
    offsets = jnp.arange(SPAN, dtype=jnp.int32) - reach_tiles
    row_ids = base_row + jnp.arange(tile_rows, dtype=jnp.int32)[:, None] + offsets[None, :]
    col_ids = base_col + jnp.arange(tile_cols, dtype=jnp.int32)[:, None] + offsets[None, :]
    row_ok = (row_ids >= 0) & (row_ids < all_rows)
    col_ok = (col_ids >= 0) & (col_ids < all_cols)
    allowed = row_ok[:, None, :, None] & col_ok[None, :, None, :]
    return jnp.repeat(allowed.reshape(tile_rows, tile_cols, SPAN * SPAN), TILE * TILE, axis=2)


def project(normed, scales, factor):
    return (normed.astype(jnp.float32) * (scales * factor)).astype(jnp.bfloat16)


def normalize(image, scales):
    x_float = image.astype(jnp.float32)
    inverse = lax.rsqrt(jnp.mean(x_float * x_float, axis=-1, keepdims=True) + EPSILON)
    return (x_float, inverse, (x_float * inverse * scales).astype(jnp.bfloat16))


def widen(array, dim, reach, move):
    own = array.shape[dim]
    need = -(-reach // own)
    above = []
    below = []
    for step_by in range(need, 0, -1):
        lower_end = max(-step_by * own, -reach)
        upper_end = -(step_by - 1) * own
        piece = array
        above.append(move(piece, step_by))
    for step_by in range(1, need + 1):
        length = min((step_by + 1) * own, own + reach) - step_by * own
        piece = array
        below.append(move(piece, -step_by))
    return jnp.concatenate(above + [array] + below, axis=dim)


def halo_per_device(saved_in, cotangent, section_gains):
    scales = section_gains[0]
    reach_tiles = SPAN // 2
    reach_cells = TILE * reach_tiles
    factor = 1.0 / math.sqrt(HEAD_DIM)
    tile_rows = saved_in.shape[1] // TILE
    tile_cols = saved_in.shape[2] // TILE
    allowed = key_valid(
        lax.axis_index("row") * tile_rows,
        lax.axis_index("col") * tile_cols,
        tile_rows,
        tile_cols,
        tile_rows * lax.axis_size("row"),
        tile_cols * lax.axis_size("col"),
    )
    saved_float, saved_inverse, saved_normed = normalize(saved_in[0], scales[0])
    upstream_image = cotangent[0].astype(jnp.float32)
    grad_image = (upstream_image * scales[4]).astype(jnp.bfloat16)
    paired = jnp.stack([saved_normed, grad_image])

    def move_cols(piece, step_by):
        return passed_along(piece, "col", step_by)

    def move_rows(piece, step_by):
        return passed_along(piece, "row", step_by)

    paired_wide = widen(widen(paired, 2, reach_cells, move_cols), 1, reach_cells, move_rows)
    paired_ext = to_tiles(paired_wide)
    normed_ext = paired_ext[0]
    grad_ext = paired_ext[1]
    normed_tiles = to_tiles(saved_normed)
    grad_tiles = to_tiles(grad_image)
    stat_shape = (HEADS, tile_rows, tile_cols, TILE * TILE)

    def own_head(head, carry):
        dnormed, log_all, delta_all = carry
        start = head * HEAD_DIM

        def part(array):
            return lax.dynamic_slice_in_dim(array, start, HEAD_DIM, array.ndim - 1)

        queries = project(part(normed_tiles), part(scales[1]), factor)
        key_win = windows(project(part(normed_ext), part(scales[2]), 1.0), tile_rows, tile_cols)
        value_win = windows(project(part(normed_ext), part(scales[3]), 1.0), tile_rows, tile_cols)
        scores = jnp.einsum("ijqc,ijkc->ijqk", queries, key_win, preferred_element_type=jnp.float32)
        scores = jnp.where(allowed[:, :, None, :], scores, NEGATIVE)
        row_max = jnp.max(scores, axis=-1, keepdims=True)
        log_total = row_max + jnp.log(jnp.sum(jnp.exp(scores - row_max), axis=-1, keepdims=True))
        weights = jnp.exp(scores - log_total)
        rounded = weights.astype(jnp.bfloat16)
        output = jnp.einsum(
            "ijqk,ijkc->ijqc", rounded, value_win, preferred_element_type=jnp.float32
        )
        grads = part(grad_tiles)
        delta_sum = jnp.sum(grads.astype(jnp.float32) * output, axis=-1)
        prob_grad = jnp.einsum(
            "ijqc,ijkc->ijqk", grads, value_win, preferred_element_type=jnp.float32
        )
        dscore = (weights * (prob_grad - delta_sum[..., None])).astype(jnp.bfloat16)
        dquery = jnp.einsum("ijqk,ijkc->ijqc", dscore, key_win, preferred_element_type=jnp.float32)
        dnormed = lax.dynamic_update_slice_in_dim(
            dnormed, dquery * (part(scales[1]) * factor), start, 3
        )
        log_all = log_all.at[head].set(log_total[..., 0])
        delta_all = delta_all.at[head].set(delta_sum)
        return (dnormed, log_all, delta_all)

    dnormed, log_all, delta_all = lax.fori_loop(
        0,
        HEADS,
        own_head,
        (
            jnp.zeros(normed_tiles.shape, jnp.float32),
            jnp.zeros(stat_shape, jnp.float32),
            jnp.zeros(stat_shape, jnp.float32),
        ),
    )
    stat_tiles = jnp.concatenate([log_all, delta_all], axis=0).transpose(1, 2, 3, 0)

    def stat_cols(piece, step_by):
        return passed_along(piece, "col", step_by)

    def stat_rows(piece, step_by):
        return passed_along(piece, "row", step_by)

    stat_wide = widen(
        widen(from_tiles(stat_tiles), 1, reach_cells, stat_cols), 0, reach_cells, stat_rows
    )
    stat_win = windows(to_tiles(stat_wide), tile_rows, tile_cols)

    def far_head(head, dnormed):
        start = head * HEAD_DIM

        def part(array):
            return lax.dynamic_slice_in_dim(array, start, HEAD_DIM, array.ndim - 1)

        query_win = windows(
            project(part(normed_ext), part(scales[1]), factor), tile_rows, tile_cols
        )
        grad_win = windows(part(grad_ext), tile_rows, tile_cols)
        own_keys = project(part(normed_tiles), part(scales[2]), 1.0)
        own_values = project(part(normed_tiles), part(scales[3]), 1.0)
        far_log = lax.dynamic_index_in_dim(stat_win, head, 3, keepdims=False)
        far_delta = lax.dynamic_index_in_dim(stat_win, HEADS + head, 3, keepdims=False)
        scores = jnp.einsum(
            "ijqc,ijkc->ijqk", query_win, own_keys, preferred_element_type=jnp.float32
        )
        weights = jnp.exp(jnp.where(allowed[..., None], scores - far_log[..., None], NEGATIVE))
        prob_grad = jnp.einsum(
            "ijqc,ijkc->ijqk", grad_win, own_values, preferred_element_type=jnp.float32
        )
        dscore = (weights * (prob_grad - far_delta[..., None])).astype(jnp.bfloat16)
        key_grad = jnp.einsum(
            "ijqk,ijqc->ijkc", dscore, query_win, preferred_element_type=jnp.float32
        )
        dvalue = jnp.einsum(
            "ijqk,ijqc->ijkc",
            weights.astype(jnp.bfloat16),
            grad_win,
            preferred_element_type=jnp.float32,
        )
        terms = key_grad * part(scales[2]) + dvalue * part(scales[3])
        return lax.dynamic_update_slice_in_dim(dnormed, part(dnormed) + terms, start, 3)

    dnormed = lax.fori_loop(0, HEADS, far_head, dnormed)
    scaled = scales[0] * dnormed
    x_tiles = to_tiles(saved_float)
    inv_tiles = to_tiles(saved_inverse)
    upstream = to_tiles(upstream_image)
    image_grad = (
        upstream
        + inv_tiles * scaled
        - x_tiles
        * (inv_tiles * inv_tiles * inv_tiles)
        * jnp.mean(x_tiles * scaled, axis=-1, keepdims=True)
    )
    sent_back = passed_along(from_tiles(image_grad.astype(jnp.bfloat16)), "pipe", -1)
    return sent_back[None]


PIECES = 16


EXTRA = 8
SCALES = [2.0 ** (12 * power) for power in range(-8, 11)]


def crossing(sizes, row_step, col_step):
    rows, cols = sizes
    return [
        (row * cols + col, (row ^ row_step) * cols + (col ^ col_step))
        for row in range(rows)
        for col in range(cols)
    ]


def crossing_back(sizes, row_step):
    pipes, rows, cols = sizes
    return [
        (
            (pipe * rows + row) * cols + col,
            ((pipe - 1) % pipes * rows + (row ^ row_step)) * cols + col,
        )
        for pipe in range(pipes)
        for row in range(rows)
        for col in range(cols)
    ]


def row_to_column(row):
    return jnp.broadcast_to(row, (row.shape[1], row.shape[1])).T


def inverse_columns(pieces):
    pieces = pieces.astype(jnp.float32)
    return row_to_column(pieces[0:1] + pieces[1:2] + pieces[2:3])


def scale_number(size):
    return sum((size >= scale).astype(jnp.float32) for scale in SCALES[1:])


def scale_value(number):
    value = jnp.full(number.shape, SCALES[0], jnp.float32)
    for index, scale in enumerate(SCALES[1:]):
        value = jnp.where(number > index + 0.5, scale, value)
    return value


def inverse_row(x_ref, ready=lambda lane: None):
    tokens, channels = x_ref.shape
    squares = None
    for lane in range(0, channels, HEAD_DIM):
        ready(lane)
        part = x_ref[:, lane : lane + HEAD_DIM].astype(jnp.float32)
        part = part * part
        squares = part if squares is None else squares + part
    total = jnp.sum(squares.T, axis=0, keepdims=True)
    return lax.rsqrt(total / channels + EPSILON)


def pack_kernel(rows, heads, x_hbm, c_hbm, *refs):
    outs = refs[: heads * 2]
    x_ref, c_ref, x_sem, c_sem = refs[heads * 2 :]
    tokens, channels = x_ref.shape
    row = lax.axis_index("row")
    col = lax.axis_index("col")
    parts = x_sem.shape[0]
    wide = channels // parts

    def fetch(source, target, sems, part):
        lanes = pl.ds(part * wide, wide)
        return pltpu.make_async_copy(source.at[:, lanes], target.at[:, lanes], sems.at[part])

    fetches = [fetch(x_hbm, x_ref, x_sem, part) for part in range(parts)]
    fetches += [fetch(c_hbm, c_ref, c_sem, part) for part in range(parts)]
    for copy in fetches:
        copy.start()

    def ready(lane):
        if lane % wide == 0:
            fetches[lane // wide].wait()

    inverse = inverse_row(x_ref, ready)
    for copy in fetches[parts:]:
        copy.wait()
    high = inverse.astype(jnp.bfloat16).astype(jnp.float32)
    mid = (inverse - high).astype(jnp.bfloat16).astype(jnp.float32)
    low = inverse - high - mid
    place = lax.broadcasted_iota(jnp.int32, (PIECES, tokens), 0)
    pieces = jnp.where(place == 0, high, jnp.where(place == 1, mid, jnp.where(place == 2, low, 0.0)))
    pieces = pieces.astype(jnp.bfloat16)
    for head in range(heads):
        for step in range(rows):
            for slot in range(2):
                first = ((row ^ step) * 2 + (col ^ slot)) * heads + head
                lanes = pl.ds(pl.multiple_of(first * HEAD_DIM, HEAD_DIM), HEAD_DIM)
                out = outs[head * 2 + slot]
                out[step, 0:tokens, :] = x_ref[:, lanes]
                out[step, tokens : 2 * tokens, :] = c_ref[:, lanes]
                if head == 0:
                    out[step, 2 * tokens :, :] = pieces


def attend_kernel(rows, heads, head, g_ref, *refs):
    held = rows + 1
    arrays, inverses = refs[0:held], refs[held : 2 * held]
    keep_ref, give_ref = refs[2 * held : 2 * held + 2]
    q_s, k_s, kt_s, v_s, d_s, p_s, ds_s, s_s, dp_s, dk_s, dv_s, dq_s = refs[2 * held + 2 :]
    tokens = keep_ref.shape[1] - EXTRA
    row = lax.axis_index("row")
    col = lax.axis_index("col")
    lanes = pl.ds(pl.multiple_of(((row * 2 + col) * heads + head) * HEAD_DIM, HEAD_DIM), HEAD_DIM)
    gn, gq, gk, gv, go = (g_ref[i : i + 1, lanes] for i in range(5))
    gq = gq * (1.0 / math.sqrt(HEAD_DIM))
    square = 2 * tokens
    pattern = (tokens // (2 * TILE), 2, TILE, tokens)
    query_right = (lax.broadcasted_iota(jnp.int32, pattern[1:], 2) // TILE) % 2
    key_right = lax.broadcasted_iota(jnp.int32, pattern[1:], 0)
    no_cap = float(jnp.finfo(jnp.float32).max)
    left_keys = jnp.where((key_right == 0) & (query_right == 1), NEGATIVE, no_cap)
    right_keys = jnp.where((key_right == 1) & (query_right == 0), NEGATIVE, no_cap)

    def capped(s, cap):
        return jnp.minimum(s.reshape(pattern), cap[None]).reshape(tokens, tokens)

    def block(step, slot):
        number, index = (slot, 0) if step == 0 else (step + 1, slot)
        ref = arrays[number]
        place = pl.multiple_of(((row ^ step) * 2 + (col ^ slot)) * tokens, tokens)
        x = ref[index, 0:tokens, :].astype(jnp.float32)
        c = ref[index, tokens : 2 * tokens, :].astype(jnp.float32)
        inverse = inverse_columns(inverses[number][index, 2 * tokens :, :])
        return pl.ds(place, tokens), x, c, inverse

    blocks = [(step, slot) for step in range(rows) for slot in range(2)]
    for step, slot in blocks:
        here, x, c, inverse = block(step, slot)
        normed = (x * inverse * gn).astype(jnp.bfloat16).astype(jnp.float32)
        q_s[here, :] = (normed * gq).astype(jnp.bfloat16)
        key = (normed * gk).astype(jnp.bfloat16)
        k_s[here, :] = key
        kt_s[:, here] = key.astype(jnp.float32).T.astype(jnp.bfloat16)
        v_s[here, :] = (normed * gv).astype(jnp.bfloat16)
        d_s[here, :] = (c * go).astype(jnp.bfloat16)

    contract_last = (((1,), (1,)), ((), ()))
    reach = SPAN // 2
    spans = []
    for at in range(rows):
        near = [r for r in range(rows) if abs(r - at) <= reach]
        spans.append((near[0] * square, (near[-1] + 1) * square))

    def own(at):
        return slice(at * square, (at + 1) * square)

    def cells(at):
        return [slice(start, start + square) for start in range(*spans[at], square)]

    def fold(combine, parts):
        total = parts[0]
        for part in parts[1:]:
            total = combine(total, part)
        return total

    def products(at, tops):
        buffer = at % 2
        q, d = q_s[own(at), :], d_s[own(at), :]
        left, right = [], []
        for cell in cells(at):
            s = lax.dot_general(k_s[cell, :], q, contract_last, preferred_element_type=jnp.float32)
            upper = slice(cell.start, cell.start + tokens)
            lower = slice(cell.start + tokens, cell.stop)
            upper_left, upper_right = s[0:tokens, 0:tokens], capped(s[0:tokens, tokens:], left_keys)
            lower_left, lower_right = capped(s[tokens:, 0:tokens], right_keys), s[tokens:, tokens:]
            s_s[buffer, upper, 0:tokens] = upper_left
            s_s[buffer, upper, tokens:] = upper_right
            s_s[buffer, lower, 0:tokens] = lower_left
            s_s[buffer, lower, tokens:] = lower_right
            left.append(jnp.max(jnp.maximum(upper_left, lower_left), axis=0, keepdims=True))
            right.append(jnp.max(jnp.maximum(upper_right, lower_right), axis=0, keepdims=True))
            yield
            dp_s[buffer, cell, :] = lax.dot_general(
                v_s[cell, :], d, contract_last, preferred_element_type=jnp.float32
            )
            yield
        tops[at] = jnp.concatenate([fold(jnp.maximum, left), fold(jnp.maximum, right)], axis=1)

    def softmax(at, tops):
        buffer = at % 2
        top = tops[at]
        sums = []
        for cell in cells(at):
            e = jnp.exp(s_s[buffer, cell, :] - top)
            s_s[buffer, cell, :] = e
            sums.append(jnp.sum(e, axis=0, keepdims=True))
            yield
        scale = 1.0 / fold(jnp.add, sums)
        sums = []
        for cell in cells(at):
            p = s_s[buffer, cell, :] * scale
            pb = p.astype(jnp.bfloat16)
            p_s[cell, own(at)] = pb
            sums.append(jnp.sum(pb.astype(jnp.float32) * dp_s[buffer, cell, :], axis=0, keepdims=True))
            yield
        delta = fold(jnp.add, sums)
        for cell in cells(at):
            p = s_s[buffer, cell, :] * scale
            ds_s[cell, own(at)] = (p * (dp_s[buffer, cell, :] - delta)).astype(jnp.bfloat16)
            yield

    def query_side(at):
        span = slice(*spans[at])
        dq = jnp.dot(kt_s[:, span], ds_s[span, own(at)], preferred_element_type=jnp.float32)
        yield
        dq_s[own(at), :] = dq.T
        yield

    def key_side(first, last):
        for at in range(rows):
            low, high = max(spans[at][0], first * square), min(spans[at][1], last * square)
            if low >= high:
                continue
            span = slice(low, high)
            dk = jnp.dot(ds_s[own(at), span], q_s[span, :], preferred_element_type=jnp.float32)
            fresh = low == spans[at][0]
            dk_s[own(at), :] = dk if fresh else dk_s[own(at), :] + dk
            yield
            dv = jnp.dot(p_s[own(at), span], d_s[span, :], preferred_element_type=jnp.float32)
            dv_s[own(at), :] = dv if fresh else dv_s[own(at), :] + dv
            yield

    def together(*works):
        works = list(works)
        while works:
            works = [work for work in works if next(work, works) is not works]


    def all_queries():
        dq = jnp.dot(kt_s[...], ds_s[...], preferred_element_type=jnp.float32)
        yield
        dq_s[...] = dq.T
        yield

    for at in range(rows):
        for other in range(rows):
            if abs(at - other) > reach:
                ds_s[own(at), own(other)] = jnp.zeros((square, square), jnp.bfloat16)
    tops = {}
    together(products(0, tops))
    for at in range(rows):
        works = [softmax(at, tops)]
        if at + 1 < rows:
            works.append(products(at + 1, tops))
        if at > 0:
            works += [key_side(at - 1, at)]
        together(*works)
    together(key_side(rows - 1, rows), all_queries())
    tops, shares = [], []
    for step, slot in blocks:
        here, x, c, inverse = block(step, slot)
        scaled = gn * (dq_s[here, :] * gq + dk_s[here, :] * gk + dv_s[here, :] * gv)
        value = c + inverse * scaled
        (keep_ref, give_ref)[slot][step, 0:tokens, :] = value
        tops.append(jnp.max(jnp.abs(value), axis=0, keepdims=True))
        shares.append(jnp.sum((x * scaled).T, axis=0, keepdims=True))
    top = jnp.max(jnp.concatenate(tops, axis=0), axis=1, keepdims=True)
    number = scale_number(jnp.broadcast_to(top, (len(blocks), tokens)))
    shrink = 1.0 / scale_value(number)
    share = jnp.concatenate(shares, axis=0)
    share_number = scale_number(jnp.abs(share))
    share = share / scale_value(share_number)
    high = share.astype(jnp.bfloat16).astype(jnp.float32)
    mid = (share - high).astype(jnp.bfloat16).astype(jnp.float32)
    low = share - high - mid
    place = lax.broadcasted_iota(jnp.int32, (EXTRA, tokens), 0)
    for index, (step, slot) in enumerate(blocks):
        out = (keep_ref, give_ref)[slot]
        at = slice(index, index + 1)
        out[step, 0:tokens, :] = out[step, 0:tokens, :] * shrink[at]
        extra = jnp.zeros((EXTRA, tokens), jnp.float32)
        for line, row_of in enumerate((number, share_number, high, mid, low)):
            extra = jnp.where(place == line, row_of[at], extra)
        out[step, tokens:, :] = extra


def attention_kernel(*operands):
    @pl.when(lax.axis_index("pipe") > 0)
    def _():
        attend_kernel(*operands)


def cube_kernel(x_ref, out_ref):
    inverse = inverse_row(x_ref)
    out_ref[...] = row_to_column(inverse * inverse * inverse)


def collect_kernel(rows, heads, x_ref, cube_ref, *refs):
    units = refs[:rows]
    out_hbm, out_ref, sems = refs[rows:]
    tokens, channels = x_ref.shape
    row = lax.axis_index("row")
    col = lax.axis_index("col")
    last = lax.axis_index("pipe") == lax.axis_size("pipe") - 1
    total, scales = None, {}
    for step in range(rows):
        for slot in range(2 * heads):
            extra = units[step][slot, tokens : tokens + 8, :]
            value = scale_value(extra)
            scales[step, slot] = value[0:1]
            share = (extra[2:3] + extra[3:4] + extra[4:5]) * value[1:2]
            total = share if total is None else total + share
    weight = cube_ref[...] * row_to_column(total / channels)
    wide = 2 * heads * HEAD_DIM
    copies = []
    for step in range(rows):
        for slot in range(2 * heads):
            first = ((row ^ step) * 2 + (col ^ (slot // heads))) * heads + slot % heads
            lanes = pl.ds(pl.multiple_of(first * HEAD_DIM, HEAD_DIM), HEAD_DIM)
            grad = units[step][slot, 0:tokens, :] * scales[step, slot] - x_ref[:, lanes].astype(jnp.float32) * weight
            out_ref[:, lanes] = jnp.where(last, 0.0, grad).astype(jnp.bfloat16)
        lanes = pl.ds(pl.multiple_of((row ^ step) * wide, wide), wide)
        copies.append(pltpu.make_async_copy(out_ref.at[:, lanes], out_hbm.at[:, lanes], sems.at[step]))
        copies[-1].start()
    for copy in copies:
        copy.wait()


def local_call(kernel, out_shape, scratch_shapes=(), **placed):
    return pl.pallas_call(
        kernel,
        out_shape=out_shape,
        **placed,
        scratch_shapes=scratch_shapes,
        compiler_params=pltpu.CompilerParams(vmem_limit_bytes=24 * 1024 * 1024),
    )


def near(arrays):
    return [pltpu.with_memory_space_constraint(array, pltpu.VMEM) for array in arrays]


def split_heads_per_device(saved_in, cotangent, section_gains):
    pipes, rows, cols = (lax.axis_size(name) for name in ("pipe", "row", "col"))
    channels = saved_in.shape[-1]
    tokens = saved_in.shape[1] * saved_in.shape[2]
    heads = channels // HEAD_DIM // (rows * cols)
    plane = ("row", "col")
    sizes = (rows, cols)
    bf, f32 = jnp.bfloat16, jnp.float32
    x = saved_in.reshape(tokens, channels)
    c = cotangent.reshape(tokens, channels)
    gains = section_gains[0]
    packets = []
    for head in range(heads):
        packets += [pltpu.VMEM((rows, 2 * tokens + (PIECES if head == 0 else 0), HEAD_DIM), bf)] * 2
    far = pl.BlockSpec(memory_space=pltpu.HBM)
    staged = [pltpu.VMEM((tokens, channels), bf)] * 2 + [pltpu.SemaphoreType.DMA((4,))] * 2
    packed = local_call(functools.partial(pack_kernel, rows, heads), packets, staged, in_specs=[far, far])(
        pltpu.with_memory_space_constraint(x, pltpu.HBM), pltpu.with_memory_space_constraint(c, pltpu.HBM)
    )
    passed = [lax.ppermute(packed[2 * head + 1], plane, crossing(sizes, 0, 1)) for head in range(heads)]
    arrays = []
    for head in range(heads):
        own, other = packed[2 * head], passed[head]
        held = [own, other]
        packets = [jnp.stack([own[step], other[step]]) for step in range(1, rows)]
        if head > 0:
            packets, arrays[head - 1][2] = lax.optimization_barrier((packets, arrays[head - 1][2]))
        for step in range(1, rows):
            held.append(lax.ppermute(packets[step - 1], plane, crossing(sizes, step, 0)))
        arrays.append(held)
    count = rows * cols * tokens
    square = 2 * tokens
    scratch = [
        pltpu.VMEM((count, HEAD_DIM), bf),
        pltpu.VMEM((count, HEAD_DIM), bf),
        pltpu.VMEM((HEAD_DIM, count), bf),
        pltpu.VMEM((count, HEAD_DIM), bf),
        pltpu.VMEM((count, HEAD_DIM), bf),
        pltpu.VMEM((count, count), bf),
        pltpu.VMEM((count, count), bf),
        pltpu.VMEM((2, count, square), f32),
        pltpu.VMEM((2, count, square), f32),
        pltpu.VMEM((count, HEAD_DIM), f32),
        pltpu.VMEM((count, HEAD_DIM), f32),
        pltpu.VMEM((count, HEAD_DIM), f32),
    ]
    behind = [(pipe, (pipe - 1) % pipes) for pipe in range(pipes)]
    arrays[0][1], free_x = lax.optimization_barrier((arrays[0][1], x))
    x_ahead = lax.ppermute(free_x, "pipe", behind)
    part = pltpu.VMEM((rows, tokens + EXTRA, HEAD_DIM), f32)
    keep, got = [], []
    for head in range(heads):
        kept, given = local_call(
            functools.partial(attention_kernel, rows, heads, head), [part, part], scratch
        )(gains, *near(arrays[head]), *near(arrays[0]))
        if head == heads - 1:
            given, x_ahead = lax.optimization_barrier((given, x_ahead))
        keep.append(kept.astype(jnp.float16))
        got.append(lax.ppermute(given.astype(jnp.float16), plane, crossing(sizes, 0, 1)))
    units = []
    for step in range(rows):
        sent = jnp.stack([unit[step] for unit in keep + got])
        sent = lax.ppermute(sent, ("pipe",) + plane, crossing_back((pipes, rows, cols), step))
        units.append(sent.astype(f32))
    cube = local_call(cube_kernel, pltpu.VMEM((tokens, HEAD_DIM), f32))(*near([x_ahead]))
    out = local_call(
        functools.partial(collect_kernel, rows, heads),
        jax.ShapeDtypeStruct((tokens, channels), bf),
        [pltpu.VMEM((tokens, channels), bf), pltpu.SemaphoreType.DMA((rows,))],
        out_specs=far,
    )(*near([x_ahead, cube] + units))
    return out.reshape(saved_in.shape)


def per_device(saved_in, cotangent, section_gains):
    rows, cols = lax.axis_size("row"), lax.axis_size("col")
    block_fits = saved_in.shape[1] == TILE and saved_in.shape[2] == 2 * TILE
    devices_fit = cols == 2 and rows & (rows - 1) == 0 and HEADS % (rows * cols) == 0
    plan = split_heads_per_device if block_fits and devices_fit else halo_per_device
    return plan(saved_in, cotangent, section_gains)


def solution(mesh):
    return jax.shard_map(
        per_device,
        mesh=mesh,
        in_specs=(
            P("pipe", "row", "col", None),
            P("pipe", "row", "col", None),
            P("pipe", None, None),
        ),
        out_specs=P("pipe", "row", "col", None),
        check_vma=False,
    )
```

```python
import functools
import math

import jax
import jax.numpy as jnp
from jax import lax
from jax.experimental import pallas as pl
from jax.experimental.pallas import tpu as pltpu
from jax.sharding import PartitionSpec as P

HEADS = 16
HEAD_DIM = 128
TILE = 8
SPAN = 5


NEGATIVE = -1e30
EPSILON = 1e-06


def passed_along(block, axis, distance):
    devices = range(lax.axis_size(axis))
    route = [(i - distance, i) for i in devices if i - distance in devices]
    return lax.ppermute(block, axis, route)


def to_tiles(image):
    lead = image.shape[:-3]
    height, width, channels = image.shape[-3:]
    count = len(lead)
    image = image.reshape(lead + (height // TILE, TILE, width // TILE, TILE, channels))
    order = tuple(range(count)) + (count, count + 2, count + 1, count + 3, count + 4)
    return image.transpose(order).reshape(
        lead + (height // TILE, width // TILE, TILE * TILE, channels)
    )


def from_tiles(tiled):
    tile_rows, tile_cols, area, channels = tiled.shape
    tiled = tiled.reshape(tile_rows, tile_cols, TILE, TILE, channels)
    return tiled.transpose(0, 2, 1, 3, 4).reshape(tile_rows * TILE, tile_cols * TILE, channels)


def windows(extended, tile_rows, tile_cols):
    return jnp.concatenate(
        [
            extended[row_off : row_off + tile_rows, col_off : col_off + tile_cols]
            for row_off in range(SPAN)
            for col_off in range(SPAN)
        ],
        axis=2,
    )


def key_valid(base_row, base_col, tile_rows, tile_cols, all_rows, all_cols):
    reach_tiles = SPAN // 2
    offsets = jnp.arange(SPAN, dtype=jnp.int32) - reach_tiles
    row_ids = base_row + jnp.arange(tile_rows, dtype=jnp.int32)[:, None] + offsets[None, :]
    col_ids = base_col + jnp.arange(tile_cols, dtype=jnp.int32)[:, None] + offsets[None, :]
    row_ok = (row_ids >= 0) & (row_ids < all_rows)
    col_ok = (col_ids >= 0) & (col_ids < all_cols)
    allowed = row_ok[:, None, :, None] & col_ok[None, :, None, :]
    return jnp.repeat(allowed.reshape(tile_rows, tile_cols, SPAN * SPAN), TILE * TILE, axis=2)


def project(normed, scales, factor):
    return (normed.astype(jnp.float32) * (scales * factor)).astype(jnp.bfloat16)


def normalize(image, scales):
    x_float = image.astype(jnp.float32)
    inverse = lax.rsqrt(jnp.mean(x_float * x_float, axis=-1, keepdims=True) + EPSILON)
    return (x_float, inverse, (x_float * inverse * scales).astype(jnp.bfloat16))


def widen(array, dim, reach, move):
    own = array.shape[dim]
    need = -(-reach // own)
    above = []
    below = []
    for step_by in range(need, 0, -1):
        lower_end = max(-step_by * own, -reach)
        upper_end = -(step_by - 1) * own
        piece = array
        above.append(move(piece, step_by))
    for step_by in range(1, need + 1):
        length = min((step_by + 1) * own, own + reach) - step_by * own
        piece = array
        below.append(move(piece, -step_by))
    return jnp.concatenate(above + [array] + below, axis=dim)


def halo_per_device(saved_in, cotangent, section_gains):
    scales = section_gains[0]
    reach_tiles = SPAN // 2
    reach_cells = TILE * reach_tiles
    factor = 1.0 / math.sqrt(HEAD_DIM)
    tile_rows = saved_in.shape[1] // TILE
    tile_cols = saved_in.shape[2] // TILE
    allowed = key_valid(
        lax.axis_index("row") * tile_rows,
        lax.axis_index("col") * tile_cols,
        tile_rows,
        tile_cols,
        tile_rows * lax.axis_size("row"),
        tile_cols * lax.axis_size("col"),
    )
    saved_float, saved_inverse, saved_normed = normalize(saved_in[0], scales[0])
    upstream_image = cotangent[0].astype(jnp.float32)
    grad_image = (upstream_image * scales[4]).astype(jnp.bfloat16)
    paired = jnp.stack([saved_normed, grad_image])

    def move_cols(piece, step_by):
        return passed_along(piece, "col", step_by)

    def move_rows(piece, step_by):
        return passed_along(piece, "row", step_by)

    paired_wide = widen(widen(paired, 2, reach_cells, move_cols), 1, reach_cells, move_rows)
    paired_ext = to_tiles(paired_wide)
    normed_ext = paired_ext[0]
    grad_ext = paired_ext[1]
    normed_tiles = to_tiles(saved_normed)
    grad_tiles = to_tiles(grad_image)
    stat_shape = (HEADS, tile_rows, tile_cols, TILE * TILE)

    def own_head(head, carry):
        dnormed, log_all, delta_all = carry
        start = head * HEAD_DIM

        def part(array):
            return lax.dynamic_slice_in_dim(array, start, HEAD_DIM, array.ndim - 1)

        queries = project(part(normed_tiles), part(scales[1]), factor)
        key_win = windows(project(part(normed_ext), part(scales[2]), 1.0), tile_rows, tile_cols)
        value_win = windows(project(part(normed_ext), part(scales[3]), 1.0), tile_rows, tile_cols)
        scores = jnp.einsum("ijqc,ijkc->ijqk", queries, key_win, preferred_element_type=jnp.float32)
        scores = jnp.where(allowed[:, :, None, :], scores, NEGATIVE)
        row_max = jnp.max(scores, axis=-1, keepdims=True)
        log_total = row_max + jnp.log(jnp.sum(jnp.exp(scores - row_max), axis=-1, keepdims=True))
        weights = jnp.exp(scores - log_total)
        rounded = weights.astype(jnp.bfloat16)
        output = jnp.einsum(
            "ijqk,ijkc->ijqc", rounded, value_win, preferred_element_type=jnp.float32
        )
        grads = part(grad_tiles)
        delta_sum = jnp.sum(grads.astype(jnp.float32) * output, axis=-1)
        prob_grad = jnp.einsum(
            "ijqc,ijkc->ijqk", grads, value_win, preferred_element_type=jnp.float32
        )
        dscore = (weights * (prob_grad - delta_sum[..., None])).astype(jnp.bfloat16)
        dquery = jnp.einsum("ijqk,ijkc->ijqc", dscore, key_win, preferred_element_type=jnp.float32)
        dnormed = lax.dynamic_update_slice_in_dim(
            dnormed, dquery * (part(scales[1]) * factor), start, 3
        )
        log_all = log_all.at[head].set(log_total[..., 0])
        delta_all = delta_all.at[head].set(delta_sum)
        return (dnormed, log_all, delta_all)

    dnormed, log_all, delta_all = lax.fori_loop(
        0,
        HEADS,
        own_head,
        (
            jnp.zeros(normed_tiles.shape, jnp.float32),
            jnp.zeros(stat_shape, jnp.float32),
            jnp.zeros(stat_shape, jnp.float32),
        ),
    )
    stat_tiles = jnp.concatenate([log_all, delta_all], axis=0).transpose(1, 2, 3, 0)

    def stat_cols(piece, step_by):
        return passed_along(piece, "col", step_by)

    def stat_rows(piece, step_by):
        return passed_along(piece, "row", step_by)

    stat_wide = widen(
        widen(from_tiles(stat_tiles), 1, reach_cells, stat_cols), 0, reach_cells, stat_rows
    )
    stat_win = windows(to_tiles(stat_wide), tile_rows, tile_cols)

    def far_head(head, dnormed):
        start = head * HEAD_DIM

        def part(array):
            return lax.dynamic_slice_in_dim(array, start, HEAD_DIM, array.ndim - 1)

        query_win = windows(
            project(part(normed_ext), part(scales[1]), factor), tile_rows, tile_cols
        )
        grad_win = windows(part(grad_ext), tile_rows, tile_cols)
        own_keys = project(part(normed_tiles), part(scales[2]), 1.0)
        own_values = project(part(normed_tiles), part(scales[3]), 1.0)
        far_log = lax.dynamic_index_in_dim(stat_win, head, 3, keepdims=False)
        far_delta = lax.dynamic_index_in_dim(stat_win, HEADS + head, 3, keepdims=False)
        scores = jnp.einsum(
            "ijqc,ijkc->ijqk", query_win, own_keys, preferred_element_type=jnp.float32
        )
        weights = jnp.exp(jnp.where(allowed[..., None], scores - far_log[..., None], NEGATIVE))
        prob_grad = jnp.einsum(
            "ijqc,ijkc->ijqk", grad_win, own_values, preferred_element_type=jnp.float32
        )
        dscore = (weights * (prob_grad - far_delta[..., None])).astype(jnp.bfloat16)
        key_grad = jnp.einsum(
            "ijqk,ijqc->ijkc", dscore, query_win, preferred_element_type=jnp.float32
        )
        dvalue = jnp.einsum(
            "ijqk,ijqc->ijkc",
            weights.astype(jnp.bfloat16),
            grad_win,
            preferred_element_type=jnp.float32,
        )
        terms = key_grad * part(scales[2]) + dvalue * part(scales[3])
        return lax.dynamic_update_slice_in_dim(dnormed, part(dnormed) + terms, start, 3)

    dnormed = lax.fori_loop(0, HEADS, far_head, dnormed)
    scaled = scales[0] * dnormed
    x_tiles = to_tiles(saved_float)
    inv_tiles = to_tiles(saved_inverse)
    upstream = to_tiles(upstream_image)
    image_grad = (
        upstream
        + inv_tiles * scaled
        - x_tiles
        * (inv_tiles * inv_tiles * inv_tiles)
        * jnp.mean(x_tiles * scaled, axis=-1, keepdims=True)
    )
    sent_back = passed_along(from_tiles(image_grad.astype(jnp.bfloat16)), "pipe", -1)
    return sent_back[None]


PIECES = 16


EXTRA = 8
SCALES = [2.0 ** (12 * power) for power in range(-8, 11)]


def crossing(sizes, row_step, col_step):
    rows, cols = sizes
    return [
        (row * cols + col, (row ^ row_step) * cols + (col ^ col_step))
        for row in range(rows)
        for col in range(cols)
    ]


def crossing_back(sizes, row_step):
    pipes, rows, cols = sizes
    return [
        (
            (pipe * rows + row) * cols + col,
            ((pipe - 1) % pipes * rows + (row ^ row_step)) * cols + col,
        )
        for pipe in range(pipes)
        for row in range(rows)
        for col in range(cols)
    ]


def row_to_column(row):
    return jnp.broadcast_to(row, (row.shape[1], row.shape[1])).T


def inverse_columns(pieces):
    pieces = pieces.astype(jnp.float32)
    return row_to_column(pieces[0:1] + pieces[1:2] + pieces[2:3])


def scale_number(size):
    return sum((size >= scale).astype(jnp.float32) for scale in SCALES[1:])


def scale_value(number):
    value = jnp.full(number.shape, SCALES[0], jnp.float32)
    for index, scale in enumerate(SCALES[1:]):
        value = jnp.where(number > index + 0.5, scale, value)
    return value


def inverse_row(x_ref):
    tokens, channels = x_ref.shape
    squares = None
    for lane in range(0, channels, HEAD_DIM):
        part = x_ref[:, lane : lane + HEAD_DIM].astype(jnp.float32)
        part = part * part
        squares = part if squares is None else squares + part
    total = jnp.sum(squares.T, axis=0, keepdims=True)
    return lax.rsqrt(total / channels + EPSILON)


def pack_kernel(rows, heads, x_hbm, c_hbm, *refs):
    outs = refs[: heads * 2]
    x_ref, c_ref, x_sem, c_sem = refs[heads * 2 :]
    tokens, channels = x_ref.shape
    row = lax.axis_index("row")
    col = lax.axis_index("col")
    parts = x_sem.shape[0]
    high_rows = tokens // parts

    def fetch(source, target, sems, part):
        here = pl.ds(part * high_rows, high_rows)
        return pltpu.make_async_copy(source.at[here, :], target.at[here, :], sems.at[part])

    fetches = [fetch(x_hbm, x_ref, x_sem, part) for part in range(parts)]
    fetches += [fetch(c_hbm, c_ref, c_sem, part) for part in range(parts)]
    for copy in fetches:
        copy.start()
    for copy in fetches[:parts]:
        copy.wait()
    inverse = inverse_row(x_ref)
    high = inverse.astype(jnp.bfloat16).astype(jnp.float32)
    mid = (inverse - high).astype(jnp.bfloat16).astype(jnp.float32)
    low = inverse - high - mid
    place = lax.broadcasted_iota(jnp.int32, (PIECES, tokens), 0)
    pieces = jnp.where(place == 0, high, jnp.where(place == 1, mid, jnp.where(place == 2, low, 0.0)))
    pieces = pieces.astype(jnp.bfloat16)
    for source, low in ((x_ref, 0), (c_ref, tokens)):
        if low > 0:
            for copy in fetches[parts:]:
                copy.wait()
        for head in range(heads):
            for step in range(rows):
                for slot in range(2):
                    first = ((row ^ step) * 2 + (col ^ slot)) * heads + head
                    lanes = pl.ds(pl.multiple_of(first * HEAD_DIM, HEAD_DIM), HEAD_DIM)
                    out = outs[head * 2 + slot]
                    out[step, low : low + tokens, :] = source[:, lanes]
                    if head == 0 and low == 0:
                        out[step, 2 * tokens :, :] = pieces


def attend_kernel(rows, heads, head, g_ref, *refs):
    held = rows + 1
    arrays, inverses = refs[0:held], refs[held : 2 * held]
    keep_ref, give_ref = refs[2 * held : 2 * held + 2]
    q_s, k_s, kt_s, v_s, d_s, p_s, ds_s, s_s, dp_s, dk_s, dv_s, dq_s = refs[2 * held + 2 :]
    tokens = keep_ref.shape[1] - EXTRA
    row = lax.axis_index("row")
    col = lax.axis_index("col")
    lanes = pl.ds(pl.multiple_of(((row * 2 + col) * heads + head) * HEAD_DIM, HEAD_DIM), HEAD_DIM)
    gn, gq, gk, gv, go = (g_ref[i : i + 1, lanes] for i in range(5))
    gq = gq * (1.0 / math.sqrt(HEAD_DIM))
    square = 2 * tokens
    pattern = (tokens // (2 * TILE), 2, TILE, tokens)
    query_right = (lax.broadcasted_iota(jnp.int32, pattern[1:], 2) // TILE) % 2
    key_right = lax.broadcasted_iota(jnp.int32, pattern[1:], 0)
    no_cap = float(jnp.finfo(jnp.float32).max)
    left_keys = jnp.where((key_right == 0) & (query_right == 1), NEGATIVE, no_cap)
    right_keys = jnp.where((key_right == 1) & (query_right == 0), NEGATIVE, no_cap)

    def capped(s, cap):
        return jnp.minimum(s.reshape(pattern), cap[None]).reshape(tokens, tokens)

    def block(step, slot):
        number, index = (slot, 0) if step == 0 else (step + 1, slot)
        ref = arrays[number]
        place = pl.multiple_of(((row ^ step) * 2 + (col ^ slot)) * tokens, tokens)
        x = ref[index, 0:tokens, :].astype(jnp.float32)
        c = ref[index, tokens : 2 * tokens, :].astype(jnp.float32)
        inverse = inverse_columns(inverses[number][index, 2 * tokens :, :])
        return pl.ds(place, tokens), x, c, inverse

    blocks = [(step, slot) for step in range(rows) for slot in range(2)]
    for step, slot in blocks:
        here, x, c, inverse = block(step, slot)
        normed = (x * inverse * gn).astype(jnp.bfloat16).astype(jnp.float32)
        q_s[here, :] = (normed * gq).astype(jnp.bfloat16)
        key = (normed * gk).astype(jnp.bfloat16)
        k_s[here, :] = key
        kt_s[:, here] = key.astype(jnp.float32).T.astype(jnp.bfloat16)
        v_s[here, :] = (normed * gv).astype(jnp.bfloat16)
        d_s[here, :] = (c * go).astype(jnp.bfloat16)

    contract_last = (((1,), (1,)), ((), ()))
    reach = SPAN // 2
    spans = []
    for at in range(rows):
        near = [r for r in range(rows) if abs(r - at) <= reach]
        spans.append((near[0] * square, (near[-1] + 1) * square))

    def own(at):
        return slice(at * square, (at + 1) * square)

    def cells(at):
        return [slice(start, start + square) for start in range(*spans[at], square)]

    def fold(combine, parts):
        total = parts[0]
        for part in parts[1:]:
            total = combine(total, part)
        return total

    def products(at, tops):
        buffer = at % 2
        q, d = q_s[own(at), :], d_s[own(at), :]
        left, right = [], []
        for cell in cells(at):
            s = lax.dot_general(k_s[cell, :], q, contract_last, preferred_element_type=jnp.float32)
            upper = slice(cell.start, cell.start + tokens)
            lower = slice(cell.start + tokens, cell.stop)
            upper_left, upper_right = s[0:tokens, 0:tokens], capped(s[0:tokens, tokens:], left_keys)
            lower_left, lower_right = capped(s[tokens:, 0:tokens], right_keys), s[tokens:, tokens:]
            s_s[buffer, upper, 0:tokens] = upper_left
            s_s[buffer, upper, tokens:] = upper_right
            s_s[buffer, lower, 0:tokens] = lower_left
            s_s[buffer, lower, tokens:] = lower_right
            left.append(jnp.max(jnp.maximum(upper_left, lower_left), axis=0, keepdims=True))
            right.append(jnp.max(jnp.maximum(upper_right, lower_right), axis=0, keepdims=True))
            yield
            dp_s[buffer, cell, :] = lax.dot_general(
                v_s[cell, :], d, contract_last, preferred_element_type=jnp.float32
            )
            yield
        tops[at] = jnp.concatenate([fold(jnp.maximum, left), fold(jnp.maximum, right)], axis=1)

    def softmax(at, tops):
        buffer = at % 2
        top = tops[at]
        sums = []
        for cell in cells(at):
            e = jnp.exp(s_s[buffer, cell, :] - top)
            s_s[buffer, cell, :] = e
            sums.append(jnp.sum(e, axis=0, keepdims=True))
            yield
        scale = 1.0 / fold(jnp.add, sums)
        sums = []
        for cell in cells(at):
            p = s_s[buffer, cell, :] * scale
            pb = p.astype(jnp.bfloat16)
            p_s[cell, own(at)] = pb
            sums.append(jnp.sum(pb.astype(jnp.float32) * dp_s[buffer, cell, :], axis=0, keepdims=True))
            yield
        delta = fold(jnp.add, sums)
        for cell in cells(at):
            p = s_s[buffer, cell, :] * scale
            ds_s[cell, own(at)] = (p * (dp_s[buffer, cell, :] - delta)).astype(jnp.bfloat16)
            yield

    def query_side(at):
        span = slice(*spans[at])
        dq = jnp.dot(kt_s[:, span], ds_s[span, own(at)], preferred_element_type=jnp.float32)
        yield
        dq_s[own(at), :] = dq.T
        yield

    def key_side(first, last):
        for at in range(rows):
            low, high = max(spans[at][0], first * square), min(spans[at][1], last * square)
            if low >= high:
                continue
            span = slice(low, high)
            dk = jnp.dot(ds_s[own(at), span], q_s[span, :], preferred_element_type=jnp.float32)
            fresh = low == spans[at][0]
            dk_s[own(at), :] = dk if fresh else dk_s[own(at), :] + dk
            yield
            dv = jnp.dot(p_s[own(at), span], d_s[span, :], preferred_element_type=jnp.float32)
            dv_s[own(at), :] = dv if fresh else dv_s[own(at), :] + dv
            yield

    def together(*works):
        works = list(works)
        while works:
            works = [work for work in works if next(work, works) is not works]


    def all_queries():
        dq = jnp.dot(kt_s[...], ds_s[...], preferred_element_type=jnp.float32)
        yield
        dq_s[...] = dq.T
        yield

    for at in range(rows):
        for other in range(rows):
            if abs(at - other) > reach:
                ds_s[own(at), own(other)] = jnp.zeros((square, square), jnp.bfloat16)
    tops = {}
    together(products(0, tops))
    for at in range(rows):
        works = [softmax(at, tops)]
        if at + 1 < rows:
            works.append(products(at + 1, tops))
        if at > 0:
            works += [key_side(at - 1, at)]
        together(*works)
    together(key_side(rows - 1, rows), all_queries())
    tops, shares = [], []
    for step, slot in blocks:
        here, x, c, inverse = block(step, slot)
        scaled = gn * (dq_s[here, :] * gq + dk_s[here, :] * gk + dv_s[here, :] * gv)
        value = c + inverse * scaled
        (keep_ref, give_ref)[slot][step, 0:tokens, :] = value
        tops.append(jnp.max(jnp.abs(value), axis=0, keepdims=True))
        shares.append(jnp.sum((x * scaled).T, axis=0, keepdims=True))
    top = jnp.max(jnp.concatenate(tops, axis=0), axis=1, keepdims=True)
    number = scale_number(jnp.broadcast_to(top, (len(blocks), tokens)))
    shrink = 1.0 / scale_value(number)
    share = jnp.concatenate(shares, axis=0)
    share_number = scale_number(jnp.abs(share))
    share = share / scale_value(share_number)
    high = share.astype(jnp.bfloat16).astype(jnp.float32)
    mid = (share - high).astype(jnp.bfloat16).astype(jnp.float32)
    low = share - high - mid
    place = lax.broadcasted_iota(jnp.int32, (EXTRA, tokens), 0)
    for index, (step, slot) in enumerate(blocks):
        out = (keep_ref, give_ref)[slot]
        at = slice(index, index + 1)
        out[step, 0:tokens, :] = out[step, 0:tokens, :] * shrink[at]
        extra = jnp.zeros((EXTRA, tokens), jnp.float32)
        for line, row_of in enumerate((number, share_number, high, mid, low)):
            extra = jnp.where(place == line, row_of[at], extra)
        out[step, tokens:, :] = extra


def attention_kernel(*operands):
    @pl.when(lax.axis_index("pipe") > 0)
    def _():
        attend_kernel(*operands)


def cube_kernel(x_ref, out_ref):
    inverse = inverse_row(x_ref)
    out_ref[...] = row_to_column(inverse * inverse * inverse)


def collect_kernel(rows, heads, x_ref, cube_ref, *refs):
    units = refs[:rows]
    out_hbm, out_ref, sems = refs[rows:]
    tokens, channels = x_ref.shape
    row = lax.axis_index("row")
    col = lax.axis_index("col")
    last = lax.axis_index("pipe") == lax.axis_size("pipe") - 1
    total, scales = None, {}
    for step in range(rows):
        for slot in range(2 * heads):
            extra = units[step][slot, tokens : tokens + 8, :]
            value = scale_value(extra)
            scales[step, slot] = value[0:1]
            share = (extra[2:3] + extra[3:4] + extra[4:5]) * value[1:2]
            total = share if total is None else total + share
    weight = cube_ref[...] * row_to_column(total / channels)
    wide = 2 * heads * HEAD_DIM
    copies = []
    for step in range(rows):
        for slot in range(2 * heads):
            first = ((row ^ step) * 2 + (col ^ (slot // heads))) * heads + slot % heads
            lanes = pl.ds(pl.multiple_of(first * HEAD_DIM, HEAD_DIM), HEAD_DIM)
            grad = units[step][slot, 0:tokens, :] * scales[step, slot] - x_ref[:, lanes].astype(jnp.float32) * weight
            out_ref[:, lanes] = jnp.where(last, 0.0, grad).astype(jnp.bfloat16)
        lanes = pl.ds(pl.multiple_of((row ^ step) * wide, wide), wide)
        copies.append(pltpu.make_async_copy(out_ref.at[:, lanes], out_hbm.at[:, lanes], sems.at[step]))
        copies[-1].start()
    for copy in copies:
        copy.wait()


def local_call(kernel, out_shape, scratch_shapes=(), **placed):
    return pl.pallas_call(
        kernel,
        out_shape=out_shape,
        **placed,
        scratch_shapes=scratch_shapes,
        compiler_params=pltpu.CompilerParams(vmem_limit_bytes=24 * 1024 * 1024),
    )


def near(arrays):
    return [pltpu.with_memory_space_constraint(array, pltpu.VMEM) for array in arrays]


def split_heads_per_device(saved_in, cotangent, section_gains):
    pipes, rows, cols = (lax.axis_size(name) for name in ("pipe", "row", "col"))
    channels = saved_in.shape[-1]
    tokens = saved_in.shape[1] * saved_in.shape[2]
    heads = channels // HEAD_DIM // (rows * cols)
    plane = ("row", "col")
    sizes = (rows, cols)
    bf, f32 = jnp.bfloat16, jnp.float32
    x = saved_in.reshape(tokens, channels)
    c = cotangent.reshape(tokens, channels)
    gains = section_gains[0]
    packets = []
    for head in range(heads):
        packets += [pltpu.VMEM((rows, 2 * tokens + (PIECES if head == 0 else 0), HEAD_DIM), bf)] * 2
    far = pl.BlockSpec(memory_space=pltpu.HBM)
    staged = [pltpu.VMEM((tokens, channels), bf)] * 2 + [pltpu.SemaphoreType.DMA((1,))] * 2
    packed = local_call(functools.partial(pack_kernel, rows, heads), packets, staged, in_specs=[far, far])(
        pltpu.with_memory_space_constraint(x, pltpu.HBM), pltpu.with_memory_space_constraint(c, pltpu.HBM)
    )

    def swap(array):
        return lax.ppermute(array, plane, crossing(sizes, 0, 1))

    passed = [[swap(packed[1][1:2]), swap(packed[1][2:]), swap(packed[1][0:1])]]
    passed += [swap(packed[2 * head + 1]) for head in range(1, heads)]
    arrays = []
    for head in range(heads):
        own, other = packed[2 * head], passed[head]
        if head == 0:
            held = [own, other[2]]
            packets = [jnp.concatenate([own[1:2], other[0]])]
            packets += [jnp.stack([own[step], other[1][step - 2]]) for step in range(2, rows)]
        else:
            held = [own, other]
            packets = [jnp.stack([own[step], other[step]]) for step in range(1, rows)]
        if head > 0:
            packets, arrays[head - 1][2] = lax.optimization_barrier((packets, arrays[head - 1][2]))
        for step in range(1, rows):
            held.append(lax.ppermute(packets[step - 1], plane, crossing(sizes, step, 0)))
        arrays.append(held)
    count = rows * cols * tokens
    square = 2 * tokens
    scratch = [
        pltpu.VMEM((count, HEAD_DIM), bf),
        pltpu.VMEM((count, HEAD_DIM), bf),
        pltpu.VMEM((HEAD_DIM, count), bf),
        pltpu.VMEM((count, HEAD_DIM), bf),
        pltpu.VMEM((count, HEAD_DIM), bf),
        pltpu.VMEM((count, count), bf),
        pltpu.VMEM((count, count), bf),
        pltpu.VMEM((2, count, square), f32),
        pltpu.VMEM((2, count, square), f32),
        pltpu.VMEM((count, HEAD_DIM), f32),
        pltpu.VMEM((count, HEAD_DIM), f32),
        pltpu.VMEM((count, HEAD_DIM), f32),
    ]
    behind = [(pipe, (pipe - 1) % pipes) for pipe in range(pipes)]
    arrays[0][2], free_x = lax.optimization_barrier((arrays[0][2], x))
    x_ahead = lax.ppermute(free_x, "pipe", behind)
    part = pltpu.VMEM((rows, tokens + EXTRA, HEAD_DIM), f32)
    keep, got = [], []
    for head in range(heads):
        kept, given = local_call(
            functools.partial(attention_kernel, rows, heads, head), [part, part], scratch
        )(gains, *near(arrays[head]), *near(arrays[0]))
        if head == heads - 1:
            given, x_ahead = lax.optimization_barrier((given, x_ahead))
        keep.append(kept.astype(jnp.float16))
        got.append(lax.ppermute(given.astype(jnp.float16), plane, crossing(sizes, 0, 1)))
    units = []
    for step in range(rows):
        sent = jnp.stack([unit[step] for unit in keep + got])
        sent = lax.ppermute(sent, ("pipe",) + plane, crossing_back((pipes, rows, cols), step))
        units.append(sent.astype(f32))
    cube = local_call(cube_kernel, pltpu.VMEM((tokens, HEAD_DIM), f32))(*near([x_ahead]))
    out = local_call(
        functools.partial(collect_kernel, rows, heads),
        jax.ShapeDtypeStruct((tokens, channels), bf),
        [pltpu.VMEM((tokens, channels), bf), pltpu.SemaphoreType.DMA((rows,))],
        out_specs=far,
    )(*near([x_ahead, cube] + units))
    return out.reshape(saved_in.shape)


def per_device(saved_in, cotangent, section_gains):
    rows, cols = lax.axis_size("row"), lax.axis_size("col")
    block_fits = saved_in.shape[1] == TILE and saved_in.shape[2] == 2 * TILE
    devices_fit = cols == 2 and rows & (rows - 1) == 0 and HEADS % (rows * cols) == 0
    plan = split_heads_per_device if block_fits and devices_fit else halo_per_device
    return plan(saved_in, cotangent, section_gains)


def solution(mesh):
    return jax.shard_map(
        per_device,
        mesh=mesh,
        in_specs=(
            P("pipe", "row", "col", None),
            P("pipe", "row", "col", None),
            P("pipe", None, None),
        ),
        out_specs=P("pipe", "row", "col", None),
        check_vma=False,
    )
```

```python
import functools
import math

import jax
import jax.numpy as jnp
from jax import lax
from jax.experimental import pallas as pl
from jax.experimental.pallas import tpu as pltpu
from jax.sharding import PartitionSpec as P

HEADS = 16
HEAD_DIM = 128
TILE = 8
SPAN = 5


NEGATIVE = -1e30
EPSILON = 1e-06


def passed_along(block, axis, distance):
    devices = range(lax.axis_size(axis))
    route = [(i - distance, i) for i in devices if i - distance in devices]
    return lax.ppermute(block, axis, route)


def to_tiles(image):
    lead = image.shape[:-3]
    height, width, channels = image.shape[-3:]
    count = len(lead)
    image = image.reshape(lead + (height // TILE, TILE, width // TILE, TILE, channels))
    order = tuple(range(count)) + (count, count + 2, count + 1, count + 3, count + 4)
    return image.transpose(order).reshape(
        lead + (height // TILE, width // TILE, TILE * TILE, channels)
    )


def from_tiles(tiled):
    tile_rows, tile_cols, area, channels = tiled.shape
    tiled = tiled.reshape(tile_rows, tile_cols, TILE, TILE, channels)
    return tiled.transpose(0, 2, 1, 3, 4).reshape(tile_rows * TILE, tile_cols * TILE, channels)


def windows(extended, tile_rows, tile_cols):
    return jnp.concatenate(
        [
            extended[row_off : row_off + tile_rows, col_off : col_off + tile_cols]
            for row_off in range(SPAN)
            for col_off in range(SPAN)
        ],
        axis=2,
    )


def key_valid(base_row, base_col, tile_rows, tile_cols, all_rows, all_cols):
    reach_tiles = SPAN // 2
    offsets = jnp.arange(SPAN, dtype=jnp.int32) - reach_tiles
    row_ids = base_row + jnp.arange(tile_rows, dtype=jnp.int32)[:, None] + offsets[None, :]
    col_ids = base_col + jnp.arange(tile_cols, dtype=jnp.int32)[:, None] + offsets[None, :]
    row_ok = (row_ids >= 0) & (row_ids < all_rows)
    col_ok = (col_ids >= 0) & (col_ids < all_cols)
    allowed = row_ok[:, None, :, None] & col_ok[None, :, None, :]
    return jnp.repeat(allowed.reshape(tile_rows, tile_cols, SPAN * SPAN), TILE * TILE, axis=2)


def project(normed, scales, factor):
    return (normed.astype(jnp.float32) * (scales * factor)).astype(jnp.bfloat16)


def normalize(image, scales):
    x_float = image.astype(jnp.float32)
    inverse = lax.rsqrt(jnp.mean(x_float * x_float, axis=-1, keepdims=True) + EPSILON)
    return (x_float, inverse, (x_float * inverse * scales).astype(jnp.bfloat16))


def widen(array, dim, reach, move):
    own = array.shape[dim]
    need = -(-reach // own)
    above = []
    below = []
    for step_by in range(need, 0, -1):
        lower_end = max(-step_by * own, -reach)
        upper_end = -(step_by - 1) * own
        piece = array
        above.append(move(piece, step_by))
    for step_by in range(1, need + 1):
        length = min((step_by + 1) * own, own + reach) - step_by * own
        piece = array
        below.append(move(piece, -step_by))
    return jnp.concatenate(above + [array] + below, axis=dim)


def halo_per_device(saved_in, cotangent, section_gains):
    scales = section_gains[0]
    reach_tiles = SPAN // 2
    reach_cells = TILE * reach_tiles
    factor = 1.0 / math.sqrt(HEAD_DIM)
    tile_rows = saved_in.shape[1] // TILE
    tile_cols = saved_in.shape[2] // TILE
    allowed = key_valid(
        lax.axis_index("row") * tile_rows,
        lax.axis_index("col") * tile_cols,
        tile_rows,
        tile_cols,
        tile_rows * lax.axis_size("row"),
        tile_cols * lax.axis_size("col"),
    )
    saved_float, saved_inverse, saved_normed = normalize(saved_in[0], scales[0])
    upstream_image = cotangent[0].astype(jnp.float32)
    grad_image = (upstream_image * scales[4]).astype(jnp.bfloat16)
    paired = jnp.stack([saved_normed, grad_image])

    def move_cols(piece, step_by):
        return passed_along(piece, "col", step_by)

    def move_rows(piece, step_by):
        return passed_along(piece, "row", step_by)

    paired_wide = widen(widen(paired, 2, reach_cells, move_cols), 1, reach_cells, move_rows)
    paired_ext = to_tiles(paired_wide)
    normed_ext = paired_ext[0]
    grad_ext = paired_ext[1]
    normed_tiles = to_tiles(saved_normed)
    grad_tiles = to_tiles(grad_image)
    stat_shape = (HEADS, tile_rows, tile_cols, TILE * TILE)

    def own_head(head, carry):
        dnormed, log_all, delta_all = carry
        start = head * HEAD_DIM

        def part(array):
            return lax.dynamic_slice_in_dim(array, start, HEAD_DIM, array.ndim - 1)

        queries = project(part(normed_tiles), part(scales[1]), factor)
        key_win = windows(project(part(normed_ext), part(scales[2]), 1.0), tile_rows, tile_cols)
        value_win = windows(project(part(normed_ext), part(scales[3]), 1.0), tile_rows, tile_cols)
        scores = jnp.einsum("ijqc,ijkc->ijqk", queries, key_win, preferred_element_type=jnp.float32)
        scores = jnp.where(allowed[:, :, None, :], scores, NEGATIVE)
        row_max = jnp.max(scores, axis=-1, keepdims=True)
        log_total = row_max + jnp.log(jnp.sum(jnp.exp(scores - row_max), axis=-1, keepdims=True))
        weights = jnp.exp(scores - log_total)
        rounded = weights.astype(jnp.bfloat16)
        output = jnp.einsum(
            "ijqk,ijkc->ijqc", rounded, value_win, preferred_element_type=jnp.float32
        )
        grads = part(grad_tiles)
        delta_sum = jnp.sum(grads.astype(jnp.float32) * output, axis=-1)
        prob_grad = jnp.einsum(
            "ijqc,ijkc->ijqk", grads, value_win, preferred_element_type=jnp.float32
        )
        dscore = (weights * (prob_grad - delta_sum[..., None])).astype(jnp.bfloat16)
        dquery = jnp.einsum("ijqk,ijkc->ijqc", dscore, key_win, preferred_element_type=jnp.float32)
        dnormed = lax.dynamic_update_slice_in_dim(
            dnormed, dquery * (part(scales[1]) * factor), start, 3
        )
        log_all = log_all.at[head].set(log_total[..., 0])
        delta_all = delta_all.at[head].set(delta_sum)
        return (dnormed, log_all, delta_all)

    dnormed, log_all, delta_all = lax.fori_loop(
        0,
        HEADS,
        own_head,
        (
            jnp.zeros(normed_tiles.shape, jnp.float32),
            jnp.zeros(stat_shape, jnp.float32),
            jnp.zeros(stat_shape, jnp.float32),
        ),
    )
    stat_tiles = jnp.concatenate([log_all, delta_all], axis=0).transpose(1, 2, 3, 0)

    def stat_cols(piece, step_by):
        return passed_along(piece, "col", step_by)

    def stat_rows(piece, step_by):
        return passed_along(piece, "row", step_by)

    stat_wide = widen(
        widen(from_tiles(stat_tiles), 1, reach_cells, stat_cols), 0, reach_cells, stat_rows
    )
    stat_win = windows(to_tiles(stat_wide), tile_rows, tile_cols)

    def far_head(head, dnormed):
        start = head * HEAD_DIM

        def part(array):
            return lax.dynamic_slice_in_dim(array, start, HEAD_DIM, array.ndim - 1)

        query_win = windows(
            project(part(normed_ext), part(scales[1]), factor), tile_rows, tile_cols
        )
        grad_win = windows(part(grad_ext), tile_rows, tile_cols)
        own_keys = project(part(normed_tiles), part(scales[2]), 1.0)
        own_values = project(part(normed_tiles), part(scales[3]), 1.0)
        far_log = lax.dynamic_index_in_dim(stat_win, head, 3, keepdims=False)
        far_delta = lax.dynamic_index_in_dim(stat_win, HEADS + head, 3, keepdims=False)
        scores = jnp.einsum(
            "ijqc,ijkc->ijqk", query_win, own_keys, preferred_element_type=jnp.float32
        )
        weights = jnp.exp(jnp.where(allowed[..., None], scores - far_log[..., None], NEGATIVE))
        prob_grad = jnp.einsum(
            "ijqc,ijkc->ijqk", grad_win, own_values, preferred_element_type=jnp.float32
        )
        dscore = (weights * (prob_grad - far_delta[..., None])).astype(jnp.bfloat16)
        key_grad = jnp.einsum(
            "ijqk,ijqc->ijkc", dscore, query_win, preferred_element_type=jnp.float32
        )
        dvalue = jnp.einsum(
            "ijqk,ijqc->ijkc",
            weights.astype(jnp.bfloat16),
            grad_win,
            preferred_element_type=jnp.float32,
        )
        terms = key_grad * part(scales[2]) + dvalue * part(scales[3])
        return lax.dynamic_update_slice_in_dim(dnormed, part(dnormed) + terms, start, 3)

    dnormed = lax.fori_loop(0, HEADS, far_head, dnormed)
    scaled = scales[0] * dnormed
    x_tiles = to_tiles(saved_float)
    inv_tiles = to_tiles(saved_inverse)
    upstream = to_tiles(upstream_image)
    image_grad = (
        upstream
        + inv_tiles * scaled
        - x_tiles
        * (inv_tiles * inv_tiles * inv_tiles)
        * jnp.mean(x_tiles * scaled, axis=-1, keepdims=True)
    )
    sent_back = passed_along(from_tiles(image_grad.astype(jnp.bfloat16)), "pipe", -1)
    return sent_back[None]


PIECES = 16


EXTRA = 8
SCALES = [2.0 ** (12 * power) for power in range(-8, 11)]


def crossing(sizes, row_step, col_step):
    rows, cols = sizes
    return [
        (row * cols + col, (row ^ row_step) * cols + (col ^ col_step))
        for row in range(rows)
        for col in range(cols)
    ]


def crossing_back(sizes, row_step):
    pipes, rows, cols = sizes
    return [
        (
            (pipe * rows + row) * cols + col,
            ((pipe - 1) % pipes * rows + (row ^ row_step)) * cols + col,
        )
        for pipe in range(pipes)
        for row in range(rows)
        for col in range(cols)
    ]


def row_to_column(row):
    return jnp.broadcast_to(row, (row.shape[1], row.shape[1])).T


def inverse_columns(pieces):
    pieces = pieces.astype(jnp.float32)
    return row_to_column(pieces[0:1] + pieces[1:2] + pieces[2:3])


def scale_number(size):
    return sum((size >= scale).astype(jnp.float32) for scale in SCALES[1:])


def scale_value(number):
    value = jnp.full(number.shape, SCALES[0], jnp.float32)
    for index, scale in enumerate(SCALES[1:]):
        value = jnp.where(number > index + 0.5, scale, value)
    return value


def inverse_row(x_ref):
    tokens, channels = x_ref.shape
    squares = None
    for lane in range(0, channels, HEAD_DIM):
        part = x_ref[:, lane : lane + HEAD_DIM].astype(jnp.float32)
        part = part * part
        squares = part if squares is None else squares + part
    total = jnp.sum(squares.T, axis=0, keepdims=True)
    return lax.rsqrt(total / channels + EPSILON)


def pack_kernel(rows, heads, x_hbm, c_hbm, *refs):
    outs = refs[: heads * 2]
    x_ref, c_ref, x_sem, c_sem = refs[heads * 2 :]
    tokens, channels = x_ref.shape
    row = lax.axis_index("row")
    col = lax.axis_index("col")
    parts = x_sem.shape[0]
    high_rows = tokens // parts

    def fetch(source, target, sems, part):
        here = pl.ds(part * high_rows, high_rows)
        return pltpu.make_async_copy(source.at[here, :], target.at[here, :], sems.at[part])

    fetches = [fetch(x_hbm, x_ref, x_sem, part) for part in range(parts)]
    fetches += [fetch(c_hbm, c_ref, c_sem, part) for part in range(parts)]
    for copy in fetches:
        copy.start()
    for copy in fetches[:parts]:
        copy.wait()
    inverse = inverse_row(x_ref)
    high = inverse.astype(jnp.bfloat16).astype(jnp.float32)
    mid = (inverse - high).astype(jnp.bfloat16).astype(jnp.float32)
    low = inverse - high - mid
    place = lax.broadcasted_iota(jnp.int32, (PIECES, tokens), 0)
    pieces = jnp.where(place == 0, high, jnp.where(place == 1, mid, jnp.where(place == 2, low, 0.0)))
    pieces = pieces.astype(jnp.bfloat16)
    for source, low in ((x_ref, 0), (c_ref, tokens)):
        if low > 0:
            for copy in fetches[parts:]:
                copy.wait()
        for head in range(heads):
            for step in range(rows):
                for slot in range(2):
                    first = ((row ^ step) * 2 + (col ^ slot)) * heads + head
                    lanes = pl.ds(pl.multiple_of(first * HEAD_DIM, HEAD_DIM), HEAD_DIM)
                    out = outs[head * 2 + slot]
                    out[step, low : low + tokens, :] = source[:, lanes]
                    if head == 0 and low == 0:
                        out[step, 2 * tokens :, :] = pieces


def attend_kernel(rows, heads, head, g_ref, *refs):
    held = rows + 1
    arrays, refs = refs[:held], list(refs[held:])
    columns_ref = refs.pop(0)
    before_ref = refs.pop(0) if head > 0 else None
    after_ref = refs.pop(0) if head < heads - 1 else None
    keep_ref, give_ref = refs[:2]
    q_s, k_s, kt_s, v_s, d_s, p_s, ds_s, s_s, dp_s, dk_s, dv_s, dq_s = refs[-12:]
    tokens = columns_ref.shape[0] // (2 * rows)
    row = lax.axis_index("row")
    col = lax.axis_index("col")
    lanes = pl.ds(pl.multiple_of(((row * 2 + col) * heads + head) * HEAD_DIM, HEAD_DIM), HEAD_DIM)
    gn, gq, gk, gv, go = (g_ref[i : i + 1, lanes] for i in range(5))
    gq = gq * (1.0 / math.sqrt(HEAD_DIM))
    square = 2 * tokens
    pattern = (tokens // (2 * TILE), 2, TILE, tokens)
    query_right = (lax.broadcasted_iota(jnp.int32, pattern[1:], 2) // TILE) % 2
    key_right = lax.broadcasted_iota(jnp.int32, pattern[1:], 0)
    no_cap = float(jnp.finfo(jnp.float32).max)
    left_keys = jnp.where((key_right == 0) & (query_right == 1), NEGATIVE, no_cap)
    right_keys = jnp.where((key_right == 1) & (query_right == 0), NEGATIVE, no_cap)

    def capped(s, cap):
        return jnp.minimum(s.reshape(pattern), cap[None]).reshape(tokens, tokens)

    def block(step, slot, fresh=False):
        number, index = (slot, 0) if step == 0 else (step + 1, slot)
        ref = arrays[number]
        place = pl.multiple_of(((row ^ step) * 2 + (col ^ slot)) * tokens, tokens)
        x = ref[index, 0:tokens, :].astype(jnp.float32)
        c = ref[index, tokens : 2 * tokens, :].astype(jnp.float32)
        here = pl.ds(place, tokens)
        return here, x, c, ref[index, 2 * tokens :, :] if fresh else columns_ref[here, :]

    blocks = [(step, slot) for step in range(rows) for slot in range(2)]
    for step, slot in blocks:
        here, x, c, inverse = block(step, slot, head == 0)
        if head == 0:
            inverse = inverse_columns(inverse)
            columns_ref[here, :] = inverse
        normed = (x * inverse * gn).astype(jnp.bfloat16).astype(jnp.float32)
        q_s[here, :] = (normed * gq).astype(jnp.bfloat16)
        key = (normed * gk).astype(jnp.bfloat16)
        k_s[here, :] = key
        kt_s[:, here] = key.astype(jnp.float32).T.astype(jnp.bfloat16)
        v_s[here, :] = (normed * gv).astype(jnp.bfloat16)
        d_s[here, :] = (c * go).astype(jnp.bfloat16)

    contract_last = (((1,), (1,)), ((), ()))
    reach = SPAN // 2
    spans = []
    for at in range(rows):
        near = [r for r in range(rows) if abs(r - at) <= reach]
        spans.append((near[0] * square, (near[-1] + 1) * square))

    def own(at):
        return slice(at * square, (at + 1) * square)

    def cells(at):
        return [slice(start, start + square) for start in range(*spans[at], square)]

    def fold(combine, parts):
        total = parts[0]
        for part in parts[1:]:
            total = combine(total, part)
        return total

    def products(at, tops):
        buffer = at % 2
        q, d = q_s[own(at), :], d_s[own(at), :]
        left, right = [], []
        for cell in cells(at):
            s = lax.dot_general(k_s[cell, :], q, contract_last, preferred_element_type=jnp.float32)
            upper = slice(cell.start, cell.start + tokens)
            lower = slice(cell.start + tokens, cell.stop)
            upper_left, upper_right = s[0:tokens, 0:tokens], capped(s[0:tokens, tokens:], left_keys)
            lower_left, lower_right = capped(s[tokens:, 0:tokens], right_keys), s[tokens:, tokens:]
            s_s[buffer, upper, 0:tokens] = upper_left
            s_s[buffer, upper, tokens:] = upper_right
            s_s[buffer, lower, 0:tokens] = lower_left
            s_s[buffer, lower, tokens:] = lower_right
            left.append(jnp.max(jnp.maximum(upper_left, lower_left), axis=0, keepdims=True))
            right.append(jnp.max(jnp.maximum(upper_right, lower_right), axis=0, keepdims=True))
            yield
            dp_s[buffer, cell, :] = lax.dot_general(
                v_s[cell, :], d, contract_last, preferred_element_type=jnp.float32
            )
            yield
        tops[at] = jnp.concatenate([fold(jnp.maximum, left), fold(jnp.maximum, right)], axis=1)

    def softmax(at, tops):
        buffer = at % 2
        top = tops[at]
        sums = []
        for cell in cells(at):
            e = jnp.exp(s_s[buffer, cell, :] - top)
            s_s[buffer, cell, :] = e
            sums.append(jnp.sum(e, axis=0, keepdims=True))
            yield
        scale = 1.0 / fold(jnp.add, sums)
        sums = []
        for cell in cells(at):
            p = s_s[buffer, cell, :] * scale
            pb = p.astype(jnp.bfloat16)
            p_s[cell, own(at)] = pb
            sums.append(jnp.sum(pb.astype(jnp.float32) * dp_s[buffer, cell, :], axis=0, keepdims=True))
            yield
        delta = fold(jnp.add, sums)
        for cell in cells(at):
            p = s_s[buffer, cell, :] * scale
            ds_s[cell, own(at)] = (p * (dp_s[buffer, cell, :] - delta)).astype(jnp.bfloat16)
            yield

    def query_side(at):
        span = slice(*spans[at])
        dq = jnp.dot(kt_s[:, span], ds_s[span, own(at)], preferred_element_type=jnp.float32)
        yield
        dq_s[own(at), :] = dq.T
        yield

    def key_side(first, last):
        for at in range(rows):
            low, high = max(spans[at][0], first * square), min(spans[at][1], last * square)
            if low >= high:
                continue
            span = slice(low, high)
            dk = jnp.dot(ds_s[own(at), span], q_s[span, :], preferred_element_type=jnp.float32)
            fresh = low == spans[at][0]
            dk_s[own(at), :] = dk if fresh else dk_s[own(at), :] + dk
            yield
            dv = jnp.dot(p_s[own(at), span], d_s[span, :], preferred_element_type=jnp.float32)
            dv_s[own(at), :] = dv if fresh else dv_s[own(at), :] + dv
            yield

    def together(*works):
        works = list(works)
        while works:
            works = [work for work in works if next(work, works) is not works]


    def all_queries():
        dq = jnp.dot(kt_s[...], ds_s[...], preferred_element_type=jnp.float32)
        yield
        dq_s[...] = dq.T
        yield

    for at in range(rows):
        for other in range(rows):
            if abs(at - other) > reach:
                ds_s[own(at), own(other)] = jnp.zeros((square, square), jnp.bfloat16)
    tops = {}
    together(products(0, tops))
    for at in range(rows):
        works = [softmax(at, tops)]
        if at + 1 < rows:
            works.append(products(at + 1, tops))
        if at > 0:
            works += [key_side(at - 1, at)]
        together(*works)
    together(key_side(rows - 1, rows), all_queries())
    tops, shares = [], []
    for step, slot in blocks:
        here, x, c, inverse = block(step, slot)
        scaled = gn * (dq_s[here, :] * gq + dk_s[here, :] * gk + dv_s[here, :] * gv)
        value = c + inverse * scaled
        (keep_ref, give_ref)[slot][step, 0:tokens, :] = value
        tops.append(jnp.max(jnp.abs(value), axis=0, keepdims=True))
        shares.append(jnp.sum((x * scaled).T, axis=0, keepdims=True))
    top = jnp.max(jnp.concatenate(tops, axis=0), axis=1, keepdims=True)
    number = scale_number(jnp.broadcast_to(top, (len(blocks), tokens)))
    shrink = 1.0 / scale_value(number)
    share = jnp.concatenate(shares, axis=0)
    numbers = [before_ref[earlier + 1] for earlier in range(head)] + [number]
    if head > 0:
        share = share + before_ref[0]
    if head < heads - 1:
        after_ref[0] = share
        for index, value in enumerate(numbers):
            after_ref[index + 1] = value
    else:
        share_number = scale_number(jnp.abs(share))
        share = share / scale_value(share_number)
        high = share.astype(jnp.bfloat16).astype(jnp.float32)
        mid = (share - high).astype(jnp.bfloat16).astype(jnp.float32)
        low = share - high - mid
        place = lax.broadcasted_iota(jnp.int32, (EXTRA, tokens), 0)
    for index, (step, slot) in enumerate(blocks):
        out = (keep_ref, give_ref)[slot]
        at = slice(index, index + 1)
        out[step, 0:tokens, :] = out[step, 0:tokens, :] * shrink[at]
        if head == heads - 1:
            extra = jnp.zeros((EXTRA, tokens), jnp.float32)
            for line, value in enumerate([share_number, high, mid, low] + numbers):
                extra = jnp.where(place == line, value[at], extra)
            out[step, tokens:, :] = extra


def attention_kernel(*operands):
    @pl.when(lax.axis_index("pipe") > 0)
    def _():
        attend_kernel(*operands)


def cube_kernel(x_ref, out_ref):
    inverse = inverse_row(x_ref)
    out_ref[...] = row_to_column(inverse * inverse * inverse)


def collect_kernel(rows, heads, x_ref, cube_ref, *refs):
    units = refs[:rows]
    out_hbm, out_ref, sems = refs[rows:]
    tokens, channels = x_ref.shape
    row = lax.axis_index("row")
    col = lax.axis_index("col")
    last = lax.axis_index("pipe") == lax.axis_size("pipe") - 1
    side = heads * tokens + EXTRA
    total, scales = None, {}
    for step in range(rows):
        for half in range(2):
            extra = units[step][half * side + heads * tokens : (half + 1) * side, :]
            value = scale_value(extra)
            for head in range(heads):
                scales[step, half * heads + head] = value[4 + head : 5 + head]
            share = (extra[1:2] + extra[2:3] + extra[3:4]) * value[0:1]
            total = share if total is None else total + share
    weight = cube_ref[...] * row_to_column(total / channels)
    wide = 2 * heads * HEAD_DIM
    copies = []
    for step in range(rows):
        for slot in range(2 * heads):
            first = ((row ^ step) * 2 + (col ^ (slot // heads))) * heads + slot % heads
            lanes = pl.ds(pl.multiple_of(first * HEAD_DIM, HEAD_DIM), HEAD_DIM)
            top = slot // heads * side + slot % heads * tokens
            part = units[step][top : top + tokens, :] * scales[step, slot]
            grad = part - x_ref[:, lanes].astype(jnp.float32) * weight
            out_ref[:, lanes] = jnp.where(last, 0.0, grad).astype(jnp.bfloat16)
        lanes = pl.ds(pl.multiple_of((row ^ step) * wide, wide), wide)
        copies.append(pltpu.make_async_copy(out_ref.at[:, lanes], out_hbm.at[:, lanes], sems.at[step]))
        copies[-1].start()
    for copy in copies:
        copy.wait()


def local_call(kernel, out_shape, scratch_shapes=(), **placed):
    return pl.pallas_call(
        kernel,
        out_shape=out_shape,
        **placed,
        scratch_shapes=scratch_shapes,
        compiler_params=pltpu.CompilerParams(vmem_limit_bytes=24 * 1024 * 1024),
    )


def near(arrays):
    return [pltpu.with_memory_space_constraint(array, pltpu.VMEM) for array in arrays]


def split_heads_per_device(saved_in, cotangent, section_gains):
    pipes, rows, cols = (lax.axis_size(name) for name in ("pipe", "row", "col"))
    channels = saved_in.shape[-1]
    tokens = saved_in.shape[1] * saved_in.shape[2]
    heads = channels // HEAD_DIM // (rows * cols)
    plane = ("row", "col")
    sizes = (rows, cols)
    bf, f32 = jnp.bfloat16, jnp.float32
    x = saved_in.reshape(tokens, channels)
    c = cotangent.reshape(tokens, channels)
    gains = section_gains[0]
    packets = []
    for head in range(heads):
        packets += [pltpu.VMEM((rows, 2 * tokens + (PIECES if head == 0 else 0), HEAD_DIM), bf)] * 2
    far = pl.BlockSpec(memory_space=pltpu.HBM)
    staged = [pltpu.VMEM((tokens, channels), bf)] * 2 + [pltpu.SemaphoreType.DMA((1,))] * 2
    packed = local_call(functools.partial(pack_kernel, rows, heads), packets, staged, in_specs=[far, far])(
        pltpu.with_memory_space_constraint(x, pltpu.HBM), pltpu.with_memory_space_constraint(c, pltpu.HBM)
    )

    def swap(array):
        return lax.ppermute(array, plane, crossing(sizes, 0, 1))

    passed = [[swap(packed[1][1:2]), swap(packed[1][2:]), swap(packed[1][0:1])]]
    passed += [swap(packed[2 * head + 1]) for head in range(1, heads)]
    arrays = []
    for head in range(heads):
        own, other = packed[2 * head], passed[head]
        if head == 0:
            held = [own, other[2]]
            packets = [jnp.concatenate([own[1:2], other[0]])]
            packets += [jnp.stack([own[step], other[1][step - 2]]) for step in range(2, rows)]
        else:
            held = [own, other]
            packets = [jnp.stack([own[step], other[step]]) for step in range(1, rows)]
        if head > 0:
            packets, arrays[head - 1][2] = lax.optimization_barrier((packets, arrays[head - 1][2]))
        for step in range(1, rows):
            held.append(lax.ppermute(packets[step - 1], plane, crossing(sizes, step, 0)))
        arrays.append(held)
    count = rows * cols * tokens
    square = 2 * tokens
    scratch = [
        pltpu.VMEM((count, HEAD_DIM), bf),
        pltpu.VMEM((count, HEAD_DIM), bf),
        pltpu.VMEM((HEAD_DIM, count), bf),
        pltpu.VMEM((count, HEAD_DIM), bf),
        pltpu.VMEM((count, HEAD_DIM), bf),
        pltpu.VMEM((count, count), bf),
        pltpu.VMEM((count, count), bf),
        pltpu.VMEM((2, count, square), f32),
        pltpu.VMEM((2, count, square), f32),
        pltpu.VMEM((count, HEAD_DIM), f32),
        pltpu.VMEM((count, HEAD_DIM), f32),
        pltpu.VMEM((count, HEAD_DIM), f32),
    ]
    behind = [(pipe, (pipe - 1) % pipes) for pipe in range(pipes)]
    arrays[0][2], free_x = lax.optimization_barrier((arrays[0][2], x))
    x_ahead = lax.ppermute(free_x, "pipe", behind)
    carried = pltpu.VMEM((heads, 2 * rows, tokens), f32)
    columns = [pltpu.VMEM((count, HEAD_DIM), f32)]
    handed = []
    keep, got = [], []
    for head in range(heads):
        results = columns if head == 0 else []
        results = results + ([carried] if head < heads - 1 else [])
        height = tokens + (EXTRA if head == heads - 1 else 0)
        results = results + [pltpu.VMEM((rows, height, HEAD_DIM), f32)] * 2
        operands = arrays[head] + ([] if head == 0 else columns + handed)
        call = local_call(functools.partial(attention_kernel, rows, heads, head), results, scratch)
        *others, kept, given = call(gains, *near(operands))
        columns = others[:1] if head == 0 else columns
        handed = others[-1:]
        if head == heads - 1:
            given, x_ahead = lax.optimization_barrier((given, x_ahead))
        keep.append(kept.astype(jnp.float16))
        got.append(lax.ppermute(given.astype(jnp.float16), plane, crossing(sizes, 0, 1)))
    units = []
    for step in range(rows):
        sent = jnp.concatenate([unit[step] for unit in keep + got])
        sent = lax.ppermute(sent, ("pipe",) + plane, crossing_back((pipes, rows, cols), step))
        units.append(sent.astype(f32))
    cube = local_call(cube_kernel, pltpu.VMEM((tokens, HEAD_DIM), f32))(*near([x_ahead]))
    out = local_call(
        functools.partial(collect_kernel, rows, heads),
        jax.ShapeDtypeStruct((tokens, channels), bf),
        [pltpu.VMEM((tokens, channels), bf), pltpu.SemaphoreType.DMA((rows,))],
        out_specs=far,
    )(*near([x_ahead, cube] + units))
    return out.reshape(saved_in.shape)


def per_device(saved_in, cotangent, section_gains):
    rows, cols = lax.axis_size("row"), lax.axis_size("col")
    block_fits = saved_in.shape[1] == TILE and saved_in.shape[2] == 2 * TILE
    devices_fit = cols == 2 and rows & (rows - 1) == 0 and HEADS % (rows * cols) == 0
    plan = split_heads_per_device if block_fits and devices_fit else halo_per_device
    return plan(saved_in, cotangent, section_gains)


def solution(mesh):
    return jax.shard_map(
        per_device,
        mesh=mesh,
        in_specs=(
            P("pipe", "row", "col", None),
            P("pipe", "row", "col", None),
            P("pipe", None, None),
        ),
        out_specs=P("pipe", "row", "col", None),
        check_vma=False,
    )
```

```python
import functools
import math

import jax
import jax.numpy as jnp
from jax import lax
from jax.experimental import pallas as pl
from jax.experimental.pallas import tpu as pltpu
from jax.sharding import PartitionSpec as P

HEADS = 16
HEAD_DIM = 128
TILE = 8
SPAN = 5


NEGATIVE = -1e30
EPSILON = 1e-06


def passed_along(block, axis, distance):
    devices = range(lax.axis_size(axis))
    route = [(i - distance, i) for i in devices if i - distance in devices]
    return lax.ppermute(block, axis, route)


def to_tiles(image):
    lead = image.shape[:-3]
    height, width, channels = image.shape[-3:]
    count = len(lead)
    image = image.reshape(lead + (height // TILE, TILE, width // TILE, TILE, channels))
    order = tuple(range(count)) + (count, count + 2, count + 1, count + 3, count + 4)
    return image.transpose(order).reshape(
        lead + (height // TILE, width // TILE, TILE * TILE, channels)
    )


def from_tiles(tiled):
    tile_rows, tile_cols, area, channels = tiled.shape
    tiled = tiled.reshape(tile_rows, tile_cols, TILE, TILE, channels)
    return tiled.transpose(0, 2, 1, 3, 4).reshape(tile_rows * TILE, tile_cols * TILE, channels)


def windows(extended, tile_rows, tile_cols):
    return jnp.concatenate(
        [
            extended[row_off : row_off + tile_rows, col_off : col_off + tile_cols]
            for row_off in range(SPAN)
            for col_off in range(SPAN)
        ],
        axis=2,
    )


def key_valid(base_row, base_col, tile_rows, tile_cols, all_rows, all_cols):
    reach_tiles = SPAN // 2
    offsets = jnp.arange(SPAN, dtype=jnp.int32) - reach_tiles
    row_ids = base_row + jnp.arange(tile_rows, dtype=jnp.int32)[:, None] + offsets[None, :]
    col_ids = base_col + jnp.arange(tile_cols, dtype=jnp.int32)[:, None] + offsets[None, :]
    row_ok = (row_ids >= 0) & (row_ids < all_rows)
    col_ok = (col_ids >= 0) & (col_ids < all_cols)
    allowed = row_ok[:, None, :, None] & col_ok[None, :, None, :]
    return jnp.repeat(allowed.reshape(tile_rows, tile_cols, SPAN * SPAN), TILE * TILE, axis=2)


def project(normed, scales, factor):
    return (normed.astype(jnp.float32) * (scales * factor)).astype(jnp.bfloat16)


def normalize(image, scales):
    x_float = image.astype(jnp.float32)
    inverse = lax.rsqrt(jnp.mean(x_float * x_float, axis=-1, keepdims=True) + EPSILON)
    return (x_float, inverse, (x_float * inverse * scales).astype(jnp.bfloat16))


def widen(array, dim, reach, move):
    own = array.shape[dim]
    need = -(-reach // own)
    above = []
    below = []
    for step_by in range(need, 0, -1):
        lower_end = max(-step_by * own, -reach)
        upper_end = -(step_by - 1) * own
        piece = array
        above.append(move(piece, step_by))
    for step_by in range(1, need + 1):
        length = min((step_by + 1) * own, own + reach) - step_by * own
        piece = array
        below.append(move(piece, -step_by))
    return jnp.concatenate(above + [array] + below, axis=dim)


def halo_per_device(saved_in, cotangent, section_gains):
    scales = section_gains[0]
    reach_tiles = SPAN // 2
    reach_cells = TILE * reach_tiles
    factor = 1.0 / math.sqrt(HEAD_DIM)
    tile_rows = saved_in.shape[1] // TILE
    tile_cols = saved_in.shape[2] // TILE
    allowed = key_valid(
        lax.axis_index("row") * tile_rows,
        lax.axis_index("col") * tile_cols,
        tile_rows,
        tile_cols,
        tile_rows * lax.axis_size("row"),
        tile_cols * lax.axis_size("col"),
    )
    saved_float, saved_inverse, saved_normed = normalize(saved_in[0], scales[0])
    upstream_image = cotangent[0].astype(jnp.float32)
    grad_image = (upstream_image * scales[4]).astype(jnp.bfloat16)
    paired = jnp.stack([saved_normed, grad_image])

    def move_cols(piece, step_by):
        return passed_along(piece, "col", step_by)

    def move_rows(piece, step_by):
        return passed_along(piece, "row", step_by)

    paired_wide = widen(widen(paired, 2, reach_cells, move_cols), 1, reach_cells, move_rows)
    paired_ext = to_tiles(paired_wide)
    normed_ext = paired_ext[0]
    grad_ext = paired_ext[1]
    normed_tiles = to_tiles(saved_normed)
    grad_tiles = to_tiles(grad_image)
    stat_shape = (HEADS, tile_rows, tile_cols, TILE * TILE)

    def own_head(head, carry):
        dnormed, log_all, delta_all = carry
        start = head * HEAD_DIM

        def part(array):
            return lax.dynamic_slice_in_dim(array, start, HEAD_DIM, array.ndim - 1)

        queries = project(part(normed_tiles), part(scales[1]), factor)
        key_win = windows(project(part(normed_ext), part(scales[2]), 1.0), tile_rows, tile_cols)
        value_win = windows(project(part(normed_ext), part(scales[3]), 1.0), tile_rows, tile_cols)
        scores = jnp.einsum("ijqc,ijkc->ijqk", queries, key_win, preferred_element_type=jnp.float32)
        scores = jnp.where(allowed[:, :, None, :], scores, NEGATIVE)
        row_max = jnp.max(scores, axis=-1, keepdims=True)
        log_total = row_max + jnp.log(jnp.sum(jnp.exp(scores - row_max), axis=-1, keepdims=True))
        weights = jnp.exp(scores - log_total)
        rounded = weights.astype(jnp.bfloat16)
        output = jnp.einsum(
            "ijqk,ijkc->ijqc", rounded, value_win, preferred_element_type=jnp.float32
        )
        grads = part(grad_tiles)
        delta_sum = jnp.sum(grads.astype(jnp.float32) * output, axis=-1)
        prob_grad = jnp.einsum(
            "ijqc,ijkc->ijqk", grads, value_win, preferred_element_type=jnp.float32
        )
        dscore = (weights * (prob_grad - delta_sum[..., None])).astype(jnp.bfloat16)
        dquery = jnp.einsum("ijqk,ijkc->ijqc", dscore, key_win, preferred_element_type=jnp.float32)
        dnormed = lax.dynamic_update_slice_in_dim(
            dnormed, dquery * (part(scales[1]) * factor), start, 3
        )
        log_all = log_all.at[head].set(log_total[..., 0])
        delta_all = delta_all.at[head].set(delta_sum)
        return (dnormed, log_all, delta_all)

    dnormed, log_all, delta_all = lax.fori_loop(
        0,
        HEADS,
        own_head,
        (
            jnp.zeros(normed_tiles.shape, jnp.float32),
            jnp.zeros(stat_shape, jnp.float32),
            jnp.zeros(stat_shape, jnp.float32),
        ),
    )
    stat_tiles = jnp.concatenate([log_all, delta_all], axis=0).transpose(1, 2, 3, 0)

    def stat_cols(piece, step_by):
        return passed_along(piece, "col", step_by)

    def stat_rows(piece, step_by):
        return passed_along(piece, "row", step_by)

    stat_wide = widen(
        widen(from_tiles(stat_tiles), 1, reach_cells, stat_cols), 0, reach_cells, stat_rows
    )
    stat_win = windows(to_tiles(stat_wide), tile_rows, tile_cols)

    def far_head(head, dnormed):
        start = head * HEAD_DIM

        def part(array):
            return lax.dynamic_slice_in_dim(array, start, HEAD_DIM, array.ndim - 1)

        query_win = windows(
            project(part(normed_ext), part(scales[1]), factor), tile_rows, tile_cols
        )
        grad_win = windows(part(grad_ext), tile_rows, tile_cols)
        own_keys = project(part(normed_tiles), part(scales[2]), 1.0)
        own_values = project(part(normed_tiles), part(scales[3]), 1.0)
        far_log = lax.dynamic_index_in_dim(stat_win, head, 3, keepdims=False)
        far_delta = lax.dynamic_index_in_dim(stat_win, HEADS + head, 3, keepdims=False)
        scores = jnp.einsum(
            "ijqc,ijkc->ijqk", query_win, own_keys, preferred_element_type=jnp.float32
        )
        weights = jnp.exp(jnp.where(allowed[..., None], scores - far_log[..., None], NEGATIVE))
        prob_grad = jnp.einsum(
            "ijqc,ijkc->ijqk", grad_win, own_values, preferred_element_type=jnp.float32
        )
        dscore = (weights * (prob_grad - far_delta[..., None])).astype(jnp.bfloat16)
        key_grad = jnp.einsum(
            "ijqk,ijqc->ijkc", dscore, query_win, preferred_element_type=jnp.float32
        )
        dvalue = jnp.einsum(
            "ijqk,ijqc->ijkc",
            weights.astype(jnp.bfloat16),
            grad_win,
            preferred_element_type=jnp.float32,
        )
        terms = key_grad * part(scales[2]) + dvalue * part(scales[3])
        return lax.dynamic_update_slice_in_dim(dnormed, part(dnormed) + terms, start, 3)

    dnormed = lax.fori_loop(0, HEADS, far_head, dnormed)
    scaled = scales[0] * dnormed
    x_tiles = to_tiles(saved_float)
    inv_tiles = to_tiles(saved_inverse)
    upstream = to_tiles(upstream_image)
    image_grad = (
        upstream
        + inv_tiles * scaled
        - x_tiles
        * (inv_tiles * inv_tiles * inv_tiles)
        * jnp.mean(x_tiles * scaled, axis=-1, keepdims=True)
    )
    sent_back = passed_along(from_tiles(image_grad.astype(jnp.bfloat16)), "pipe", -1)
    return sent_back[None]


PIECES = 16


EXTRA = 8
SCALES = [2.0 ** (12 * power) for power in range(-8, 11)]


def crossing(sizes, row_step, col_step):
    rows, cols = sizes
    return [
        (row * cols + col, (row ^ row_step) * cols + (col ^ col_step))
        for row in range(rows)
        for col in range(cols)
    ]


def crossing_back(sizes, row_step):
    pipes, rows, cols = sizes
    return [
        (
            (pipe * rows + row) * cols + col,
            ((pipe - 1) % pipes * rows + (row ^ row_step)) * cols + col,
        )
        for pipe in range(pipes)
        for row in range(rows)
        for col in range(cols)
    ]


def row_to_column(row):
    return jnp.broadcast_to(row, (row.shape[1], row.shape[1])).T


def inverse_columns(pieces):
    pieces = pieces.astype(jnp.float32)
    return row_to_column(pieces[0:1] + pieces[1:2] + pieces[2:3])


def scale_number(size):
    return sum((size >= scale).astype(jnp.float32) for scale in SCALES[1:])


def scale_value(number):
    value = jnp.full(number.shape, SCALES[0], jnp.float32)
    for index, scale in enumerate(SCALES[1:]):
        value = jnp.where(number > index + 0.5, scale, value)
    return value


def inverse_row(x_ref):
    tokens, channels = x_ref.shape
    squares = None
    for lane in range(0, channels, HEAD_DIM):
        part = x_ref[:, lane : lane + HEAD_DIM].astype(jnp.float32)
        part = part * part
        squares = part if squares is None else squares + part
    total = jnp.sum(squares.T, axis=0, keepdims=True)
    return lax.rsqrt(total / channels + EPSILON)


def pack_kernel(rows, heads, x_hbm, c_hbm, *refs):
    outs = refs[: heads * 2]
    x_ref, c_ref, x_sem, c_sem = refs[heads * 2 :]
    tokens, channels = x_ref.shape
    row = lax.axis_index("row")
    col = lax.axis_index("col")
    parts = x_sem.shape[0]
    high_rows = tokens // parts

    def fetch(source, target, sems, part):
        here = pl.ds(part * high_rows, high_rows)
        return pltpu.make_async_copy(source.at[here, :], target.at[here, :], sems.at[part])

    fetches = [fetch(x_hbm, x_ref, x_sem, part) for part in range(parts)]
    fetches += [fetch(c_hbm, c_ref, c_sem, part) for part in range(parts)]
    for copy in fetches:
        copy.start()
    for copy in fetches[:parts]:
        copy.wait()
    inverse = inverse_row(x_ref)
    high = inverse.astype(jnp.bfloat16).astype(jnp.float32)
    mid = (inverse - high).astype(jnp.bfloat16).astype(jnp.float32)
    low = inverse - high - mid
    place = lax.broadcasted_iota(jnp.int32, (PIECES, tokens), 0)
    pieces = jnp.where(place == 0, high, jnp.where(place == 1, mid, jnp.where(place == 2, low, 0.0)))
    pieces = pieces.astype(jnp.bfloat16)
    for source, low in ((x_ref, 0), (c_ref, tokens)):
        if low > 0:
            for copy in fetches[parts:]:
                copy.wait()
        for head in range(heads):
            for step in range(rows):
                for slot in range(2):
                    first = ((row ^ step) * 2 + (col ^ slot)) * heads + head
                    lanes = pl.ds(pl.multiple_of(first * HEAD_DIM, HEAD_DIM), HEAD_DIM)
                    out = outs[head * 2 + slot]
                    out[step, low : low + tokens, :] = source[:, lanes]
                    if head == 0 and low == 0:
                        out[step, 2 * tokens :, :] = pieces


def attend_kernel(rows, heads, head, g_ref, *refs):
    held = rows + 1
    arrays, refs = refs[:held], list(refs[held:])
    columns_ref = refs.pop(0)
    before_ref = refs.pop(0) if head > 0 else None
    after_ref = refs.pop(0) if head < heads - 1 else None
    keep_ref, give_ref = refs[:2]
    q_s, k_s, kt_s, v_s, d_s, p_s, ds_s, s_s, dp_s, dk_s, dv_s, dq_s = refs[-12:]
    tokens = columns_ref.shape[0] // (2 * rows)
    row = lax.axis_index("row")
    col = lax.axis_index("col")
    lanes = pl.ds(pl.multiple_of(((row * 2 + col) * heads + head) * HEAD_DIM, HEAD_DIM), HEAD_DIM)
    gn, gq, gk, gv, go = (g_ref[i : i + 1, lanes] for i in range(5))
    gq = gq * (1.0 / math.sqrt(HEAD_DIM))
    square = 2 * tokens
    pattern = (tokens // (2 * TILE), 2, TILE, tokens)
    query_right = (lax.broadcasted_iota(jnp.int32, pattern[1:], 2) // TILE) % 2
    key_right = lax.broadcasted_iota(jnp.int32, pattern[1:], 0)
    no_cap = float(jnp.finfo(jnp.float32).max)
    left_keys = jnp.where((key_right == 0) & (query_right == 1), NEGATIVE, no_cap)
    right_keys = jnp.where((key_right == 1) & (query_right == 0), NEGATIVE, no_cap)

    def capped(s, cap):
        return jnp.minimum(s.reshape(pattern), cap[None]).reshape(tokens, tokens)

    def block(step, slot, fresh=False):
        number, index = (slot, 0) if step == 0 else (step + 1, slot)
        ref = arrays[number]
        place = pl.multiple_of(((row ^ step) * 2 + (col ^ slot)) * tokens, tokens)
        x = ref[index, 0:tokens, :].astype(jnp.float32)
        c = ref[index, tokens : 2 * tokens, :].astype(jnp.float32)
        here = pl.ds(place, tokens)
        return here, x, c, ref[index, 2 * tokens :, :] if fresh else columns_ref[here, :]

    blocks = [(step, slot) for step in range(rows) for slot in range(2)]
    for step, slot in blocks:
        here, x, c, inverse = block(step, slot, head == 0)
        if head == 0:
            inverse = inverse_columns(inverse)
            columns_ref[here, :] = inverse
        normed = (x * inverse * gn).astype(jnp.bfloat16).astype(jnp.float32)
        q_s[here, :] = (normed * gq).astype(jnp.bfloat16)
        key = (normed * gk).astype(jnp.bfloat16)
        k_s[here, :] = key
        kt_s[:, here] = key.astype(jnp.float32).T.astype(jnp.bfloat16)
        v_s[here, :] = (normed * gv).astype(jnp.bfloat16)
        d_s[here, :] = (c * go).astype(jnp.bfloat16)

    contract_last = (((1,), (1,)), ((), ()))
    reach = SPAN // 2
    spans = []
    for at in range(rows):
        near = [r for r in range(rows) if abs(r - at) <= reach]
        spans.append((near[0] * square, (near[-1] + 1) * square))

    def own(at):
        return slice(at * square, (at + 1) * square)

    def cells(at):
        return [slice(start, start + square) for start in range(*spans[at], square)]

    def fold(combine, parts):
        total = parts[0]
        for part in parts[1:]:
            total = combine(total, part)
        return total

    def products(at, tops):
        buffer = at % 2
        q, d = q_s[own(at), :], d_s[own(at), :]
        left, right = [], []
        for cell in cells(at):
            s = lax.dot_general(k_s[cell, :], q, contract_last, preferred_element_type=jnp.float32)
            upper = slice(cell.start, cell.start + tokens)
            lower = slice(cell.start + tokens, cell.stop)
            upper_left, upper_right = s[0:tokens, 0:tokens], capped(s[0:tokens, tokens:], left_keys)
            lower_left, lower_right = capped(s[tokens:, 0:tokens], right_keys), s[tokens:, tokens:]
            s_s[buffer, upper, 0:tokens] = upper_left
            s_s[buffer, upper, tokens:] = upper_right
            s_s[buffer, lower, 0:tokens] = lower_left
            s_s[buffer, lower, tokens:] = lower_right
            left.append(jnp.max(jnp.maximum(upper_left, lower_left), axis=0, keepdims=True))
            right.append(jnp.max(jnp.maximum(upper_right, lower_right), axis=0, keepdims=True))
            yield
            dp_s[buffer, cell, :] = lax.dot_general(
                v_s[cell, :], d, contract_last, preferred_element_type=jnp.float32
            )
            yield
        tops[at] = jnp.concatenate([fold(jnp.maximum, left), fold(jnp.maximum, right)], axis=1)

    def softmax(at, tops):
        buffer = at % 2
        top = tops[at]
        sums = []
        for cell in cells(at):
            e = jnp.exp(s_s[buffer, cell, :] - top)
            s_s[buffer, cell, :] = e
            sums.append(jnp.sum(e, axis=0, keepdims=True))
            yield
        scale = 1.0 / fold(jnp.add, sums)
        sums = []
        for cell in cells(at):
            p = s_s[buffer, cell, :] * scale
            pb = p.astype(jnp.bfloat16)
            p_s[cell, own(at)] = pb
            sums.append(jnp.sum(pb.astype(jnp.float32) * dp_s[buffer, cell, :], axis=0, keepdims=True))
            yield
        delta = fold(jnp.add, sums)
        for cell in cells(at):
            p = s_s[buffer, cell, :] * scale
            ds_s[cell, own(at)] = (p * (dp_s[buffer, cell, :] - delta)).astype(jnp.bfloat16)
            yield

    def query_side(at):
        span = slice(*spans[at])
        dq = jnp.dot(kt_s[:, span], ds_s[span, own(at)], preferred_element_type=jnp.float32)
        yield
        dq_s[own(at), :] = dq.T
        yield

    def key_side(first, last):
        for at in range(rows):
            low, high = max(spans[at][0], first * square), min(spans[at][1], last * square)
            if low >= high:
                continue
            span = slice(low, high)
            dk = jnp.dot(ds_s[own(at), span], q_s[span, :], preferred_element_type=jnp.float32)
            fresh = low == spans[at][0]
            dk_s[own(at), :] = dk if fresh else dk_s[own(at), :] + dk
            yield
            dv = jnp.dot(p_s[own(at), span], d_s[span, :], preferred_element_type=jnp.float32)
            dv_s[own(at), :] = dv if fresh else dv_s[own(at), :] + dv
            yield

    def together(*works):
        works = list(works)
        while works:
            works = [work for work in works if next(work, works) is not works]


    def all_queries():
        dq = jnp.dot(kt_s[...], ds_s[...], preferred_element_type=jnp.float32)
        yield
        dq_s[...] = dq.T
        yield

    for at in range(rows):
        for other in range(rows):
            if abs(at - other) > reach:
                ds_s[own(at), own(other)] = jnp.zeros((square, square), jnp.bfloat16)
    tops = {}
    together(products(0, tops))
    for at in range(rows):
        works = [softmax(at, tops)]
        if at + 1 < rows:
            works.append(products(at + 1, tops))
        if at > 0:
            works += [key_side(at - 1, at)]
        together(*works)
    together(key_side(rows - 1, rows), all_queries())
    tops, shares = [], []
    for step, slot in blocks:
        here, x, c, inverse = block(step, slot)
        scaled = gn * (dq_s[here, :] * gq + dk_s[here, :] * gk + dv_s[here, :] * gv)
        value = c + inverse * scaled
        (keep_ref, give_ref)[slot][step, 0:tokens, :] = value
        tops.append(jnp.max(jnp.abs(value), axis=0, keepdims=True))
        shares.append(jnp.sum((x * scaled).T, axis=0, keepdims=True))
    top = jnp.max(jnp.concatenate(tops, axis=0), axis=1, keepdims=True)
    number = scale_number(jnp.broadcast_to(top, (len(blocks), tokens)))
    shrink = 1.0 / scale_value(number)
    share = jnp.concatenate(shares, axis=0)
    numbers = [before_ref[earlier + 1] for earlier in range(head)] + [number]
    if head > 0:
        share = share + before_ref[0]
    if head < heads - 1:
        after_ref[0] = share
        for index, value in enumerate(numbers):
            after_ref[index + 1] = value
    else:
        share_number = scale_number(jnp.abs(share))
        share = share / scale_value(share_number)
        high = share.astype(jnp.bfloat16).astype(jnp.float32)
        mid = (share - high).astype(jnp.bfloat16).astype(jnp.float32)
        low = share - high - mid
        place = lax.broadcasted_iota(jnp.int32, (EXTRA, tokens), 0)
    for index, (step, slot) in enumerate(blocks):
        out = (keep_ref, give_ref)[slot]
        at = slice(index, index + 1)
        out[step, 0:tokens, :] = out[step, 0:tokens, :] * shrink[at]
        if head == heads - 1:
            extra = jnp.zeros((EXTRA, tokens), jnp.float32)
            for line, value in enumerate([share_number, high, mid, low] + numbers):
                extra = jnp.where(place == line, value[at], extra)
            out[step, tokens:, :] = extra


def attention_kernel(*operands):
    @pl.when(lax.axis_index("pipe") > 0)
    def _():
        attend_kernel(*operands)


def cube_kernel(x_ref, out_ref):
    inverse = inverse_row(x_ref)
    cube = row_to_column(inverse * inverse * inverse)
    for lane in range(0, x_ref.shape[1], HEAD_DIM):
        lanes = slice(lane, lane + HEAD_DIM)
        out_ref[:, lanes] = x_ref[:, lanes].astype(jnp.float32) * cube


def collect_kernel(rows, heads, x_ref, *refs):
    units = refs[:rows]
    out_hbm, out_ref, sems = refs[rows:]
    tokens, channels = x_ref.shape
    row = lax.axis_index("row")
    col = lax.axis_index("col")
    last = lax.axis_index("pipe") == lax.axis_size("pipe") - 1
    side = heads * tokens + EXTRA
    total, scales = None, {}
    for step in range(rows):
        for half in range(2):
            extra = units[step][half * side + heads * tokens : (half + 1) * side, :]
            value = scale_value(extra)
            for head in range(heads):
                scales[step, half * heads + head] = value[4 + head : 5 + head]
            share = (extra[1:2] + extra[2:3] + extra[3:4]) * value[0:1]
            total = share if total is None else total + share
    mean = row_to_column(total / channels)
    wide = 2 * heads * HEAD_DIM
    copies = []
    for step in range(rows):
        for slot in range(2 * heads):
            first = ((row ^ step) * 2 + (col ^ (slot // heads))) * heads + slot % heads
            lanes = pl.ds(pl.multiple_of(first * HEAD_DIM, HEAD_DIM), HEAD_DIM)
            top = slot // heads * side + slot % heads * tokens
            part = units[step][top : top + tokens, :] * scales[step, slot]
            grad = part - x_ref[:, lanes] * mean
            out_ref[:, lanes] = jnp.where(last, 0.0, grad).astype(jnp.bfloat16)
        lanes = pl.ds(pl.multiple_of((row ^ step) * wide, wide), wide)
        copies.append(pltpu.make_async_copy(out_ref.at[:, lanes], out_hbm.at[:, lanes], sems.at[step]))
        copies[-1].start()
    for copy in copies:
        copy.wait()


def local_call(kernel, out_shape, scratch_shapes=(), **placed):
    return pl.pallas_call(
        kernel,
        out_shape=out_shape,
        **placed,
        scratch_shapes=scratch_shapes,
        compiler_params=pltpu.CompilerParams(vmem_limit_bytes=24 * 1024 * 1024),
    )


def near(arrays):
    return [pltpu.with_memory_space_constraint(array, pltpu.VMEM) for array in arrays]


def split_heads_per_device(saved_in, cotangent, section_gains):
    pipes, rows, cols = (lax.axis_size(name) for name in ("pipe", "row", "col"))
    channels = saved_in.shape[-1]
    tokens = saved_in.shape[1] * saved_in.shape[2]
    heads = channels // HEAD_DIM // (rows * cols)
    plane = ("row", "col")
    sizes = (rows, cols)
    bf, f32 = jnp.bfloat16, jnp.float32
    x = saved_in.reshape(tokens, channels)
    c = cotangent.reshape(tokens, channels)
    gains = section_gains[0]
    packets = []
    for head in range(heads):
        packets += [pltpu.VMEM((rows, 2 * tokens + (PIECES if head == 0 else 0), HEAD_DIM), bf)] * 2
    far = pl.BlockSpec(memory_space=pltpu.HBM)
    staged = [pltpu.VMEM((tokens, channels), bf)] * 2 + [pltpu.SemaphoreType.DMA((1,))] * 2
    packed = local_call(functools.partial(pack_kernel, rows, heads), packets, staged, in_specs=[far, far])(
        pltpu.with_memory_space_constraint(x, pltpu.HBM), pltpu.with_memory_space_constraint(c, pltpu.HBM)
    )

    def swap(array):
        return lax.ppermute(array, plane, crossing(sizes, 0, 1))

    passed = [[swap(packed[1][1:2]), swap(packed[1][2:]), swap(packed[1][0:1])]]
    passed += [swap(packed[2 * head + 1]) for head in range(1, heads)]
    arrays = []
    for head in range(heads):
        own, other = packed[2 * head], passed[head]
        if head == 0:
            held = [own, other[2]]
            packets = [jnp.concatenate([own[1:2], other[0]])]
            packets += [jnp.stack([own[step], other[1][step - 2]]) for step in range(2, rows)]
        else:
            held = [own, other]
            packets = [jnp.stack([own[step], other[step]]) for step in range(1, rows)]
        if head > 0:
            packets, arrays[head - 1][2] = lax.optimization_barrier((packets, arrays[head - 1][2]))
        for step in range(1, rows):
            held.append(lax.ppermute(packets[step - 1], plane, crossing(sizes, step, 0)))
        arrays.append(held)
    count = rows * cols * tokens
    square = 2 * tokens
    scratch = [
        pltpu.VMEM((count, HEAD_DIM), bf),
        pltpu.VMEM((count, HEAD_DIM), bf),
        pltpu.VMEM((HEAD_DIM, count), bf),
        pltpu.VMEM((count, HEAD_DIM), bf),
        pltpu.VMEM((count, HEAD_DIM), bf),
        pltpu.VMEM((count, count), bf),
        pltpu.VMEM((count, count), bf),
        pltpu.VMEM((2, count, square), f32),
        pltpu.VMEM((2, count, square), f32),
        pltpu.VMEM((count, HEAD_DIM), f32),
        pltpu.VMEM((count, HEAD_DIM), f32),
        pltpu.VMEM((count, HEAD_DIM), f32),
    ]
    behind = [(pipe, (pipe - 1) % pipes) for pipe in range(pipes)]
    arrays[0][2], free_x = lax.optimization_barrier((arrays[0][2], x))
    x_ahead = lax.ppermute(free_x, "pipe", behind)
    carried = pltpu.VMEM((heads, 2 * rows, tokens), f32)
    columns = [pltpu.VMEM((count, HEAD_DIM), f32)]
    handed = []
    keep, got = [], []
    for head in range(heads):
        results = columns if head == 0 else []
        results = results + ([carried] if head < heads - 1 else [])
        height = tokens + (EXTRA if head == heads - 1 else 0)
        results = results + [pltpu.VMEM((rows, height, HEAD_DIM), f32)] * 2
        operands = arrays[head] + ([] if head == 0 else columns + handed)
        call = local_call(functools.partial(attention_kernel, rows, heads, head), results, scratch)
        *others, kept, given = call(gains, *near(operands))
        columns = others[:1] if head == 0 else columns
        handed = others[-1:]
        if head == heads - 1:
            given, x_ahead = lax.optimization_barrier((given, x_ahead))
        keep.append(kept.astype(jnp.float16))
        got.append(lax.ppermute(given.astype(jnp.float16), plane, crossing(sizes, 0, 1)))
    units = []
    for step in range(rows):
        sent = jnp.concatenate([unit[step] for unit in keep + got])
        sent = lax.ppermute(sent, ("pipe",) + plane, crossing_back((pipes, rows, cols), step))
        units.append(sent.astype(f32))
    cubed = local_call(cube_kernel, pltpu.VMEM((tokens, channels), f32))(*near([x_ahead]))
    out = local_call(
        functools.partial(collect_kernel, rows, heads),
        jax.ShapeDtypeStruct((tokens, channels), bf),
        [pltpu.VMEM((tokens, channels), bf), pltpu.SemaphoreType.DMA((rows,))],
        out_specs=far,
    )(*near([cubed] + units))
    return out.reshape(saved_in.shape)


def per_device(saved_in, cotangent, section_gains):
    rows, cols = lax.axis_size("row"), lax.axis_size("col")
    block_fits = saved_in.shape[1] == TILE and saved_in.shape[2] == 2 * TILE
    devices_fit = cols == 2 and rows & (rows - 1) == 0 and HEADS % (rows * cols) == 0
    plan = split_heads_per_device if block_fits and devices_fit else halo_per_device
    return plan(saved_in, cotangent, section_gains)


def solution(mesh):
    return jax.shard_map(
        per_device,
        mesh=mesh,
        in_specs=(
            P("pipe", "row", "col", None),
            P("pipe", "row", "col", None),
            P("pipe", None, None),
        ),
        out_specs=P("pipe", "row", "col", None),
        check_vma=False,
    )
```

```python
import functools
import math

import jax
import jax.numpy as jnp
from jax import lax
from jax.experimental import pallas as pl
from jax.experimental.pallas import tpu as pltpu
from jax.sharding import PartitionSpec as P

HEADS = 16
HEAD_DIM = 128
TILE = 8
SPAN = 5


NEGATIVE = -1e30
EPSILON = 1e-06


def passed_along(block, axis, distance):
    devices = range(lax.axis_size(axis))
    route = [(i - distance, i) for i in devices if i - distance in devices]
    return lax.ppermute(block, axis, route)


def to_tiles(image):
    lead = image.shape[:-3]
    height, width, channels = image.shape[-3:]
    count = len(lead)
    image = image.reshape(lead + (height // TILE, TILE, width // TILE, TILE, channels))
    order = tuple(range(count)) + (count, count + 2, count + 1, count + 3, count + 4)
    return image.transpose(order).reshape(
        lead + (height // TILE, width // TILE, TILE * TILE, channels)
    )


def from_tiles(tiled):
    tile_rows, tile_cols, area, channels = tiled.shape
    tiled = tiled.reshape(tile_rows, tile_cols, TILE, TILE, channels)
    return tiled.transpose(0, 2, 1, 3, 4).reshape(tile_rows * TILE, tile_cols * TILE, channels)


def windows(extended, tile_rows, tile_cols):
    return jnp.concatenate(
        [
            extended[row_off : row_off + tile_rows, col_off : col_off + tile_cols]
            for row_off in range(SPAN)
            for col_off in range(SPAN)
        ],
        axis=2,
    )


def key_valid(base_row, base_col, tile_rows, tile_cols, all_rows, all_cols):
    reach_tiles = SPAN // 2
    offsets = jnp.arange(SPAN, dtype=jnp.int32) - reach_tiles
    row_ids = base_row + jnp.arange(tile_rows, dtype=jnp.int32)[:, None] + offsets[None, :]
    col_ids = base_col + jnp.arange(tile_cols, dtype=jnp.int32)[:, None] + offsets[None, :]
    row_ok = (row_ids >= 0) & (row_ids < all_rows)
    col_ok = (col_ids >= 0) & (col_ids < all_cols)
    allowed = row_ok[:, None, :, None] & col_ok[None, :, None, :]
    return jnp.repeat(allowed.reshape(tile_rows, tile_cols, SPAN * SPAN), TILE * TILE, axis=2)


def project(normed, scales, factor):
    return (normed.astype(jnp.float32) * (scales * factor)).astype(jnp.bfloat16)


def normalize(image, scales):
    x_float = image.astype(jnp.float32)
    inverse = lax.rsqrt(jnp.mean(x_float * x_float, axis=-1, keepdims=True) + EPSILON)
    return (x_float, inverse, (x_float * inverse * scales).astype(jnp.bfloat16))


def widen(array, dim, reach, move):
    own = array.shape[dim]
    need = -(-reach // own)
    above = []
    below = []
    for step_by in range(need, 0, -1):
        lower_end = max(-step_by * own, -reach)
        upper_end = -(step_by - 1) * own
        piece = array
        above.append(move(piece, step_by))
    for step_by in range(1, need + 1):
        length = min((step_by + 1) * own, own + reach) - step_by * own
        piece = array
        below.append(move(piece, -step_by))
    return jnp.concatenate(above + [array] + below, axis=dim)


def halo_per_device(saved_in, cotangent, section_gains):
    scales = section_gains[0]
    reach_tiles = SPAN // 2
    reach_cells = TILE * reach_tiles
    factor = 1.0 / math.sqrt(HEAD_DIM)
    tile_rows = saved_in.shape[1] // TILE
    tile_cols = saved_in.shape[2] // TILE
    allowed = key_valid(
        lax.axis_index("row") * tile_rows,
        lax.axis_index("col") * tile_cols,
        tile_rows,
        tile_cols,
        tile_rows * lax.axis_size("row"),
        tile_cols * lax.axis_size("col"),
    )
    saved_float, saved_inverse, saved_normed = normalize(saved_in[0], scales[0])
    upstream_image = cotangent[0].astype(jnp.float32)
    grad_image = (upstream_image * scales[4]).astype(jnp.bfloat16)
    paired = jnp.stack([saved_normed, grad_image])

    def move_cols(piece, step_by):
        return passed_along(piece, "col", step_by)

    def move_rows(piece, step_by):
        return passed_along(piece, "row", step_by)

    paired_wide = widen(widen(paired, 2, reach_cells, move_cols), 1, reach_cells, move_rows)
    paired_ext = to_tiles(paired_wide)
    normed_ext = paired_ext[0]
    grad_ext = paired_ext[1]
    normed_tiles = to_tiles(saved_normed)
    grad_tiles = to_tiles(grad_image)
    stat_shape = (HEADS, tile_rows, tile_cols, TILE * TILE)

    def own_head(head, carry):
        dnormed, log_all, delta_all = carry
        start = head * HEAD_DIM

        def part(array):
            return lax.dynamic_slice_in_dim(array, start, HEAD_DIM, array.ndim - 1)

        queries = project(part(normed_tiles), part(scales[1]), factor)
        key_win = windows(project(part(normed_ext), part(scales[2]), 1.0), tile_rows, tile_cols)
        value_win = windows(project(part(normed_ext), part(scales[3]), 1.0), tile_rows, tile_cols)
        scores = jnp.einsum("ijqc,ijkc->ijqk", queries, key_win, preferred_element_type=jnp.float32)
        scores = jnp.where(allowed[:, :, None, :], scores, NEGATIVE)
        row_max = jnp.max(scores, axis=-1, keepdims=True)
        log_total = row_max + jnp.log(jnp.sum(jnp.exp(scores - row_max), axis=-1, keepdims=True))
        weights = jnp.exp(scores - log_total)
        rounded = weights.astype(jnp.bfloat16)
        output = jnp.einsum(
            "ijqk,ijkc->ijqc", rounded, value_win, preferred_element_type=jnp.float32
        )
        grads = part(grad_tiles)
        delta_sum = jnp.sum(grads.astype(jnp.float32) * output, axis=-1)
        prob_grad = jnp.einsum(
            "ijqc,ijkc->ijqk", grads, value_win, preferred_element_type=jnp.float32
        )
        dscore = (weights * (prob_grad - delta_sum[..., None])).astype(jnp.bfloat16)
        dquery = jnp.einsum("ijqk,ijkc->ijqc", dscore, key_win, preferred_element_type=jnp.float32)
        dnormed = lax.dynamic_update_slice_in_dim(
            dnormed, dquery * (part(scales[1]) * factor), start, 3
        )
        log_all = log_all.at[head].set(log_total[..., 0])
        delta_all = delta_all.at[head].set(delta_sum)
        return (dnormed, log_all, delta_all)

    dnormed, log_all, delta_all = lax.fori_loop(
        0,
        HEADS,
        own_head,
        (
            jnp.zeros(normed_tiles.shape, jnp.float32),
            jnp.zeros(stat_shape, jnp.float32),
            jnp.zeros(stat_shape, jnp.float32),
        ),
    )
    stat_tiles = jnp.concatenate([log_all, delta_all], axis=0).transpose(1, 2, 3, 0)

    def stat_cols(piece, step_by):
        return passed_along(piece, "col", step_by)

    def stat_rows(piece, step_by):
        return passed_along(piece, "row", step_by)

    stat_wide = widen(
        widen(from_tiles(stat_tiles), 1, reach_cells, stat_cols), 0, reach_cells, stat_rows
    )
    stat_win = windows(to_tiles(stat_wide), tile_rows, tile_cols)

    def far_head(head, dnormed):
        start = head * HEAD_DIM

        def part(array):
            return lax.dynamic_slice_in_dim(array, start, HEAD_DIM, array.ndim - 1)

        query_win = windows(
            project(part(normed_ext), part(scales[1]), factor), tile_rows, tile_cols
        )
        grad_win = windows(part(grad_ext), tile_rows, tile_cols)
        own_keys = project(part(normed_tiles), part(scales[2]), 1.0)
        own_values = project(part(normed_tiles), part(scales[3]), 1.0)
        far_log = lax.dynamic_index_in_dim(stat_win, head, 3, keepdims=False)
        far_delta = lax.dynamic_index_in_dim(stat_win, HEADS + head, 3, keepdims=False)
        scores = jnp.einsum(
            "ijqc,ijkc->ijqk", query_win, own_keys, preferred_element_type=jnp.float32
        )
        weights = jnp.exp(jnp.where(allowed[..., None], scores - far_log[..., None], NEGATIVE))
        prob_grad = jnp.einsum(
            "ijqc,ijkc->ijqk", grad_win, own_values, preferred_element_type=jnp.float32
        )
        dscore = (weights * (prob_grad - far_delta[..., None])).astype(jnp.bfloat16)
        key_grad = jnp.einsum(
            "ijqk,ijqc->ijkc", dscore, query_win, preferred_element_type=jnp.float32
        )
        dvalue = jnp.einsum(
            "ijqk,ijqc->ijkc",
            weights.astype(jnp.bfloat16),
            grad_win,
            preferred_element_type=jnp.float32,
        )
        terms = key_grad * part(scales[2]) + dvalue * part(scales[3])
        return lax.dynamic_update_slice_in_dim(dnormed, part(dnormed) + terms, start, 3)

    dnormed = lax.fori_loop(0, HEADS, far_head, dnormed)
    scaled = scales[0] * dnormed
    x_tiles = to_tiles(saved_float)
    inv_tiles = to_tiles(saved_inverse)
    upstream = to_tiles(upstream_image)
    image_grad = (
        upstream
        + inv_tiles * scaled
        - x_tiles
        * (inv_tiles * inv_tiles * inv_tiles)
        * jnp.mean(x_tiles * scaled, axis=-1, keepdims=True)
    )
    sent_back = passed_along(from_tiles(image_grad.astype(jnp.bfloat16)), "pipe", -1)
    return sent_back[None]


PIECES = 16


EXTRA = 8
SCALES = [2.0 ** (12 * power) for power in range(-8, 11)]


def crossing(sizes, row_step, col_step):
    rows, cols = sizes
    return [
        (row * cols + col, (row ^ row_step) * cols + (col ^ col_step))
        for row in range(rows)
        for col in range(cols)
    ]


def crossing_back(sizes, row_step):
    pipes, rows, cols = sizes
    return [
        (
            (pipe * rows + row) * cols + col,
            ((pipe - 1) % pipes * rows + (row ^ row_step)) * cols + col,
        )
        for pipe in range(pipes)
        for row in range(rows)
        for col in range(cols)
    ]


def row_to_column(row):
    return jnp.broadcast_to(row, (row.shape[1], row.shape[1])).T


def inverse_columns(pieces):
    pieces = pieces.astype(jnp.float32)
    return row_to_column(pieces[0:1] + pieces[1:2] + pieces[2:3])


def scale_number(size):
    return sum((size >= scale).astype(jnp.float32) for scale in SCALES[1:])


def scale_value(number):
    value = jnp.full(number.shape, SCALES[0], jnp.float32)
    for index, scale in enumerate(SCALES[1:]):
        value = jnp.where(number > index + 0.5, scale, value)
    return value


def inverse_row(x_ref):
    tokens, channels = x_ref.shape
    squares = None
    for lane in range(0, channels, HEAD_DIM):
        part = x_ref[:, lane : lane + HEAD_DIM].astype(jnp.float32)
        part = part * part
        squares = part if squares is None else squares + part
    total = jnp.sum(squares.T, axis=0, keepdims=True)
    return lax.rsqrt(total / channels + EPSILON)


def pack_kernel(rows, heads, x_hbm, c_hbm, *refs):
    outs = refs[: heads * 2]
    x_ref, c_ref, x_sem, c_sem = refs[heads * 2 :]
    tokens, channels = x_ref.shape
    row = lax.axis_index("row")
    col = lax.axis_index("col")
    parts = x_sem.shape[0]
    high_rows = tokens // parts

    def fetch(source, target, sems, part):
        here = pl.ds(part * high_rows, high_rows)
        return pltpu.make_async_copy(source.at[here, :], target.at[here, :], sems.at[part])

    fetches = [fetch(x_hbm, x_ref, x_sem, part) for part in range(parts)]
    fetches += [fetch(c_hbm, c_ref, c_sem, part) for part in range(parts)]
    for copy in fetches:
        copy.start()
    for copy in fetches[:parts]:
        copy.wait()
    inverse = inverse_row(x_ref)
    high = inverse.astype(jnp.bfloat16).astype(jnp.float32)
    mid = (inverse - high).astype(jnp.bfloat16).astype(jnp.float32)
    low = inverse - high - mid
    place = lax.broadcasted_iota(jnp.int32, (PIECES, tokens), 0)
    pieces = jnp.where(place == 0, high, jnp.where(place == 1, mid, jnp.where(place == 2, low, 0.0)))
    pieces = pieces.astype(jnp.bfloat16)
    for source, low in ((x_ref, 0), (c_ref, tokens)):
        if low > 0:
            for copy in fetches[parts:]:
                copy.wait()
        for head in range(heads):
            for step in range(rows):
                for slot in range(2):
                    first = ((row ^ step) * 2 + (col ^ slot)) * heads + head
                    lanes = pl.ds(pl.multiple_of(first * HEAD_DIM, HEAD_DIM), HEAD_DIM)
                    out = outs[head * 2 + slot]
                    out[step, low : low + tokens, :] = source[:, lanes]
                    if head == 0 and low == 0:
                        out[step, 2 * tokens :, :] = pieces


def attend_kernel(rows, heads, head, g_ref, *refs):
    held = rows + 1
    arrays, refs = refs[:held], list(refs[held:])
    columns_ref = refs.pop(0)
    before_ref = refs.pop(0) if head > 0 else None
    after_ref = refs.pop(0) if head < heads - 1 else None
    keep_ref, give_ref = refs[:2]
    q_s, k_s, kt_s, v_s, d_s, p_s, ds_s, s_s, dp_s, dk_s, dv_s, dq_s = refs[-12:]
    tokens = columns_ref.shape[0] // (2 * rows)
    row = lax.axis_index("row")
    col = lax.axis_index("col")
    lanes = pl.ds(pl.multiple_of(((row * 2 + col) * heads + head) * HEAD_DIM, HEAD_DIM), HEAD_DIM)
    gn, gq, gk, gv, go = (g_ref[i : i + 1, lanes] for i in range(5))
    gq = gq * (1.0 / math.sqrt(HEAD_DIM))
    square = 2 * tokens
    pattern = (tokens // (2 * TILE), 2, TILE, tokens)
    query_right = (lax.broadcasted_iota(jnp.int32, pattern[1:], 2) // TILE) % 2
    key_right = lax.broadcasted_iota(jnp.int32, pattern[1:], 0)
    no_cap = float(jnp.finfo(jnp.float32).max)
    left_keys = jnp.where((key_right == 0) & (query_right == 1), NEGATIVE, no_cap)
    right_keys = jnp.where((key_right == 1) & (query_right == 0), NEGATIVE, no_cap)

    def capped(s, cap):
        return jnp.minimum(s.reshape(pattern), cap[None]).reshape(tokens, tokens)

    def block(step, slot, fresh=False):
        number, index = (slot, 0) if step == 0 else (step + 1, slot)
        ref = arrays[number]
        place = pl.multiple_of(((row ^ step) * 2 + (col ^ slot)) * tokens, tokens)
        x = ref[index, 0:tokens, :].astype(jnp.float32)
        c = ref[index, tokens : 2 * tokens, :].astype(jnp.float32)
        here = pl.ds(place, tokens)
        return here, x, c, ref[index, 2 * tokens :, :] if fresh else columns_ref[here, :]

    blocks = [(step, slot) for step in range(rows) for slot in range(2)]
    for step, slot in blocks:
        here, x, c, inverse = block(step, slot, head == 0)
        if head == 0:
            inverse = inverse_columns(inverse)
            columns_ref[here, :] = inverse
        normed = (x * inverse * gn).astype(jnp.bfloat16).astype(jnp.float32)
        q_s[here, :] = (normed * gq).astype(jnp.bfloat16)
        key = (normed * gk).astype(jnp.bfloat16)
        k_s[here, :] = key
        kt_s[:, here] = key.astype(jnp.float32).T.astype(jnp.bfloat16)
        v_s[here, :] = (normed * gv).astype(jnp.bfloat16)
        d_s[here, :] = (c * go).astype(jnp.bfloat16)

    contract_last = (((1,), (1,)), ((), ()))
    reach = SPAN // 2
    spans = []
    for at in range(rows):
        near = [r for r in range(rows) if abs(r - at) <= reach]
        spans.append((near[0] * square, (near[-1] + 1) * square))

    def own(at):
        return slice(at * square, (at + 1) * square)

    def cells(at):
        return [slice(start, start + square) for start in range(*spans[at], square)]

    def fold(combine, parts):
        total = parts[0]
        for part in parts[1:]:
            total = combine(total, part)
        return total

    def products(at, tops):
        buffer = at % 2
        q, d = q_s[own(at), :], d_s[own(at), :]
        left, right = [], []
        for cell in cells(at):
            s = lax.dot_general(k_s[cell, :], q, contract_last, preferred_element_type=jnp.float32)
            upper = slice(cell.start, cell.start + tokens)
            lower = slice(cell.start + tokens, cell.stop)
            upper_left, upper_right = s[0:tokens, 0:tokens], capped(s[0:tokens, tokens:], left_keys)
            lower_left, lower_right = capped(s[tokens:, 0:tokens], right_keys), s[tokens:, tokens:]
            s_s[buffer, upper, 0:tokens] = upper_left
            s_s[buffer, upper, tokens:] = upper_right
            s_s[buffer, lower, 0:tokens] = lower_left
            s_s[buffer, lower, tokens:] = lower_right
            left.append(jnp.max(jnp.maximum(upper_left, lower_left), axis=0, keepdims=True))
            right.append(jnp.max(jnp.maximum(upper_right, lower_right), axis=0, keepdims=True))
            yield
            dp_s[buffer, cell, :] = lax.dot_general(
                v_s[cell, :], d, contract_last, preferred_element_type=jnp.float32
            )
            yield
        tops[at] = jnp.concatenate([fold(jnp.maximum, left), fold(jnp.maximum, right)], axis=1)

    def softmax(at, tops):
        buffer = at % 2
        top = tops[at]
        sums = []
        for cell in cells(at):
            e = jnp.exp(s_s[buffer, cell, :] - top)
            s_s[buffer, cell, :] = e
            sums.append(jnp.sum(e, axis=0, keepdims=True))
            yield
        scale = 1.0 / fold(jnp.add, sums)
        sums = []
        for cell in cells(at):
            p = s_s[buffer, cell, :] * scale
            pb = p.astype(jnp.bfloat16)
            p_s[cell, own(at)] = pb
            sums.append(jnp.sum(pb.astype(jnp.float32) * dp_s[buffer, cell, :], axis=0, keepdims=True))
            yield
        delta = fold(jnp.add, sums)
        for cell in cells(at):
            p = s_s[buffer, cell, :] * scale
            ds_s[cell, own(at)] = (p * (dp_s[buffer, cell, :] - delta)).astype(jnp.bfloat16)
            yield

    def query_side(at):
        span = slice(*spans[at])
        dq = jnp.dot(kt_s[:, span], ds_s[span, own(at)], preferred_element_type=jnp.float32)
        yield
        dq_s[own(at), :] = dq.T
        yield

    def key_side(first, last):
        for at in range(rows):
            low, high = max(spans[at][0], first * square), min(spans[at][1], last * square)
            if low >= high:
                continue
            span = slice(low, high)
            dk = jnp.dot(ds_s[own(at), span], q_s[span, :], preferred_element_type=jnp.float32)
            fresh = low == spans[at][0]
            dk_s[own(at), :] = dk if fresh else dk_s[own(at), :] + dk
            yield
            dv = jnp.dot(p_s[own(at), span], d_s[span, :], preferred_element_type=jnp.float32)
            dv_s[own(at), :] = dv if fresh else dv_s[own(at), :] + dv
            yield

    def together(*works):
        works = list(works)
        while works:
            works = [work for work in works if next(work, works) is not works]


    def all_queries():
        dq = jnp.dot(kt_s[...], ds_s[...], preferred_element_type=jnp.float32)
        yield
        dq_s[...] = dq.T
        yield

    for at in range(rows):
        for other in range(rows):
            if abs(at - other) > reach:
                ds_s[own(at), own(other)] = jnp.zeros((square, square), jnp.bfloat16)
    tops = {}
    together(products(0, tops))
    for at in range(rows):
        works = [softmax(at, tops)]
        if at + 1 < rows:
            works.append(products(at + 1, tops))
        if at > 0:
            works += [key_side(at - 1, at)]
        together(*works)
    together(all_queries(), key_side(rows - 1, rows))
    tops, shares = [], []
    for step, slot in blocks:
        here, x, c, inverse = block(step, slot)
        scaled = gn * (dq_s[here, :] * gq + dk_s[here, :] * gk + dv_s[here, :] * gv)
        value = c + inverse * scaled
        (keep_ref, give_ref)[slot][step, 0:tokens, :] = value
        tops.append(jnp.max(jnp.abs(value), axis=0, keepdims=True))
        shares.append(jnp.sum((x * scaled).T, axis=0, keepdims=True))
    top = jnp.max(jnp.concatenate(tops, axis=0), axis=1, keepdims=True)
    number = scale_number(jnp.broadcast_to(top, (len(blocks), tokens)))
    shrink = 1.0 / scale_value(number)
    share = jnp.concatenate(shares, axis=0)
    numbers = [before_ref[earlier + 1] for earlier in range(head)] + [number]
    if head > 0:
        share = share + before_ref[0]
    if head < heads - 1:
        after_ref[0] = share
        for index, value in enumerate(numbers):
            after_ref[index + 1] = value
    else:
        share_number = scale_number(jnp.abs(share))
        share = share / scale_value(share_number)
        high = share.astype(jnp.bfloat16).astype(jnp.float32)
        mid = (share - high).astype(jnp.bfloat16).astype(jnp.float32)
        low = share - high - mid
        place = lax.broadcasted_iota(jnp.int32, (EXTRA, tokens), 0)
    for index, (step, slot) in enumerate(blocks):
        out = (keep_ref, give_ref)[slot]
        at = slice(index, index + 1)
        out[step, 0:tokens, :] = out[step, 0:tokens, :] * shrink[at]
        if head == heads - 1:
            extra = jnp.zeros((EXTRA, tokens), jnp.float32)
            for line, value in enumerate([share_number, high, mid, low] + numbers):
                extra = jnp.where(place == line, value[at], extra)
            out[step, tokens:, :] = extra


def attention_kernel(*operands):
    @pl.when(lax.axis_index("pipe") > 0)
    def _():
        attend_kernel(*operands)


def cube_kernel(x_ref, out_ref):
    inverse = inverse_row(x_ref)
    cube = row_to_column(inverse * inverse * inverse)
    for lane in range(0, x_ref.shape[1], HEAD_DIM):
        lanes = slice(lane, lane + HEAD_DIM)
        out_ref[:, lanes] = x_ref[:, lanes].astype(jnp.float32) * cube


def collect_kernel(rows, heads, x_ref, *refs):
    units = refs[:rows]
    out_hbm, out_ref, sems = refs[rows:]
    tokens, channels = x_ref.shape
    row = lax.axis_index("row")
    col = lax.axis_index("col")
    last = lax.axis_index("pipe") == lax.axis_size("pipe") - 1
    side = heads * tokens + EXTRA
    total, scales = None, {}
    for step in range(rows):
        for half in range(2):
            extra = units[step][half * side + heads * tokens : (half + 1) * side, :]
            value = scale_value(extra)
            for head in range(heads):
                scales[step, half * heads + head] = value[4 + head : 5 + head]
            share = (extra[1:2] + extra[2:3] + extra[3:4]) * value[0:1]
            total = share if total is None else total + share
    mean = row_to_column(total / channels)
    wide = 2 * heads * HEAD_DIM
    copies = []
    for step in range(rows):
        for slot in range(2 * heads):
            first = ((row ^ step) * 2 + (col ^ (slot // heads))) * heads + slot % heads
            lanes = pl.ds(pl.multiple_of(first * HEAD_DIM, HEAD_DIM), HEAD_DIM)
            top = slot // heads * side + slot % heads * tokens
            part = units[step][top : top + tokens, :] * scales[step, slot]
            grad = part - x_ref[:, lanes] * mean
            out_ref[:, lanes] = jnp.where(last, 0.0, grad).astype(jnp.bfloat16)
        lanes = pl.ds(pl.multiple_of((row ^ step) * wide, wide), wide)
        copies.append(pltpu.make_async_copy(out_ref.at[:, lanes], out_hbm.at[:, lanes], sems.at[step]))
        copies[-1].start()
    for copy in copies:
        copy.wait()


def local_call(kernel, out_shape, scratch_shapes=(), **placed):
    return pl.pallas_call(
        kernel,
        out_shape=out_shape,
        **placed,
        scratch_shapes=scratch_shapes,
        compiler_params=pltpu.CompilerParams(vmem_limit_bytes=24 * 1024 * 1024),
    )


def near(arrays):
    return [pltpu.with_memory_space_constraint(array, pltpu.VMEM) for array in arrays]


def split_heads_per_device(saved_in, cotangent, section_gains):
    pipes, rows, cols = (lax.axis_size(name) for name in ("pipe", "row", "col"))
    channels = saved_in.shape[-1]
    tokens = saved_in.shape[1] * saved_in.shape[2]
    heads = channels // HEAD_DIM // (rows * cols)
    plane = ("row", "col")
    sizes = (rows, cols)
    bf, f32 = jnp.bfloat16, jnp.float32
    x = saved_in.reshape(tokens, channels)
    c = cotangent.reshape(tokens, channels)
    gains = section_gains[0]
    packets = []
    for head in range(heads):
        packets += [pltpu.VMEM((rows, 2 * tokens + (PIECES if head == 0 else 0), HEAD_DIM), bf)] * 2
    far = pl.BlockSpec(memory_space=pltpu.HBM)
    staged = [pltpu.VMEM((tokens, channels), bf)] * 2 + [pltpu.SemaphoreType.DMA((1,))] * 2
    packed = local_call(functools.partial(pack_kernel, rows, heads), packets, staged, in_specs=[far, far])(
        pltpu.with_memory_space_constraint(x, pltpu.HBM), pltpu.with_memory_space_constraint(c, pltpu.HBM)
    )

    def swap(array):
        return lax.ppermute(array, plane, crossing(sizes, 0, 1))

    passed = [[swap(packed[1][1:2]), swap(packed[1][2:]), swap(packed[1][0:1])]]
    passed += [swap(packed[2 * head + 1]) for head in range(1, heads)]
    arrays = []
    for head in range(heads):
        own, other = packed[2 * head], passed[head]
        if head == 0:
            held = [own, other[2]]
            packets = [jnp.concatenate([own[1:2], other[0]])]
            packets += [jnp.stack([own[step], other[1][step - 2]]) for step in range(2, rows)]
        else:
            held = [own, other]
            packets = [jnp.stack([own[step], other[step]]) for step in range(1, rows)]
        if head > 0:
            packets, arrays[head - 1][2] = lax.optimization_barrier((packets, arrays[head - 1][2]))
        for step in range(1, rows):
            held.append(lax.ppermute(packets[step - 1], plane, crossing(sizes, step, 0)))
        arrays.append(held)
    count = rows * cols * tokens
    square = 2 * tokens
    scratch = [
        pltpu.VMEM((count, HEAD_DIM), bf),
        pltpu.VMEM((count, HEAD_DIM), bf),
        pltpu.VMEM((HEAD_DIM, count), bf),
        pltpu.VMEM((count, HEAD_DIM), bf),
        pltpu.VMEM((count, HEAD_DIM), bf),
        pltpu.VMEM((count, count), bf),
        pltpu.VMEM((count, count), bf),
        pltpu.VMEM((2, count, square), f32),
        pltpu.VMEM((2, count, square), f32),
        pltpu.VMEM((count, HEAD_DIM), f32),
        pltpu.VMEM((count, HEAD_DIM), f32),
        pltpu.VMEM((count, HEAD_DIM), f32),
    ]
    behind = [(pipe, (pipe - 1) % pipes) for pipe in range(pipes)]
    arrays[0][2], free_x = lax.optimization_barrier((arrays[0][2], x))
    x_ahead = lax.ppermute(free_x, "pipe", behind)
    carried = pltpu.VMEM((heads, 2 * rows, tokens), f32)
    columns = [pltpu.VMEM((count, HEAD_DIM), f32)]
    handed = []
    keep, got = [], []
    for head in range(heads):
        results = columns if head == 0 else []
        results = results + ([carried] if head < heads - 1 else [])
        height = tokens + (EXTRA if head == heads - 1 else 0)
        results = results + [pltpu.VMEM((rows, height, HEAD_DIM), f32)] * 2
        operands = arrays[head] + ([] if head == 0 else columns + handed)
        call = local_call(functools.partial(attention_kernel, rows, heads, head), results, scratch)
        *others, kept, given = call(gains, *near(operands))
        columns = others[:1] if head == 0 else columns
        handed = others[-1:]
        if head == heads - 1:
            given, x_ahead = lax.optimization_barrier((given, x_ahead))
        keep.append(kept.astype(jnp.float16))
        got.append(lax.ppermute(given.astype(jnp.float16), plane, crossing(sizes, 0, 1)))
    units = []
    for step in range(rows):
        sent = jnp.concatenate([unit[step] for unit in keep + got])
        sent = lax.ppermute(sent, ("pipe",) + plane, crossing_back((pipes, rows, cols), step))
        units.append(sent.astype(f32))
    cubed = local_call(cube_kernel, pltpu.VMEM((tokens, channels), f32))(*near([x_ahead]))
    out = local_call(
        functools.partial(collect_kernel, rows, heads),
        jax.ShapeDtypeStruct((tokens, channels), bf),
        [pltpu.VMEM((tokens, channels), bf), pltpu.SemaphoreType.DMA((rows,))],
        out_specs=far,
    )(*near([cubed] + units))
    return out.reshape(saved_in.shape)


def per_device(saved_in, cotangent, section_gains):
    rows, cols = lax.axis_size("row"), lax.axis_size("col")
    block_fits = saved_in.shape[1] == TILE and saved_in.shape[2] == 2 * TILE
    devices_fit = cols == 2 and rows & (rows - 1) == 0 and HEADS % (rows * cols) == 0
    plan = split_heads_per_device if block_fits and devices_fit else halo_per_device
    return plan(saved_in, cotangent, section_gains)


def solution(mesh):
    return jax.shard_map(
        per_device,
        mesh=mesh,
        in_specs=(
            P("pipe", "row", "col", None),
            P("pipe", "row", "col", None),
            P("pipe", None, None),
        ),
        out_specs=P("pipe", "row", "col", None),
        check_vma=False,
    )
```
